32 devices in a mesh: rows: 8 (over z, x), cols: 4 (over y, core).
Axes of the slice: x: 2, y: 2, z: 4, core: 2. Of those that a mesh axis runs over, the one named last changes fastest.
Arguments:
- tile_density: bfloat16 [2048, 64, 64], P(('rows', 'cols')), may hold values from -6 to 6
- tile_dest: int32 [2048, 1], P(('rows', 'cols')), may hold values from 0 to 7; in each aligned block of 64 rows (0 to 63, 64 to 127, ...) at most 16 rows name the same one
- tile_place: int32 [2048], P(('rows', 'cols')), may hold values from 0 to 31
- psf_spectrum: bfloat16 [2048, 2048], P('rows', 'cols'), may hold values from 0.049804688 to 1
Outputs:
- flare_spectrum: float32 [2048, 2, 2048], P('rows', None, 'cols')
The draws below stay inside these ranges and needn't reach their ends.
Inputs may be any that keep to these rules, and one draw needn't show every extreme that they name: `tile_dest`: among the 64 tiles of one owner, at most 16 lie in the same row slab, and some owner has exactly 16 in one row slab.
All inputs are finite; a program needn't handle non-finite values.
Results may differ from the reference program's by a relative error of at most 0.0075.
Values may be sent and summed in bfloat16 or wider, within the bound.
A program may use at most 64 MiB of HBM per device.

```python
import math
import jax
import jax.numpy as jnp
import numpy as np
from jax import lax

ROWS_DEV = 256
COLS_DEV = 512
TILE = 64
OWNER_TILES = 64
GRID_ROWS = 2048
SLAB_COLS = 2048
CAPACITY = 16
ALL_TILES = 2048
N_ROWS = 8
N_COLS = 4


def place_ends(values, stream_key, smallest, largest):
    longest = values.shape.index(max(values.shape))
    spots = []
    for shift in (0, 1):
        where = [jax.random.randint(jax.random.fold_in(stream_key, axis), (), 0, length) for axis, length in enumerate(values.shape)]
        where[longest] = (where[longest] + shift) % values.shape[longest]
        spots.append(tuple(where))
    return values.at[spots[0]].set(smallest).at[spots[1]].set(largest)


def levels(stream_key, dims, shards, low, largest):
    def one(axis_at, parts):
        heights = jax.random.uniform(jax.random.fold_in(jax.random.fold_in(stream_key, 6), axis_at), (parts,), jnp.float32, low / len(shards), largest / len(shards))
        return jnp.repeat(jnp.exp(heights), dims[axis_at] // parts).reshape((-1,) + (1,) * (len(dims) - axis_at - 1))

    level = one(*shards[0])
    for cut in shards[1:]:
        level = level * one(*cut)
    return level


def shared_out(stream_key, own, number, rows, number_of, top, bound, lean):
    sequence = jax.random.permutation(stream_key, number_of)
    heavy_load, ordinary = shares(number_of, rows * top, bound, lean, True), shares(number_of, rows * top, bound, lean, False)
    places = jnp.arange(number_of)

    def named(sizes, rotation):
        used = int((sizes > 0).sum())
        fixed = max(1, used // 4)
        passed = fixed + (places - fixed + rotation * (used - fixed)) % max(1, number_of - fixed)
        return jnp.zeros((number_of,), jnp.int32).at[sequence[jnp.where(places < fixed, places, passed)]].set(jnp.asarray(sizes, jnp.int32))

    sizes = jnp.where(number % 4 == 0, named(heavy_load, number // 4), named(ordinary, number - number // 4 - 1))
    mixed = jax.random.permutation(jax.random.fold_in(own, 3), number_of)
    source_of, receiver = mixed[0:number_of // 2 * 2:2], mixed[1:number_of // 2 * 2:2]
    slack = jnp.minimum(sizes[source_of] - 1, bound - sizes[receiver]) // 2
    slack = jnp.where((source_of == sequence[0]) | (receiver == sequence[0]) | (sizes[receiver] == 0), 0, jnp.maximum(slack, 0))
    passed = jax.random.randint(jax.random.fold_in(own, 4), (number_of // 2,), 0, 1 << 20) % (slack + 1)
    sizes = sizes.at[source_of].add(-passed).at[receiver].add(passed)
    labels = jnp.searchsorted(jnp.cumsum(sizes), jnp.arange(rows * top), side="right").astype(jnp.int32)
    grid = labels.reshape(top, rows).T
    grid = grid[jax.random.permutation(jax.random.fold_in(own, 1), rows)]
    rotation = jax.random.randint(jax.random.fold_in(own, 2), (rows, 1), 0, top)
    return jnp.take_along_axis(grid, (jnp.arange(top)[None, :] + rotation) % top, axis=1)


def shares(amount, total, bound, skew, full):
    portions = [(1 << 20) // math.isqrt(grade ** skew) + 1 for grade in range(1, amount + 1)]
    largest = bound if full else min(bound, max(-(-total // amount), total * portions[0] // sum(portions)))
    least = 1 if total - largest >= amount - 1 else 0
    counts, spare = [largest] + [least] * (amount - 1), total - largest - least * (amount - 1)
    while spare > 0:
        candidates = [i for i in range(1, amount) if counts[i] < largest] or [i for i in range(1, amount) if counts[i] < bound]
        whole, left = sum([portions[i] for i in candidates]), spare
        for i in candidates:
            more = min(bound - counts[i], max(1, left * portions[i] // whole), spare)
            counts[i] = counts[i] + more
            spare = spare - more
    return np.array(counts)


def scatter_about(own_key, extent, width, bound, split=(), kind=jnp.bfloat16):
    level = levels(own_key, extent, split, -0.22, 0.18) if split else 1.0
    array = jax.random.normal(own_key, extent, jnp.float32) * width * level
    return jnp.minimum(jnp.maximum(array, -bound), bound).astype(kind)


def setup_inputs(seed: int = 0) -> dict:
    arg_keys = jax.random.split(jax.random.key(seed), 5)
    tile_density = scatter_about(arg_keys[0], (ALL_TILES, TILE, TILE), 1.0, 6.0, ((0, 32),))
    tile_dest_keys = jax.random.split(jax.random.fold_in(arg_keys[1], 1), ALL_TILES // OWNER_TILES)
    tile_dest_turns = jax.random.permutation(jax.random.fold_in(arg_keys[1], 3), ALL_TILES // OWNER_TILES)
    tile_dest = jax.vmap(lambda own, number: shared_out(jax.random.fold_in(arg_keys[1], 2), own, number, OWNER_TILES, N_ROWS, 1, CAPACITY, 2))(tile_dest_keys, tile_dest_turns).reshape((ALL_TILES, 1))
    tile_place = place_ends(jax.random.randint(arg_keys[2], (ALL_TILES,), 0, (ROWS_DEV // TILE) * (COLS_DEV // TILE)), jax.random.fold_in(arg_keys[2], 1), 0, ((ROWS_DEV // TILE) * (COLS_DEV // TILE)) - 1).astype(jnp.int32)
    psf_spectrum = jnp.clip(jnp.exp(math.log(1.0) - 2.9996462 * jax.random.uniform(arg_keys[3], (GRID_ROWS, SLAB_COLS), jnp.float32) ** levels(arg_keys[3], (GRID_ROWS, SLAB_COLS), ((0, 8), (1, 4)), -0.2, 0.2)), 0.049804688, 1.0).astype(jnp.bfloat16)
    return dict(tile_density=tile_density, tile_dest=tile_dest, tile_place=tile_place, psf_spectrum=psf_spectrum)


def make_table(length, factor):
    positions = jnp.arange(length, dtype=jnp.int32)
    angles = 2.0 * math.pi / length * (positions[:, None] * positions[None, :] % length).astype(jnp.float32)
    cosine = jnp.cos(angles) * factor
    sine_part = jnp.sin(angles) * factor
    upper_rows = jnp.stack([cosine, -sine_part], 1)
    bottom = jnp.stack([sine_part, cosine], 1)
    return jnp.stack([upper_rows, bottom], 0).astype(jnp.bfloat16)

def twiddle(real_part, imag_part, position, frequency, period):
    angles = 2.0 * math.pi / period * (position * frequency % period).astype(jnp.float32)
    cosine = jnp.cos(angles)
    sine_part = jnp.sin(angles)
    return (real_part * cosine + imag_part * sine_part, imag_part * cosine - real_part * sine_part)

def reference(tile_density, tile_dest, tile_place, psf_spectrum):
    per_row = COLS_DEV // TILE
    tile_index = jnp.arange(ALL_TILES, dtype=jnp.int32)
    owner_col = tile_index // OWNER_TILES % N_COLS
    tile_row = ROWS_DEV // TILE * tile_dest[:, 0] + tile_place // per_row
    tile_col = per_row * owner_col + tile_place % per_row
    grid_cols = SLAB_COLS // TILE
    flat_index = (tile_row * grid_cols + tile_col).astype(jnp.int32)
    tile_sums = jnp.zeros((GRID_ROWS // TILE * grid_cols, TILE, TILE), jnp.float32)
    tile_sums = tile_sums.at[flat_index].add(tile_density.astype(jnp.float32))
    density_grid = tile_sums.reshape(GRID_ROWS // TILE, grid_cols, TILE, TILE).transpose(0, 2, 1, 3)
    density_grid = lax.optimization_barrier(density_grid.reshape(GRID_ROWS, SLAB_COLS).astype(jnp.bfloat16))
    blocks = density_grid.reshape(GRID_ROWS, N_COLS, COLS_DEV).astype(jnp.float32)
    row_table = make_table(COLS_DEV, 1.0 / math.sqrt(SLAB_COLS)).reshape(2 * COLS_DEV, 2 * COLS_DEV).astype(jnp.float32)
    col_table = make_table(N_ROWS, 1.0).transpose(3, 2, 1, 0).astype(jnp.float32)
    final_table = make_table(ROWS_DEV, 1.0 / math.sqrt(GRID_ROWS)).transpose(3, 2, 1, 0)
    final_table = final_table.reshape(2 * ROWS_DEV, 2 * ROWS_DEV).astype(jnp.float32)
    owners = jnp.arange(N_COLS, dtype=jnp.int32)
    columns = jnp.arange(COLS_DEV, dtype=jnp.int32)
    row_index = jnp.arange(ROWS_DEV, dtype=jnp.int32)
    row_freq = jnp.arange(N_ROWS, dtype=jnp.int32)
    highest = lax.Precision.HIGHEST

    def one_block(frequency):
        angles = 2.0 * math.pi / N_COLS * (owners * frequency % N_COLS).astype(jnp.float32)
        sum_real = jnp.einsum('jef,e->jf', blocks, jnp.cos(angles), precision=highest)
        sum_imag = -jnp.einsum('jef,e->jf', blocks, jnp.sin(angles), precision=highest)
        real_part, imag_part = twiddle(sum_real, sum_imag, columns[None, :], frequency, SLAB_COLS)
        section_one = lax.optimization_barrier(jnp.concatenate([real_part, imag_part], 1).astype(jnp.bfloat16))
        rows_spectrum = jnp.dot(section_one.astype(jnp.float32), row_table, precision=highest)
        rows_spectrum = lax.optimization_barrier(rows_spectrum.astype(jnp.bfloat16))
        values = rows_spectrum.reshape(N_ROWS, ROWS_DEV, 2, COLS_DEV).astype(jnp.float32)
        combined = jnp.einsum('kqap,abpc->kbqc', col_table, values, precision=highest)
        real_two, imag_two = twiddle(combined[:, :, 0], combined[:, :, 1], row_index[None, :, None], row_freq[:, None, None], GRID_ROWS)
        section_two = lax.optimization_barrier(jnp.stack([real_two, imag_two], 2).astype(jnp.bfloat16))
        section_two = section_two.astype(jnp.float32).reshape(N_ROWS, 2 * ROWS_DEV, COLS_DEV)
        result_spec = jnp.einsum('mn,knc->kmc', final_table, section_two, precision=highest)
        result_spec = result_spec.reshape(GRID_ROWS, 2, COLS_DEV)
        psf_block = lax.dynamic_slice_in_dim(psf_spectrum, (frequency * COLS_DEV).astype(jnp.int32), COLS_DEV, 1)
        return result_spec * psf_block.astype(jnp.float32)[:, None, :]
    spectra = lax.map(one_block, jnp.arange(N_COLS, dtype=jnp.int32))
    return spectra.transpose(1, 2, 0, 3).reshape(GRID_ROWS, 2, SLAB_COLS)
```

```python
import functools
import math

import jax
import jax.numpy as jnp
import numpy as np
from jax import lax
from jax.experimental import pallas as pl
from jax.experimental.pallas import tpu as pltpu
from jax.sharding import PartitionSpec as P


def make_table(length, factor):
    positions = jnp.arange(length, dtype=jnp.int32)
    angles = (
        2.0
        * math.pi
        / length
        * (positions[:, None] * positions[None, :] % length).astype(jnp.float32)
    )
    cosine = jnp.cos(angles) * factor
    sine_part = jnp.sin(angles) * factor
    upper_rows = jnp.stack([cosine, -sine_part], 1)
    bottom = jnp.stack([sine_part, cosine], 1)
    return jnp.stack([upper_rows, bottom], 0).astype(jnp.bfloat16)


def twiddle(real_part, imag_part, position, frequency, period):
    angles = 2.0 * math.pi / period * (position * frequency % period).astype(jnp.float32)
    cosine = jnp.cos(angles)
    sine_part = jnp.sin(angles)
    return (real_part * cosine + imag_part * sine_part, imag_part * cosine - real_part * sine_part)


def on_device(tile_density, tile_dest, tile_place, psf_spectrum):
    tile_count, tile_side, _ = tile_density.shape
    rows_dev, cols_dev = psf_spectrum.shape
    rows_n = lax.axis_size("rows")
    cols_n = lax.axis_size("cols")
    capacity = max(2, 2 * tile_count // rows_n)
    slot_total = rows_n * capacity
    target = tile_dest[:, 0]
    matches = (target[:, None] == jnp.arange(rows_n, dtype=jnp.int32)[None, :]).astype(jnp.int32)
    order_within = jnp.sum((jnp.cumsum(matches, 0) - matches) * matches, 1)
    slot_index = target * capacity + order_within
    chosen = slot_index[:, None] == jnp.arange(slot_total, dtype=jnp.int32)[None, :]
    tiles_flat = tile_density.reshape(tile_count, tile_side * tile_side)
    outgoing = jnp.einsum(
        "ts,tc->sc", chosen.astype(jnp.bfloat16), tiles_flat, preferred_element_type=jnp.float32
    ).astype(jnp.bfloat16)
    labels = jnp.sum(jnp.where(chosen, (tile_place + 1)[:, None], 0), axis=0)
    arrived, arrived_marks = (
        lax.all_to_all(outgoing, "rows", split_axis=0, concat_axis=0, tiled=True),
        lax.all_to_all(labels, "rows", split_axis=0, concat_axis=0, tiled=True),
    )
    per_row = cols_dev // tile_side
    positions_count = rows_dev // tile_side * per_row
    placement_hot = (
        arrived_marks[:, None] - 1 == jnp.arange(positions_count, dtype=jnp.int32)[None, :]
    ).astype(jnp.bfloat16)
    cell_tiles = jnp.einsum(
        "sp,sc->pc", placement_hot, arrived, preferred_element_type=jnp.float32
    ).astype(jnp.bfloat16)
    density_grid = cell_tiles.reshape(
        rows_dev // tile_side, per_row, tile_side, tile_side
    ).transpose(0, 2, 1, 3)
    density_grid = density_grid.reshape(rows_dev, cols_dev)
    me_col = lax.axis_index("cols")
    highest = lax.Precision.HIGHEST
    slab_cols = cols_dev * cols_n
    part_cols = cols_dev // cols_n
    pieces = lax.all_to_all(density_grid[None], "cols", split_axis=2, concat_axis=0, tiled=True)
    frequency = jnp.arange(cols_n, dtype=jnp.int32)
    angles = (
        2.0
        * math.pi
        / cols_n
        * (frequency[:, None] * frequency[None, :] % cols_n).astype(jnp.float32)
    )
    values = pieces.astype(jnp.float32)
    sum_real = jnp.einsum("ejt,ek->kjt", values, jnp.cos(angles), precision=highest)
    sum_imag = -jnp.einsum("ejt,ek->kjt", values, jnp.sin(angles), precision=highest)
    columns = (me_col * part_cols + jnp.arange(part_cols, dtype=jnp.int32))[None, None, :]
    real_part, imag_part = twiddle(sum_real, sum_imag, columns, frequency[:, None, None], slab_cols)
    packed = jnp.stack([real_part, imag_part], 2).astype(jnp.bfloat16)
    returned = lax.all_to_all(packed, "cols", split_axis=0, concat_axis=3, tiled=True)
    section_one = returned.reshape(rows_dev, 2 * cols_dev)
    row_table = make_table(cols_dev, 1.0 / math.sqrt(slab_cols)).reshape(2 * cols_dev, 2 * cols_dev)
    rows_spectrum = jnp.dot(section_one, row_table, preferred_element_type=jnp.float32).astype(
        jnp.bfloat16
    )
    rows_spectrum = rows_spectrum.reshape(rows_dev, 2, cols_dev)
    me_row = lax.axis_index("rows")
    group_rows = rows_dev // rows_n
    grid_rows = rows_dev * rows_n
    col_table = make_table(rows_n, 1.0).transpose(3, 2, 1, 0)
    column_block = lax.all_to_all(rows_spectrum, "rows", split_axis=0, concat_axis=0, tiled=True)
    item_width = column_block.shape[2]
    values = column_block.reshape(rows_n, group_rows, 2, item_width)
    combined = jnp.einsum("kqap,atpc->ktqc", col_table, values, preferred_element_type=jnp.float32)
    row_index = (me_row * group_rows + jnp.arange(group_rows, dtype=jnp.int32))[None, :, None]
    row_freq = jnp.arange(rows_n, dtype=jnp.int32)[:, None, None]
    real_two, imag_two = twiddle(
        combined[:, :, 0], combined[:, :, 1], row_index, row_freq, grid_rows
    )
    section_two = lax.all_to_all(
        jnp.stack([real_two, imag_two], 2).astype(jnp.bfloat16).reshape(rows_dev, 2, item_width),
        "rows",
        split_axis=0,
        concat_axis=0,
        tiled=True,
    )
    final_table = (
        make_table(rows_dev, 1.0 / math.sqrt(grid_rows))
        .transpose(3, 2, 1, 0)
        .reshape(2 * rows_dev, 2 * rows_dev)
    )
    result_spec = jnp.dot(
        final_table, section_two.reshape(2 * rows_dev, cols_dev), preferred_element_type=jnp.float32
    )
    result_spec = result_spec.reshape(rows_dev, 2, cols_dev)
    return result_spec * psf_spectrum.astype(jnp.float32)[:, None, :]


CHUNKS = 2
MESH = pl.DeviceIdType.MESH


def fits(rows_n, cols_n, tile_count, tile_side, rows_dev, cols_dev):
    return (
        cols_n == 4
        and rows_n > 1
        and tile_side * 2 == 128
        and tile_side % (rows_n * 2 * CHUNKS) == 0
        and tile_count % 16 == 0
        and tile_count <= 128
        and cols_dev % 128 == 0
        and rows_dev % tile_side == 0
        and (tile_side // rows_n // CHUNKS) * (rows_dev // tile_side) % 16 == 0
        and rows_n * rows_dev * cols_dev * 2 <= 1 << 22
    )


def constants(rows_n, cols_n, tile_side, rows_dev, cols_dev):
    slab_cols, grid_rows = cols_dev * cols_n, rows_dev * rows_n
    bands = rows_dev // tile_side
    band_rows = tile_side // rows_n
    step_rows = band_rows // CHUNKS

    def parts(phase, factor):
        angles = 2.0 * np.pi * phase
        return np.cos(angles) * factor, -np.sin(angles) * factor

    f = np.arange(cols_dev)
    re, im = parts((f[:, None] * f[None, :] % cols_dev) / cols_dev, 1.0 / math.sqrt(slab_cols))
    row_table = np.block([[re, im], [-im, re]])
    k = np.arange(cols_n)
    re, im = parts((f[None, :] * k[:, None] % slab_cols) / slab_cols, 1.0)
    twiddles = np.stack([re, -im], 1).astype(np.float32)
    b = (
        tile_side * np.arange(bands)[None, None, None, :]
        + band_rows * np.arange(rows_n)[:, None, None, None]
        + step_rows * np.arange(CHUNKS)[None, :, None, None]
        + np.arange(step_rows)[None, None, :, None]
    )
    u = np.arange(rows_n)
    row = b[:, :, None, None] + rows_dev * u[None, None, None, :, None, None]
    re, im = parts((row * u[None, None, :, None, None, None] % grid_rows) / grid_rows, 1.0)
    width = step_rows * bands
    mix = np.zeros((rows_n, CHUNKS, rows_n, 2, step_rows, bands, 2, step_rows, rows_n, bands), np.float32)
    for i in range(step_rows):
        for t in range(bands):
            mix[:, :, :, 0, i, t, 0, i, :, t] = re[:, :, :, :, i, t]
            mix[:, :, :, 0, i, t, 1, i, :, t] = -im[:, :, :, :, i, t]
            mix[:, :, :, 1, i, t, 0, i, :, t] = im[:, :, :, :, i, t]
            mix[:, :, :, 1, i, t, 1, i, :, t] = re[:, :, :, :, i, t]
    mix = mix.reshape(rows_n, CHUNKS, rows_n * 2 * width, 2 * rows_n * width)
    w = np.arange(rows_dev)
    order = b.transpose(1, 0, 2, 3).reshape(CHUNKS, rows_n, 1, width)
    re, im = parts(
        (w[:, None, None, None, None] * order % rows_dev) / rows_dev, 1.0 / math.sqrt(grid_rows)
    )
    final = np.stack(
        [np.concatenate([re, -im], 3), np.concatenate([im, re], 3)], 0
    ).reshape(2 * rows_dev, 2 * rows_dev)
    return (
        jnp.asarray(row_table.astype(jnp.bfloat16)),
        jnp.asarray(twiddles),
        jnp.asarray(mix.astype(jnp.bfloat16)),
        jnp.asarray(final.astype(jnp.bfloat16)),
    )


def exchange_kernel(
    rows_n, cols_n, tile_side, bands, per_row,
    x_ref, dest_ref, place_ref, twiddle_ref, table_hbm, mix_hbm,
    out_ref,
    labels, arrived, dense, outgoing, table, mix,
    label_send, label_recv, a_send, a_recv, g_send, g_recv, e_send, e_recv, local_sem,
):
    me_row, me_col = lax.axis_index("rows"), lax.axis_index("cols")
    tiles = x_ref.shape[0]
    chunk = arrived.shape[3]
    band = chunk * CHUNKS
    cols_dev = per_row * tile_side
    row_peers = [lax.rem(me_row + d, rows_n) for d in range(rows_n)]
    row_sources = [lax.rem(me_row + rows_n - d, rows_n) for d in range(rows_n)]
    col_peers = [lax.rem(me_col + d, cols_n) for d in range(cols_n)]

    barrier = pltpu.get_barrier_semaphore()
    for d in range(1, rows_n):
        pl.semaphore_signal(barrier, inc=1, device_id=(row_peers[d], me_col), device_id_type=MESH)
    for d in range(1, cols_n):
        pl.semaphore_signal(barrier, inc=1, device_id=(me_row, col_peers[d]), device_id_type=MESH)

    place = place_ref[...]
    code = (place % per_row) * (rows_n * bands) + dest_ref[...] * bands + place // per_row
    labels[0] = jnp.broadcast_to(
        jnp.concatenate([code, jnp.zeros((1, 128 - tiles), jnp.int32)], 1)
        if tiles < 128
        else code,
        labels.shape[1:],
    )
    pl.semaphore_wait(barrier, rows_n + cols_n - 2)

    def band_copy(h, d):
        start = pl.multiple_of(row_peers[d] * band + h * chunk, 128)
        return pltpu.make_async_remote_copy(
            src_ref=x_ref.at[:, pl.ds(start, chunk)],
            dst_ref=arrived.at[h, d],
            send_sem=a_send.at[h, d],
            recv_sem=a_recv.at[h, d],
            device_id=(row_peers[d], me_col),
            device_id_type=MESH,
        )

    label_copies = [
        pltpu.make_async_remote_copy(
            src_ref=labels.at[0],
            dst_ref=labels.at[d],
            send_sem=label_send.at[d],
            recv_sem=label_recv.at[d],
            device_id=(row_peers[d], me_col),
            device_id_type=MESH,
        )
        for d in range(1, rows_n)
    ]
    band_copies = [[band_copy(h, d) for d in range(1, rows_n)] for h in range(CHUNKS)]
    for copy in label_copies + [copy for group in band_copies for copy in group]:
        copy.start()
    own_copies = []
    for h in range(CHUNKS):
        start = pl.multiple_of(me_row * band + h * chunk, 128)
        own_copies.append(
            pltpu.make_async_copy(
                x_ref.at[:, pl.ds(start, chunk)], arrived.at[h, 0], local_sem.at[h]
            )
        )
    table_copy = pltpu.make_async_copy(table_hbm, table, local_sem.at[CHUNKS])
    mix_copy = pltpu.make_async_copy(mix_hbm.at[me_row], mix, local_sem.at[CHUNKS + 1])
    for copy in own_copies + [table_copy, mix_copy]:
        copy.start()

    for copy in label_copies:
        copy.wait_recv()
    codes = jnp.concatenate([labels[d, 0:1, 0:tiles] for d in range(rows_n)], 1)
    cells = per_row * rows_n * bands
    hot = jnp.where(
        lax.broadcasted_iota(jnp.int32, (cells, rows_n * tiles), 0) == codes, 1.0, 0.0
    ).astype(jnp.bfloat16)
    low_lanes = lax.broadcasted_iota(jnp.int32, (rows_n * bands, 128), 1) < tile_side

    gathers = []
    for h in range(CHUNKS):
        own_copies[h].wait()
        for copy in band_copies[h]:
            copy.wait_recv()
        summed = jnp.dot(
            hot,
            arrived[h].reshape(rows_n * tiles, chunk),
            preferred_element_type=jnp.float32,
        )
        height = rows_n * bands
        for pair in range(chunk // 128):
            lanes = slice(128 * pair, 128 * pair + 128)
            for q in range(per_row // 2):
                left = summed[2 * q * height : (2 * q + 1) * height, lanes]
                right = summed[(2 * q + 1) * height : (2 * q + 2) * height, lanes]
                upper = jnp.where(low_lanes, left, pltpu.roll(right, tile_side, 1))
                lower = jnp.where(low_lanes, pltpu.roll(left, tile_side, 1), right)
                out_lanes = slice(128 * q, 128 * q + 128)
                first = 2 * pair * height
                dense[h, 0, first : first + height, out_lanes] = upper.astype(jnp.bfloat16)
                dense[h, 0, first + height : first + 2 * height, out_lanes] = lower.astype(
                    jnp.bfloat16
                )
        group = [
            pltpu.make_async_remote_copy(
                src_ref=dense.at[h, 0],
                dst_ref=dense.at[h, d],
                send_sem=g_send.at[h, d],
                recv_sem=g_recv.at[h, d],
                device_id=(me_row, col_peers[d]),
                device_id_type=MESH,
            )
            for d in range(1, cols_n)
        ]
        for copy in group:
            copy.start()
        gathers.append(group)

    cosine = twiddle_ref[me_col, 0:1, :]
    sine = twiddle_ref[me_col, 1:2, :]
    table_copy.wait()
    mix_copy.wait()
    sends = []
    for h in range(CHUNKS):
        for copy in gathers[h]:
            copy.wait_recv()
        sum_real = sum_imag = None
        for d in range(cols_n):
            turn = lax.rem(lax.rem(me_col + cols_n - d, cols_n) * me_col, cols_n)
            cos_turn = jnp.where(turn == 0, 1.0, jnp.where(turn == 2, -1.0, 0.0))
            sin_turn = jnp.where(turn == 1, 1.0, jnp.where(turn == 3, -1.0, 0.0))
            value = dense[h, d].astype(jnp.float32)
            real, imag = value * cos_turn, value * (-sin_turn)
            sum_real = real if d == 0 else sum_real + real
            sum_imag = imag if d == 0 else sum_imag + imag
        section_one = jnp.concatenate(
            [sum_real * cosine + sum_imag * sine, sum_imag * cosine - sum_real * sine], 1
        ).astype(jnp.bfloat16)
        spectrum = jnp.dot(section_one, table[...], preferred_element_type=jnp.float32)
        spectrum = spectrum.astype(jnp.bfloat16)
        stacked = jnp.concatenate([spectrum[:, :cols_dev], spectrum[:, cols_dev:]], 0)
        section_two = jnp.dot(mix[h], stacked, preferred_element_type=jnp.float32)
        outgoing[h] = section_two.astype(jnp.bfloat16).reshape(outgoing.shape[1:])
        group = [
            pltpu.make_async_remote_copy(
                src_ref=outgoing.at[h, row_peers[d]],
                dst_ref=out_ref.at[h, me_row],
                send_sem=e_send.at[h, d],
                recv_sem=e_recv.at[h, d],
                device_id=(row_peers[d], me_col),
                device_id_type=MESH,
            )
            for d in range(1, rows_n)
        ]
        for copy in group:
            copy.start()
        own = pltpu.make_async_copy(
            outgoing.at[h, me_row], out_ref.at[h, me_row], local_sem.at[CHUNKS + 2 + h]
        )
        own.start()
        sends.append((group, own))

    for copy in label_copies:
        copy.wait_send()
    for h in range(CHUNKS):
        for copy in band_copies[h] + gathers[h]:
            copy.wait_send()
    for h in range(CHUNKS):
        group, own = sends[h]
        own.wait()
        for d in range(1, rows_n):
            pltpu.make_async_remote_copy(
                src_ref=outgoing.at[h, row_peers[d]],
                dst_ref=out_ref.at[h, row_sources[d]],
                send_sem=e_send.at[h, d],
                recv_sem=e_recv.at[h, d],
                device_id=(row_peers[d], me_col),
                device_id_type=MESH,
            ).wait()


def final_kernel(final_ref, section_ref, psf_ref, out_ref):
    rows_dev = psf_ref.shape[0]
    result = jnp.dot(final_ref[...], section_ref[...], preferred_element_type=jnp.float32)
    psf = psf_ref[...].astype(jnp.float32)
    out_ref[:, 0, :] = result[:rows_dev] * psf
    out_ref[:, 1, :] = result[rows_dev:] * psf


def on_device_kernels(tile_density, tile_dest, tile_place, psf_spectrum):
    tile_count, tile_side, _ = tile_density.shape
    rows_dev, cols_dev = psf_spectrum.shape
    rows_n = lax.axis_size("rows")
    cols_n = lax.axis_size("cols")
    bands, per_row = rows_dev // tile_side, cols_dev // tile_side
    step_rows = tile_side // rows_n // CHUNKS
    chunk = step_rows * tile_side
    row_table, twiddles, mix, final = constants(rows_n, cols_n, tile_side, rows_dev, cols_dev)
    bf16 = jnp.bfloat16
    vmem = pl.BlockSpec(memory_space=pltpu.VMEM)
    anywhere = pl.BlockSpec(memory_space=pl.ANY)
    width = 2 * step_rows * bands
    dma = pltpu.SemaphoreType.DMA
    section = pl.pallas_call(
        functools.partial(exchange_kernel, rows_n, cols_n, tile_side, bands, per_row),
        out_shape=jax.ShapeDtypeStruct((CHUNKS, rows_n, width, cols_dev), bf16),
        in_specs=[vmem, vmem, vmem, vmem, anywhere, anywhere],
        out_specs=vmem,
        scratch_shapes=[
            pltpu.VMEM((rows_n, 8, 128), jnp.int32),
            pltpu.VMEM((CHUNKS, rows_n, tile_count, chunk), bf16),
            pltpu.VMEM((CHUNKS, cols_n, step_rows * rows_n * bands, cols_dev), bf16),
            pltpu.VMEM((CHUNKS, rows_n, width, cols_dev), bf16),
            pltpu.VMEM(row_table.shape, bf16),
            pltpu.VMEM(mix.shape[1:], bf16),
            dma((rows_n,)),
            dma((rows_n,)),
            dma((CHUNKS, rows_n)),
            dma((CHUNKS, rows_n)),
            dma((CHUNKS, cols_n)),
            dma((CHUNKS, cols_n)),
            dma((CHUNKS, rows_n)),
            dma((CHUNKS, rows_n)),
            dma((2 * CHUNKS + 2,)),
        ],
        compiler_params=pltpu.CompilerParams(
            collective_id=0, has_side_effects=True, vmem_limit_bytes=48 << 20
        ),
    )(
        tile_density.reshape(tile_count, tile_side * tile_side),
        tile_dest.reshape(1, tile_count),
        tile_place.reshape(1, tile_count),
        twiddles,
        row_table,
        mix,
    )
    return pl.pallas_call(
        final_kernel,
        out_shape=jax.ShapeDtypeStruct((rows_dev, 2, cols_dev), jnp.float32),
        in_specs=[vmem, vmem, vmem],
        out_specs=vmem,
        compiler_params=pltpu.CompilerParams(vmem_limit_bytes=32 << 20),
    )(final, section.reshape(2 * rows_dev, cols_dev), psf_spectrum)


def solution(mesh):
    in_specs = (
        P(("rows", "cols"), None, None),
        P(("rows", "cols"), None),
        P(("rows", "cols")),
        P("rows", "cols"),
    )
    out_specs = P("rows", None, "cols")

    def local(tile_density, tile_dest, tile_place, psf_spectrum):
        fast = fits(
            lax.axis_size("rows"),
            lax.axis_size("cols"),
            *tile_density.shape[:2],
            *psf_spectrum.shape,
        )
        run = on_device_kernels if fast else on_device
        return run(tile_density, tile_dest, tile_place, psf_spectrum)

    return jax.shard_map(
        local, mesh=mesh, in_specs=in_specs, out_specs=out_specs, check_vma=False
    )
```

```python
import functools
import math

import jax
import jax.numpy as jnp
import numpy as np
from jax import lax
from jax.experimental import pallas as pl
from jax.experimental.pallas import tpu as pltpu
from jax.sharding import PartitionSpec as P


def make_table(length, factor):
    positions = jnp.arange(length, dtype=jnp.int32)
    angles = (
        2.0
        * math.pi
        / length
        * (positions[:, None] * positions[None, :] % length).astype(jnp.float32)
    )
    cosine = jnp.cos(angles) * factor
    sine_part = jnp.sin(angles) * factor
    upper_rows = jnp.stack([cosine, -sine_part], 1)
    bottom = jnp.stack([sine_part, cosine], 1)
    return jnp.stack([upper_rows, bottom], 0).astype(jnp.bfloat16)


def twiddle(real_part, imag_part, position, frequency, period):
    angles = 2.0 * math.pi / period * (position * frequency % period).astype(jnp.float32)
    cosine = jnp.cos(angles)
    sine_part = jnp.sin(angles)
    return (real_part * cosine + imag_part * sine_part, imag_part * cosine - real_part * sine_part)


def on_device(tile_density, tile_dest, tile_place, psf_spectrum):
    tile_count, tile_side, _ = tile_density.shape
    rows_dev, cols_dev = psf_spectrum.shape
    rows_n = lax.axis_size("rows")
    cols_n = lax.axis_size("cols")
    capacity = max(2, 2 * tile_count // rows_n)
    slot_total = rows_n * capacity
    target = tile_dest[:, 0]
    matches = (target[:, None] == jnp.arange(rows_n, dtype=jnp.int32)[None, :]).astype(jnp.int32)
    order_within = jnp.sum((jnp.cumsum(matches, 0) - matches) * matches, 1)
    slot_index = target * capacity + order_within
    chosen = slot_index[:, None] == jnp.arange(slot_total, dtype=jnp.int32)[None, :]
    tiles_flat = tile_density.reshape(tile_count, tile_side * tile_side)
    outgoing = jnp.einsum(
        "ts,tc->sc", chosen.astype(jnp.bfloat16), tiles_flat, preferred_element_type=jnp.float32
    ).astype(jnp.bfloat16)
    labels = jnp.sum(jnp.where(chosen, (tile_place + 1)[:, None], 0), axis=0)
    arrived, arrived_marks = (
        lax.all_to_all(outgoing, "rows", split_axis=0, concat_axis=0, tiled=True),
        lax.all_to_all(labels, "rows", split_axis=0, concat_axis=0, tiled=True),
    )
    per_row = cols_dev // tile_side
    positions_count = rows_dev // tile_side * per_row
    placement_hot = (
        arrived_marks[:, None] - 1 == jnp.arange(positions_count, dtype=jnp.int32)[None, :]
    ).astype(jnp.bfloat16)
    cell_tiles = jnp.einsum(
        "sp,sc->pc", placement_hot, arrived, preferred_element_type=jnp.float32
    ).astype(jnp.bfloat16)
    density_grid = cell_tiles.reshape(
        rows_dev // tile_side, per_row, tile_side, tile_side
    ).transpose(0, 2, 1, 3)
    density_grid = density_grid.reshape(rows_dev, cols_dev)
    me_col = lax.axis_index("cols")
    highest = lax.Precision.HIGHEST
    slab_cols = cols_dev * cols_n
    part_cols = cols_dev // cols_n
    pieces = lax.all_to_all(density_grid[None], "cols", split_axis=2, concat_axis=0, tiled=True)
    frequency = jnp.arange(cols_n, dtype=jnp.int32)
    angles = (
        2.0
        * math.pi
        / cols_n
        * (frequency[:, None] * frequency[None, :] % cols_n).astype(jnp.float32)
    )
    values = pieces.astype(jnp.float32)
    sum_real = jnp.einsum("ejt,ek->kjt", values, jnp.cos(angles), precision=highest)
    sum_imag = -jnp.einsum("ejt,ek->kjt", values, jnp.sin(angles), precision=highest)
    columns = (me_col * part_cols + jnp.arange(part_cols, dtype=jnp.int32))[None, None, :]
    real_part, imag_part = twiddle(sum_real, sum_imag, columns, frequency[:, None, None], slab_cols)
    packed = jnp.stack([real_part, imag_part], 2).astype(jnp.bfloat16)
    returned = lax.all_to_all(packed, "cols", split_axis=0, concat_axis=3, tiled=True)
    section_one = returned.reshape(rows_dev, 2 * cols_dev)
    row_table = make_table(cols_dev, 1.0 / math.sqrt(slab_cols)).reshape(2 * cols_dev, 2 * cols_dev)
    rows_spectrum = jnp.dot(section_one, row_table, preferred_element_type=jnp.float32).astype(
        jnp.bfloat16
    )
    rows_spectrum = rows_spectrum.reshape(rows_dev, 2, cols_dev)
    me_row = lax.axis_index("rows")
    group_rows = rows_dev // rows_n
    grid_rows = rows_dev * rows_n
    col_table = make_table(rows_n, 1.0).transpose(3, 2, 1, 0)
    column_block = lax.all_to_all(rows_spectrum, "rows", split_axis=0, concat_axis=0, tiled=True)
    item_width = column_block.shape[2]
    values = column_block.reshape(rows_n, group_rows, 2, item_width)
    combined = jnp.einsum("kqap,atpc->ktqc", col_table, values, preferred_element_type=jnp.float32)
    row_index = (me_row * group_rows + jnp.arange(group_rows, dtype=jnp.int32))[None, :, None]
    row_freq = jnp.arange(rows_n, dtype=jnp.int32)[:, None, None]
    real_two, imag_two = twiddle(
        combined[:, :, 0], combined[:, :, 1], row_index, row_freq, grid_rows
    )
    section_two = lax.all_to_all(
        jnp.stack([real_two, imag_two], 2).astype(jnp.bfloat16).reshape(rows_dev, 2, item_width),
        "rows",
        split_axis=0,
        concat_axis=0,
        tiled=True,
    )
    final_table = (
        make_table(rows_dev, 1.0 / math.sqrt(grid_rows))
        .transpose(3, 2, 1, 0)
        .reshape(2 * rows_dev, 2 * rows_dev)
    )
    result_spec = jnp.dot(
        final_table, section_two.reshape(2 * rows_dev, cols_dev), preferred_element_type=jnp.float32
    )
    result_spec = result_spec.reshape(rows_dev, 2, cols_dev)
    return result_spec * psf_spectrum.astype(jnp.float32)[:, None, :]


CHUNKS = 2
MESH = pl.DeviceIdType.MESH


def fits(rows_n, cols_n, tile_count, tile_side, rows_dev, cols_dev):
    return (
        cols_n == 4
        and rows_n > 1
        and tile_side * 2 == 128
        and tile_side % (rows_n * 2 * CHUNKS) == 0
        and tile_count % 16 == 0
        and tile_count <= 128
        and cols_dev % 128 == 0
        and rows_dev % tile_side == 0
        and (tile_side // rows_n // CHUNKS) * (rows_dev // tile_side) % 16 == 0
        and 2 * cols_dev % (2 * tile_side // CHUNKS * (rows_dev // tile_side)) == 0
        and rows_n * rows_dev * cols_dev * 2 <= 1 << 22
    )


def constants(rows_n, cols_n, tile_side, rows_dev, cols_dev):
    slab_cols, grid_rows = cols_dev * cols_n, rows_dev * rows_n
    bands = rows_dev // tile_side
    band_rows = tile_side // rows_n
    step_rows = band_rows // CHUNKS

    def parts(phase, factor):
        angles = 2.0 * np.pi * phase
        return np.cos(angles) * factor, -np.sin(angles) * factor

    f = np.arange(cols_dev)
    re, im = parts((f[:, None] * f[None, :] % cols_dev) / cols_dev, 1.0 / math.sqrt(slab_cols))
    row_table = np.block([[re, im], [-im, re]])
    bf16 = jnp.bfloat16
    k = np.arange(cols_n)
    re, im = parts((f[None, :] * k[:, None] % slab_cols) / slab_cols, 1.0)
    pair = np.concatenate([re, -im], 1)
    upper = pair.astype(bf16).astype(np.float64)
    extra = np.zeros((16, 2 * cols_dev))
    extra[: 2 * cols_n] = np.stack([upper, pair - upper], 1).reshape(2 * cols_n, -1)
    row_table = np.concatenate([row_table, extra], 0)
    b = (
        tile_side * np.arange(bands)[None, None, None, :]
        + band_rows * np.arange(rows_n)[:, None, None, None]
        + step_rows * np.arange(CHUNKS)[None, :, None, None]
        + np.arange(step_rows)[None, None, :, None]
    )
    u = np.arange(rows_n)
    row = b[:, :, None, None] + rows_dev * u[None, None, None, :, None, None]
    re, im = parts((row * u[None, None, :, None, None, None] % grid_rows) / grid_rows, 1.0)
    width = step_rows * bands
    mix = np.zeros((rows_n, CHUNKS, rows_n, 2, step_rows, bands, 2, step_rows, rows_n, bands), np.float32)
    for i in range(step_rows):
        for t in range(bands):
            mix[:, :, :, 0, i, t, 0, i, :, t] = re[:, :, :, :, i, t]
            mix[:, :, :, 0, i, t, 1, i, :, t] = -im[:, :, :, :, i, t]
            mix[:, :, :, 1, i, t, 0, i, :, t] = im[:, :, :, :, i, t]
            mix[:, :, :, 1, i, t, 1, i, :, t] = re[:, :, :, :, i, t]
    mix = mix.reshape(rows_n, CHUNKS, rows_n * 2 * width, 2 * rows_n * width)
    w = np.arange(rows_dev)
    order = b.transpose(1, 0, 2, 3).reshape(CHUNKS, rows_n, 1, width)
    re, im = parts(
        (w[:, None, None, None, None] * order % rows_dev) / rows_dev, 1.0 / math.sqrt(grid_rows)
    )
    final = np.stack(
        [np.concatenate([re, -im], 3), np.concatenate([im, re], 3)], 0
    ).reshape(2 * rows_dev, 2 * rows_dev)
    lanes = mix.shape[-1]
    blocks = [row_table[:, at : at + lanes] for at in range(0, row_table.shape[1], lanes)]
    tables = np.concatenate(blocks + [mix.reshape(-1, lanes)], 0)
    return jnp.asarray(tables.astype(bf16)), jnp.asarray(final.astype(bf16))


def exchange_kernel(
    rows_n, cols_n, tile_side, bands, per_row,
    x_ref, dest_hbm, place_hbm, tables_hbm,
    out_ref,
    owned, labels, arrived, dense, outgoing, table, mix,
    label_send, label_recv, a_send, a_recv, g_send, g_recv, e_send, e_recv, local_sem, table_sem,
):
    me_row, me_col = lax.axis_index("rows"), lax.axis_index("cols")
    tiles = x_ref.shape[0]
    chunk = arrived.shape[3]
    band = chunk * CHUNKS
    cols_dev = per_row * tile_side
    row_peers = [lax.rem(me_row + d, rows_n) for d in range(rows_n)]
    row_sources = [lax.rem(me_row + rows_n - d, rows_n) for d in range(rows_n)]
    col_peers = [lax.rem(me_col + d, cols_n) for d in range(cols_n)]

    barrier = pltpu.get_barrier_semaphore()
    for d in range(1, rows_n):
        pl.semaphore_signal(barrier, inc=1, device_id=(row_peers[d], me_col), device_id_type=MESH)
    for d in range(1, cols_n):
        pl.semaphore_signal(barrier, inc=1, device_id=(me_row, col_peers[d]), device_id_type=MESH)

    owned_copies = [
        pltpu.make_async_copy(dest_hbm, owned.at[0], local_sem.at[2 * CHUNKS + 2]),
        pltpu.make_async_copy(place_hbm, owned.at[1], local_sem.at[2 * CHUNKS + 3]),
    ]
    table_rows, lanes = table.shape[0], mix.shape[1]
    table_copies = [
        pltpu.make_async_copy(
            tables_hbm.at[pl.ds(j * table_rows, table_rows), :],
            table.at[:, pl.ds(j * lanes, lanes)],
            table_sem.at[j],
        )
        for j in range(table.shape[1] // lanes)
    ]
    mix_start = table_rows * len(table_copies) + me_row * mix.shape[0]
    mix_copy = pltpu.make_async_copy(
        tables_hbm.at[pl.ds(pl.multiple_of(mix_start, 16), mix.shape[0]), :],
        mix,
        local_sem.at[CHUNKS],
    )
    for copy in owned_copies + table_copies + [mix_copy]:
        copy.start()
    for copy in owned_copies:
        copy.wait()
    slab, place = owned[0], owned[1]
    code = (place % per_row) * (rows_n * bands) + slab * bands + place // per_row
    labels[0] = jnp.broadcast_to(
        jnp.concatenate([code, jnp.zeros((1, 128 - tiles), jnp.int32)], 1)
        if tiles < 128
        else code,
        labels.shape[1:],
    )
    pl.semaphore_wait(barrier, rows_n + cols_n - 2)

    def band_copy(h, d):
        start = pl.multiple_of(row_peers[d] * band + h * chunk, 128)
        return pltpu.make_async_remote_copy(
            src_ref=x_ref.at[:, pl.ds(start, chunk)],
            dst_ref=arrived.at[h, d],
            send_sem=a_send.at[h, d],
            recv_sem=a_recv.at[h, d],
            device_id=(row_peers[d], me_col),
            device_id_type=MESH,
        )

    label_copies = [
        pltpu.make_async_remote_copy(
            src_ref=labels.at[0],
            dst_ref=labels.at[d],
            send_sem=label_send.at[d],
            recv_sem=label_recv.at[d],
            device_id=(row_peers[d], me_col),
            device_id_type=MESH,
        )
        for d in range(1, rows_n)
    ]
    band_copies = [[band_copy(h, d) for d in range(1, rows_n)] for h in range(CHUNKS)]
    for copy in label_copies + [copy for group in band_copies for copy in group]:
        copy.start()
    own_copies = []
    for h in range(CHUNKS):
        start = pl.multiple_of(me_row * band + h * chunk, 128)
        own_copies.append(
            pltpu.make_async_copy(
                x_ref.at[:, pl.ds(start, chunk)], arrived.at[h, 0], local_sem.at[h]
            )
        )
    for copy in own_copies:
        copy.start()

    for copy in label_copies:
        copy.wait_recv()
    codes = jnp.concatenate([labels[d, 0:1, 0:tiles] for d in range(rows_n)], 1)
    cells = per_row * rows_n * bands
    hot = jnp.where(
        lax.broadcasted_iota(jnp.int32, (cells, rows_n * tiles), 0) == codes, 1.0, 0.0
    ).astype(jnp.bfloat16)
    low_lanes = lax.broadcasted_iota(jnp.int32, (rows_n * bands, 128), 1) < tile_side

    gathers = []
    for h in range(CHUNKS):
        own_copies[h].wait()
        for copy in band_copies[h]:
            copy.wait_recv()
        summed = jnp.dot(
            hot,
            arrived[h].reshape(rows_n * tiles, chunk),
            preferred_element_type=jnp.float32,
        )
        height = rows_n * bands
        for pair in range(chunk // 128):
            lanes = slice(128 * pair, 128 * pair + 128)
            for q in range(per_row // 2):
                left = summed[2 * q * height : (2 * q + 1) * height, lanes]
                right = summed[(2 * q + 1) * height : (2 * q + 2) * height, lanes]
                upper = jnp.where(low_lanes, left, pltpu.roll(right, tile_side, 1))
                lower = jnp.where(low_lanes, pltpu.roll(left, tile_side, 1), right)
                out_lanes = slice(128 * q, 128 * q + 128)
                first = 2 * pair * height
                dense[h, 0, first : first + height, out_lanes] = upper.astype(jnp.bfloat16)
                dense[h, 0, first + height : first + 2 * height, out_lanes] = lower.astype(
                    jnp.bfloat16
                )
        group = [
            pltpu.make_async_remote_copy(
                src_ref=dense.at[h, 0],
                dst_ref=dense.at[h, d],
                send_sem=g_send.at[h, d],
                recv_sem=g_recv.at[h, d],
                device_id=(me_row, col_peers[d]),
                device_id_type=MESH,
            )
            for d in range(1, cols_n)
        ]
        for copy in group:
            copy.start()
        gathers.append(group)

    for copy in table_copies:
        copy.wait()
    mix_copy.wait()
    terms = table[2 * cols_dev :, :].astype(jnp.float32)
    row = lax.broadcasted_iota(jnp.int32, terms.shape, 0)
    twiddle_pair = jnp.sum(jnp.where(row // 2 == me_col, terms, 0.0), axis=0, keepdims=True)
    mix_rows = mix.shape[0] // CHUNKS
    cosine, sine = twiddle_pair[:, :cols_dev], twiddle_pair[:, cols_dev:]
    sends = []
    for h in range(CHUNKS):
        for copy in gathers[h]:
            copy.wait_recv()
        sum_real = sum_imag = None
        for d in range(cols_n):
            turn = lax.rem(lax.rem(me_col + cols_n - d, cols_n) * me_col, cols_n)
            cos_turn = jnp.where(turn == 0, 1.0, jnp.where(turn == 2, -1.0, 0.0))
            sin_turn = jnp.where(turn == 1, 1.0, jnp.where(turn == 3, -1.0, 0.0))
            value = dense[h, d].astype(jnp.float32)
            real, imag = value * cos_turn, value * (-sin_turn)
            sum_real = real if d == 0 else sum_real + real
            sum_imag = imag if d == 0 else sum_imag + imag
        section_one = jnp.concatenate(
            [sum_real * cosine + sum_imag * sine, sum_imag * cosine - sum_real * sine], 1
        ).astype(jnp.bfloat16)
        spectrum = jnp.dot(section_one, table[0 : 2 * cols_dev, :], preferred_element_type=jnp.float32)
        spectrum = spectrum.astype(jnp.bfloat16)
        stacked = jnp.concatenate([spectrum[:, :cols_dev], spectrum[:, cols_dev:]], 0)
        section_two = jnp.dot(
            mix[h * mix_rows : (h + 1) * mix_rows, :], stacked, preferred_element_type=jnp.float32
        )
        outgoing[h] = section_two.astype(jnp.bfloat16).reshape(outgoing.shape[1:])
        group = [
            pltpu.make_async_remote_copy(
                src_ref=outgoing.at[h, row_peers[d]],
                dst_ref=out_ref.at[h, me_row],
                send_sem=e_send.at[h, d],
                recv_sem=e_recv.at[h, d],
                device_id=(row_peers[d], me_col),
                device_id_type=MESH,
            )
            for d in range(1, rows_n)
        ]
        for copy in group:
            copy.start()
        own = pltpu.make_async_copy(
            outgoing.at[h, me_row], out_ref.at[h, me_row], local_sem.at[CHUNKS + 2 + h]
        )
        own.start()
        sends.append((group, own))

    for copy in label_copies:
        copy.wait_send()
    for h in range(CHUNKS):
        for copy in band_copies[h] + gathers[h]:
            copy.wait_send()
    for h in range(CHUNKS):
        group, own = sends[h]
        own.wait()
        for d in range(1, rows_n):
            pltpu.make_async_remote_copy(
                src_ref=outgoing.at[h, row_peers[d]],
                dst_ref=out_ref.at[h, row_sources[d]],
                send_sem=e_send.at[h, d],
                recv_sem=e_recv.at[h, d],
                device_id=(row_peers[d], me_col),
                device_id_type=MESH,
            ).wait()


def final_kernel(final_ref, section_ref, psf_ref, out_ref):
    rows_dev = psf_ref.shape[0]
    result = jnp.dot(final_ref[...], section_ref[...], preferred_element_type=jnp.float32)
    psf = psf_ref[...].astype(jnp.float32)
    out_ref[:, 0, :] = result[:rows_dev] * psf
    out_ref[:, 1, :] = result[rows_dev:] * psf


def on_device_kernels(tile_density, tile_dest, tile_place, psf_spectrum):
    tile_count, tile_side, _ = tile_density.shape
    rows_dev, cols_dev = psf_spectrum.shape
    rows_n = lax.axis_size("rows")
    cols_n = lax.axis_size("cols")
    bands, per_row = rows_dev // tile_side, cols_dev // tile_side
    step_rows = tile_side // rows_n // CHUNKS
    chunk = step_rows * tile_side
    tables, final = constants(rows_n, cols_n, tile_side, rows_dev, cols_dev)
    bf16 = jnp.bfloat16
    vmem = pl.BlockSpec(memory_space=pltpu.VMEM)
    anywhere = pl.BlockSpec(memory_space=pl.ANY)
    width = 2 * step_rows * bands
    mix_side = width * rows_n
    dma = pltpu.SemaphoreType.DMA
    section = pl.pallas_call(
        functools.partial(exchange_kernel, rows_n, cols_n, tile_side, bands, per_row),
        out_shape=jax.ShapeDtypeStruct((CHUNKS, rows_n, width, cols_dev), bf16),
        in_specs=[anywhere] * 4,
        out_specs=vmem,
        scratch_shapes=[
            pltpu.VMEM((2, 1, tile_count), jnp.int32),
            pltpu.VMEM((rows_n, 8, 128), jnp.int32),
            pltpu.VMEM((CHUNKS, rows_n, tile_count, chunk), bf16),
            pltpu.VMEM((CHUNKS, cols_n, step_rows * rows_n * bands, cols_dev), bf16),
            pltpu.VMEM((CHUNKS, rows_n, width, cols_dev), bf16),
            pltpu.VMEM((2 * cols_dev + 16, 2 * cols_dev), bf16),
            pltpu.VMEM((CHUNKS * mix_side, mix_side), bf16),
            dma((rows_n,)),
            dma((rows_n,)),
            dma((CHUNKS, rows_n)),
            dma((CHUNKS, rows_n)),
            dma((CHUNKS, cols_n)),
            dma((CHUNKS, cols_n)),
            dma((CHUNKS, rows_n)),
            dma((CHUNKS, rows_n)),
            dma((2 * CHUNKS + 4,)),
            dma((2 * cols_dev // mix_side,)),
        ],
        compiler_params=pltpu.CompilerParams(
            collective_id=0, has_side_effects=True, vmem_limit_bytes=58 << 20
        ),
    )(
        tile_density.reshape(tile_count, tile_side * tile_side),
        tile_dest.reshape(1, tile_count),
        tile_place.reshape(1, tile_count),
        tables,
    )
    return pl.pallas_call(
        final_kernel,
        out_shape=jax.ShapeDtypeStruct((rows_dev, 2, cols_dev), jnp.float32),
        in_specs=[vmem, vmem, vmem],
        out_specs=vmem,
        compiler_params=pltpu.CompilerParams(vmem_limit_bytes=32 << 20),
    )(final, section.reshape(2 * rows_dev, cols_dev), psf_spectrum)


def solution(mesh):
    in_specs = (
        P(("rows", "cols"), None, None),
        P(("rows", "cols"), None),
        P(("rows", "cols")),
        P("rows", "cols"),
    )
    out_specs = P("rows", None, "cols")

    def local(tile_density, tile_dest, tile_place, psf_spectrum):
        fast = fits(
            lax.axis_size("rows"),
            lax.axis_size("cols"),
            *tile_density.shape[:2],
            *psf_spectrum.shape,
        )
        run = on_device_kernels if fast else on_device
        return run(tile_density, tile_dest, tile_place, psf_spectrum)

    return jax.shard_map(
        local, mesh=mesh, in_specs=in_specs, out_specs=out_specs, check_vma=False
    )
```

```python
import functools
import math

import jax
import jax.numpy as jnp
import numpy as np
from jax import lax
from jax.experimental import pallas as pl
from jax.experimental.pallas import tpu as pltpu
from jax.sharding import PartitionSpec as P


def make_table(length, factor):
    positions = jnp.arange(length, dtype=jnp.int32)
    angles = (
        2.0
        * math.pi
        / length
        * (positions[:, None] * positions[None, :] % length).astype(jnp.float32)
    )
    cosine = jnp.cos(angles) * factor
    sine_part = jnp.sin(angles) * factor
    upper_rows = jnp.stack([cosine, -sine_part], 1)
    bottom = jnp.stack([sine_part, cosine], 1)
    return jnp.stack([upper_rows, bottom], 0).astype(jnp.bfloat16)


def twiddle(real_part, imag_part, position, frequency, period):
    angles = 2.0 * math.pi / period * (position * frequency % period).astype(jnp.float32)
    cosine = jnp.cos(angles)
    sine_part = jnp.sin(angles)
    return (real_part * cosine + imag_part * sine_part, imag_part * cosine - real_part * sine_part)


def on_device(tile_density, tile_dest, tile_place, psf_spectrum):
    tile_count, tile_side, _ = tile_density.shape
    rows_dev, cols_dev = psf_spectrum.shape
    rows_n = lax.axis_size("rows")
    cols_n = lax.axis_size("cols")
    capacity = max(2, 2 * tile_count // rows_n)
    slot_total = rows_n * capacity
    target = tile_dest[:, 0]
    matches = (target[:, None] == jnp.arange(rows_n, dtype=jnp.int32)[None, :]).astype(jnp.int32)
    order_within = jnp.sum((jnp.cumsum(matches, 0) - matches) * matches, 1)
    slot_index = target * capacity + order_within
    chosen = slot_index[:, None] == jnp.arange(slot_total, dtype=jnp.int32)[None, :]
    tiles_flat = tile_density.reshape(tile_count, tile_side * tile_side)
    outgoing = jnp.einsum(
        "ts,tc->sc", chosen.astype(jnp.bfloat16), tiles_flat, preferred_element_type=jnp.float32
    ).astype(jnp.bfloat16)
    labels = jnp.sum(jnp.where(chosen, (tile_place + 1)[:, None], 0), axis=0)
    arrived, arrived_marks = (
        lax.all_to_all(outgoing, "rows", split_axis=0, concat_axis=0, tiled=True),
        lax.all_to_all(labels, "rows", split_axis=0, concat_axis=0, tiled=True),
    )
    per_row = cols_dev // tile_side
    positions_count = rows_dev // tile_side * per_row
    placement_hot = (
        arrived_marks[:, None] - 1 == jnp.arange(positions_count, dtype=jnp.int32)[None, :]
    ).astype(jnp.bfloat16)
    cell_tiles = jnp.einsum(
        "sp,sc->pc", placement_hot, arrived, preferred_element_type=jnp.float32
    ).astype(jnp.bfloat16)
    density_grid = cell_tiles.reshape(
        rows_dev // tile_side, per_row, tile_side, tile_side
    ).transpose(0, 2, 1, 3)
    density_grid = density_grid.reshape(rows_dev, cols_dev)
    me_col = lax.axis_index("cols")
    highest = lax.Precision.HIGHEST
    slab_cols = cols_dev * cols_n
    part_cols = cols_dev // cols_n
    pieces = lax.all_to_all(density_grid[None], "cols", split_axis=2, concat_axis=0, tiled=True)
    frequency = jnp.arange(cols_n, dtype=jnp.int32)
    angles = (
        2.0
        * math.pi
        / cols_n
        * (frequency[:, None] * frequency[None, :] % cols_n).astype(jnp.float32)
    )
    values = pieces.astype(jnp.float32)
    sum_real = jnp.einsum("ejt,ek->kjt", values, jnp.cos(angles), precision=highest)
    sum_imag = -jnp.einsum("ejt,ek->kjt", values, jnp.sin(angles), precision=highest)
    columns = (me_col * part_cols + jnp.arange(part_cols, dtype=jnp.int32))[None, None, :]
    real_part, imag_part = twiddle(sum_real, sum_imag, columns, frequency[:, None, None], slab_cols)
    packed = jnp.stack([real_part, imag_part], 2).astype(jnp.bfloat16)
    returned = lax.all_to_all(packed, "cols", split_axis=0, concat_axis=3, tiled=True)
    section_one = returned.reshape(rows_dev, 2 * cols_dev)
    row_table = make_table(cols_dev, 1.0 / math.sqrt(slab_cols)).reshape(2 * cols_dev, 2 * cols_dev)
    rows_spectrum = jnp.dot(section_one, row_table, preferred_element_type=jnp.float32).astype(
        jnp.bfloat16
    )
    rows_spectrum = rows_spectrum.reshape(rows_dev, 2, cols_dev)
    me_row = lax.axis_index("rows")
    group_rows = rows_dev // rows_n
    grid_rows = rows_dev * rows_n
    col_table = make_table(rows_n, 1.0).transpose(3, 2, 1, 0)
    column_block = lax.all_to_all(rows_spectrum, "rows", split_axis=0, concat_axis=0, tiled=True)
    item_width = column_block.shape[2]
    values = column_block.reshape(rows_n, group_rows, 2, item_width)
    combined = jnp.einsum("kqap,atpc->ktqc", col_table, values, preferred_element_type=jnp.float32)
    row_index = (me_row * group_rows + jnp.arange(group_rows, dtype=jnp.int32))[None, :, None]
    row_freq = jnp.arange(rows_n, dtype=jnp.int32)[:, None, None]
    real_two, imag_two = twiddle(
        combined[:, :, 0], combined[:, :, 1], row_index, row_freq, grid_rows
    )
    section_two = lax.all_to_all(
        jnp.stack([real_two, imag_two], 2).astype(jnp.bfloat16).reshape(rows_dev, 2, item_width),
        "rows",
        split_axis=0,
        concat_axis=0,
        tiled=True,
    )
    final_table = (
        make_table(rows_dev, 1.0 / math.sqrt(grid_rows))
        .transpose(3, 2, 1, 0)
        .reshape(2 * rows_dev, 2 * rows_dev)
    )
    result_spec = jnp.dot(
        final_table, section_two.reshape(2 * rows_dev, cols_dev), preferred_element_type=jnp.float32
    )
    result_spec = result_spec.reshape(rows_dev, 2, cols_dev)
    return result_spec * psf_spectrum.astype(jnp.float32)[:, None, :]


CHUNKS = 4
TABLE_LANES = 256
MESH = pl.DeviceIdType.MESH


def fits(rows_n, cols_n, tile_count, tile_side, rows_dev, cols_dev):
    return (
        cols_n == 4
        and rows_n > 1
        and tile_side * 2 == 128
        and tile_side % (rows_n * 2 * CHUNKS) == 0
        and tile_count % 16 == 0
        and tile_count <= 128
        and cols_dev % 128 == 0
        and rows_dev % tile_side == 0
        and 2 * (tile_side // rows_n // CHUNKS) * (rows_dev // tile_side) % 16 == 0
        and 2 * tile_side // CHUNKS * (rows_dev // tile_side) <= TABLE_LANES
        and 2 * cols_dev % TABLE_LANES == 0
        and rows_n * rows_dev * cols_dev * 2 <= 1 << 22
    )


def constants(rows_n, cols_n, tile_side, rows_dev, cols_dev):
    slab_cols, grid_rows = cols_dev * cols_n, rows_dev * rows_n
    bands = rows_dev // tile_side
    band_rows = tile_side // rows_n
    step_rows = band_rows // CHUNKS

    def parts(phase, factor):
        angles = 2.0 * np.pi * phase
        return np.cos(angles) * factor, -np.sin(angles) * factor

    f = np.arange(cols_dev)
    re, im = parts((f[:, None] * f[None, :] % cols_dev) / cols_dev, 1.0 / math.sqrt(slab_cols))
    row_table = np.block([[re, im], [-im, re]])
    bf16 = jnp.bfloat16
    k = np.arange(cols_n)
    re, im = parts((f[None, :] * k[:, None] % slab_cols) / slab_cols, 1.0)
    pair = np.concatenate([re, -im], 1)
    upper = pair.astype(bf16).astype(np.float64)
    extra = np.zeros((16, 2 * cols_dev))
    extra[: 2 * cols_n] = np.stack([upper, pair - upper], 1).reshape(2 * cols_n, -1)
    row_table = np.concatenate([row_table, extra], 0)
    b = (
        tile_side * np.arange(bands)[None, None, None, :]
        + band_rows * np.arange(rows_n)[:, None, None, None]
        + step_rows * np.arange(CHUNKS)[None, :, None, None]
        + np.arange(step_rows)[None, None, :, None]
    )
    u = np.arange(rows_n)
    row = b[:, :, None, None] + rows_dev * u[None, None, None, :, None, None]
    re, im = parts((row * u[None, None, :, None, None, None] % grid_rows) / grid_rows, 1.0)
    width = step_rows * bands
    mix = np.zeros((rows_n, CHUNKS, rows_n, 2, step_rows, bands, 2, step_rows, rows_n, bands), np.float32)
    for i in range(step_rows):
        for t in range(bands):
            mix[:, :, :, 0, i, t, 0, i, :, t] = re[:, :, :, :, i, t]
            mix[:, :, :, 0, i, t, 1, i, :, t] = -im[:, :, :, :, i, t]
            mix[:, :, :, 1, i, t, 0, i, :, t] = im[:, :, :, :, i, t]
            mix[:, :, :, 1, i, t, 1, i, :, t] = re[:, :, :, :, i, t]
    mix = mix.reshape(rows_n, CHUNKS, rows_n * 2 * width, 2 * rows_n * width)
    w = np.arange(rows_dev)
    order = b.transpose(1, 0, 2, 3).reshape(CHUNKS, rows_n, 1, width)
    re, im = parts(
        (w[:, None, None, None, None] * order % rows_dev) / rows_dev, 1.0 / math.sqrt(grid_rows)
    )
    final = np.stack(
        [np.concatenate([re, -im], 3), np.concatenate([im, re], 3)], 0
    ).reshape(2 * rows_dev, 2 * rows_dev)
    lanes = TABLE_LANES
    mix = np.pad(mix.reshape(-1, mix.shape[-1]), ((0, 0), (0, lanes - mix.shape[-1])))
    blocks = [row_table[:, at : at + lanes] for at in range(0, row_table.shape[1], lanes)]
    tables = np.concatenate(blocks + [mix], 0)
    return jnp.asarray(tables.astype(bf16)), jnp.asarray(final.astype(bf16))


def exchange_kernel(
    rows_n, cols_n, tile_side, bands, per_row,
    x_ref, dest_hbm, place_hbm, tables_hbm,
    out_ref,
    owned, labels, arrived, dense, outgoing, table, mix,
    label_send, label_recv, a_send, a_recv, g_send, g_recv, e_send, e_recv, local_sem, table_sem,
):
    me_row, me_col = lax.axis_index("rows"), lax.axis_index("cols")
    tiles = x_ref.shape[0]
    chunk = arrived.shape[3]
    band = chunk * CHUNKS
    cols_dev = per_row * tile_side
    row_peers = [lax.rem(me_row + d, rows_n) for d in range(rows_n)]
    row_sources = [lax.rem(me_row + rows_n - d, rows_n) for d in range(rows_n)]
    col_peers = [lax.rem(me_col + d, cols_n) for d in range(cols_n)]

    barrier = pltpu.get_barrier_semaphore()
    for d in range(1, rows_n):
        pl.semaphore_signal(barrier, inc=1, device_id=(row_peers[d], me_col), device_id_type=MESH)
    for d in range(1, cols_n):
        pl.semaphore_signal(barrier, inc=1, device_id=(me_row, col_peers[d]), device_id_type=MESH)

    owned_copies = [
        pltpu.make_async_copy(dest_hbm, owned.at[0], local_sem.at[2 * CHUNKS + 2]),
        pltpu.make_async_copy(place_hbm, owned.at[1], local_sem.at[2 * CHUNKS + 3]),
    ]
    table_rows, lanes = table.shape[0], TABLE_LANES
    table_copies = [
        pltpu.make_async_copy(
            tables_hbm.at[pl.ds(j * table_rows, table_rows), :],
            table.at[:, pl.ds(j * lanes, lanes)],
            table_sem.at[j],
        )
        for j in range(table.shape[1] // lanes)
    ]
    mix_start = table_rows * len(table_copies) + me_row * mix.shape[0]
    mix_copy = pltpu.make_async_copy(
        tables_hbm.at[pl.ds(pl.multiple_of(mix_start, 16), mix.shape[0]), pl.ds(0, mix.shape[1])],
        mix,
        local_sem.at[CHUNKS],
    )
    for copy in owned_copies + table_copies + [mix_copy]:
        copy.start()
    for copy in owned_copies:
        copy.wait()
    slab, place = owned[0], owned[1]
    code = (place % per_row) * (rows_n * bands) + slab * bands + place // per_row
    labels[0] = jnp.broadcast_to(
        jnp.concatenate([code, jnp.zeros((1, 128 - tiles), jnp.int32)], 1)
        if tiles < 128
        else code,
        labels.shape[1:],
    )
    pl.semaphore_wait(barrier, rows_n + cols_n - 2)

    def band_copy(h, d):
        start = pl.multiple_of(row_peers[d] * band + h * chunk, 128)
        return pltpu.make_async_remote_copy(
            src_ref=x_ref.at[:, pl.ds(start, chunk)],
            dst_ref=arrived.at[h, d],
            send_sem=a_send.at[h, d],
            recv_sem=a_recv.at[h, d],
            device_id=(row_peers[d], me_col),
            device_id_type=MESH,
        )

    label_copies = [
        pltpu.make_async_remote_copy(
            src_ref=labels.at[0],
            dst_ref=labels.at[d],
            send_sem=label_send.at[d],
            recv_sem=label_recv.at[d],
            device_id=(row_peers[d], me_col),
            device_id_type=MESH,
        )
        for d in range(1, rows_n)
    ]
    band_copies = [[band_copy(h, d) for d in range(1, rows_n)] for h in range(CHUNKS)]
    for copy in label_copies + [copy for group in band_copies for copy in group]:
        copy.start()
    own_copies = []
    for h in range(CHUNKS):
        start = pl.multiple_of(me_row * band + h * chunk, 128)
        own_copies.append(
            pltpu.make_async_copy(
                x_ref.at[:, pl.ds(start, chunk)], arrived.at[h, 0], local_sem.at[h]
            )
        )
    for copy in own_copies:
        copy.start()

    for copy in label_copies:
        copy.wait_recv()
    codes = jnp.concatenate([labels[d, 0:1, 0:tiles] for d in range(rows_n)], 1)
    cells = per_row * rows_n * bands
    hot = jnp.where(
        lax.broadcasted_iota(jnp.int32, (cells, rows_n * tiles), 0) == codes, 1.0, 0.0
    ).astype(jnp.bfloat16)
    low_lanes = lax.broadcasted_iota(jnp.int32, (rows_n * bands, 128), 1) < tile_side

    for copy in table_copies + [mix_copy]:
        copy.wait()
    terms = table[2 * cols_dev :, :].astype(jnp.float32)
    row = lax.broadcasted_iota(jnp.int32, terms.shape, 0)
    twiddle_pair = jnp.sum(jnp.where(row // 2 == me_col, terms, 0.0), axis=0, keepdims=True)
    mix_rows = mix.shape[0] // CHUNKS
    cosine, sine = twiddle_pair[:, :cols_dev], twiddle_pair[:, cols_dev:]

    gathers = []

    def density_stage(h):
        own_copies[h].wait()
        for copy in band_copies[h]:
            copy.wait_recv()
        summed = jnp.dot(
            hot,
            arrived[h].reshape(rows_n * tiles, chunk),
            preferred_element_type=jnp.float32,
        )
        height = rows_n * bands
        for pair in range(chunk // 128):
            lanes = slice(128 * pair, 128 * pair + 128)
            for q in range(per_row // 2):
                left = summed[2 * q * height : (2 * q + 1) * height, lanes]
                right = summed[(2 * q + 1) * height : (2 * q + 2) * height, lanes]
                upper = jnp.where(low_lanes, left, pltpu.roll(right, tile_side, 1))
                lower = jnp.where(low_lanes, pltpu.roll(left, tile_side, 1), right)
                out_lanes = slice(128 * q, 128 * q + 128)
                first = 2 * pair * height
                dense[h, 0, first : first + height, out_lanes] = upper.astype(jnp.bfloat16)
                dense[h, 0, first + height : first + 2 * height, out_lanes] = lower.astype(
                    jnp.bfloat16
                )
        group = [
            pltpu.make_async_remote_copy(
                src_ref=dense.at[h, 0],
                dst_ref=dense.at[h, d],
                send_sem=g_send.at[h, d],
                recv_sem=g_recv.at[h, d],
                device_id=(me_row, col_peers[d]),
                device_id_type=MESH,
            )
            for d in range(1, cols_n)
        ]
        for copy in group:
            copy.start()
        gathers.append(group)

    sends = []

    def section_stage(h):
        for copy in gathers[h]:
            copy.wait_recv()
        sum_real = sum_imag = None
        for d in range(cols_n):
            turn = lax.rem(lax.rem(me_col + cols_n - d, cols_n) * me_col, cols_n)
            cos_turn = jnp.where(turn == 0, 1.0, jnp.where(turn == 2, -1.0, 0.0))
            sin_turn = jnp.where(turn == 1, 1.0, jnp.where(turn == 3, -1.0, 0.0))
            value = dense[h, d].astype(jnp.float32)
            real, imag = value * cos_turn, value * (-sin_turn)
            sum_real = real if d == 0 else sum_real + real
            sum_imag = imag if d == 0 else sum_imag + imag
        section_one = jnp.concatenate(
            [sum_real * cosine + sum_imag * sine, sum_imag * cosine - sum_real * sine], 1
        ).astype(jnp.bfloat16)
        spectrum = jnp.dot(section_one, table[0 : 2 * cols_dev, :], preferred_element_type=jnp.float32)
        spectrum = spectrum.astype(jnp.bfloat16)
        stacked = jnp.concatenate([spectrum[:, :cols_dev], spectrum[:, cols_dev:]], 0)
        section_two = jnp.dot(
            mix[h * mix_rows : (h + 1) * mix_rows, :], stacked, preferred_element_type=jnp.float32
        )
        outgoing[h] = section_two.astype(jnp.bfloat16).reshape(outgoing.shape[1:])
        group = [
            pltpu.make_async_remote_copy(
                src_ref=outgoing.at[h, row_peers[d]],
                dst_ref=out_ref.at[h, me_row],
                send_sem=e_send.at[h, d],
                recv_sem=e_recv.at[h, d],
                device_id=(row_peers[d], me_col),
                device_id_type=MESH,
            )
            for d in range(1, rows_n)
        ]
        for copy in group:
            copy.start()
        own = pltpu.make_async_copy(
            outgoing.at[h, me_row], out_ref.at[h, me_row], local_sem.at[CHUNKS + 2 + h]
        )
        own.start()
        sends.append((group, own))

    for h in range(CHUNKS):
        density_stage(h)
        if h > 0:
            section_stage(h - 1)
    section_stage(CHUNKS - 1)

    for copy in label_copies:
        copy.wait_send()
    for h in range(CHUNKS):
        for copy in band_copies[h] + gathers[h]:
            copy.wait_send()
    for h in range(CHUNKS):
        group, own = sends[h]
        own.wait()
        for d in range(1, rows_n):
            pltpu.make_async_remote_copy(
                src_ref=outgoing.at[h, row_peers[d]],
                dst_ref=out_ref.at[h, row_sources[d]],
                send_sem=e_send.at[h, d],
                recv_sem=e_recv.at[h, d],
                device_id=(row_peers[d], me_col),
                device_id_type=MESH,
            ).wait()


def final_kernel(final_ref, section_ref, psf_ref, out_ref):
    rows_dev = psf_ref.shape[0]
    result = jnp.dot(final_ref[...], section_ref[...], preferred_element_type=jnp.float32)
    psf = psf_ref[...].astype(jnp.float32)
    out_ref[:, 0, :] = result[:rows_dev] * psf
    out_ref[:, 1, :] = result[rows_dev:] * psf


def on_device_kernels(tile_density, tile_dest, tile_place, psf_spectrum):
    tile_count, tile_side, _ = tile_density.shape
    rows_dev, cols_dev = psf_spectrum.shape
    rows_n = lax.axis_size("rows")
    cols_n = lax.axis_size("cols")
    bands, per_row = rows_dev // tile_side, cols_dev // tile_side
    step_rows = tile_side // rows_n // CHUNKS
    chunk = step_rows * tile_side
    tables, final = constants(rows_n, cols_n, tile_side, rows_dev, cols_dev)
    bf16 = jnp.bfloat16
    vmem = pl.BlockSpec(memory_space=pltpu.VMEM)
    anywhere = pl.BlockSpec(memory_space=pl.ANY)
    width = 2 * step_rows * bands
    mix_side = width * rows_n
    dma = pltpu.SemaphoreType.DMA
    section = pl.pallas_call(
        functools.partial(exchange_kernel, rows_n, cols_n, tile_side, bands, per_row),
        out_shape=jax.ShapeDtypeStruct((CHUNKS, rows_n, width, cols_dev), bf16),
        in_specs=[anywhere] * 4,
        out_specs=vmem,
        scratch_shapes=[
            pltpu.VMEM((2, 1, tile_count), jnp.int32),
            pltpu.VMEM((rows_n, 8, 128), jnp.int32),
            pltpu.VMEM((CHUNKS, rows_n, tile_count, chunk), bf16),
            pltpu.VMEM((CHUNKS, cols_n, step_rows * rows_n * bands, cols_dev), bf16),
            pltpu.VMEM((CHUNKS, rows_n, width, cols_dev), bf16),
            pltpu.VMEM((2 * cols_dev + 16, 2 * cols_dev), bf16),
            pltpu.VMEM((CHUNKS * mix_side, mix_side), bf16),
            dma((rows_n,)),
            dma((rows_n,)),
            dma((CHUNKS, rows_n)),
            dma((CHUNKS, rows_n)),
            dma((CHUNKS, cols_n)),
            dma((CHUNKS, cols_n)),
            dma((CHUNKS, rows_n)),
            dma((CHUNKS, rows_n)),
            dma((2 * CHUNKS + 4,)),
            dma((2 * cols_dev // TABLE_LANES,)),
        ],
        compiler_params=pltpu.CompilerParams(
            collective_id=0, has_side_effects=True, vmem_limit_bytes=56 << 20
        ),
    )(
        tile_density.reshape(tile_count, tile_side * tile_side),
        tile_dest.reshape(1, tile_count),
        tile_place.reshape(1, tile_count),
        tables,
    )
    return pl.pallas_call(
        final_kernel,
        out_shape=jax.ShapeDtypeStruct((rows_dev, 2, cols_dev), jnp.float32),
        in_specs=[vmem, vmem, vmem],
        out_specs=vmem,
        compiler_params=pltpu.CompilerParams(vmem_limit_bytes=32 << 20),
    )(final, section.reshape(2 * rows_dev, cols_dev), psf_spectrum)


def solution(mesh):
    in_specs = (
        P(("rows", "cols"), None, None),
        P(("rows", "cols"), None),
        P(("rows", "cols")),
        P("rows", "cols"),
    )
    out_specs = P("rows", None, "cols")

    def local(tile_density, tile_dest, tile_place, psf_spectrum):
        fast = fits(
            lax.axis_size("rows"),
            lax.axis_size("cols"),
            *tile_density.shape[:2],
            *psf_spectrum.shape,
        )
        run = on_device_kernels if fast else on_device
        return run(tile_density, tile_dest, tile_place, psf_spectrum)

    return jax.shard_map(
        local, mesh=mesh, in_specs=in_specs, out_specs=out_specs, check_vma=False
    )
```

```python
import functools
import math

import jax
import jax.numpy as jnp
import numpy as np
from jax import lax
from jax.experimental import pallas as pl
from jax.experimental.pallas import tpu as pltpu
from jax.sharding import PartitionSpec as P


def make_table(length, factor):
    positions = jnp.arange(length, dtype=jnp.int32)
    angles = (
        2.0
        * math.pi
        / length
        * (positions[:, None] * positions[None, :] % length).astype(jnp.float32)
    )
    cosine = jnp.cos(angles) * factor
    sine_part = jnp.sin(angles) * factor
    upper_rows = jnp.stack([cosine, -sine_part], 1)
    bottom = jnp.stack([sine_part, cosine], 1)
    return jnp.stack([upper_rows, bottom], 0).astype(jnp.bfloat16)


def twiddle(real_part, imag_part, position, frequency, period):
    angles = 2.0 * math.pi / period * (position * frequency % period).astype(jnp.float32)
    cosine = jnp.cos(angles)
    sine_part = jnp.sin(angles)
    return (real_part * cosine + imag_part * sine_part, imag_part * cosine - real_part * sine_part)


def on_device(tile_density, tile_dest, tile_place, psf_spectrum):
    tile_count, tile_side, _ = tile_density.shape
    rows_dev, cols_dev = psf_spectrum.shape
    rows_n = lax.axis_size("rows")
    cols_n = lax.axis_size("cols")
    capacity = max(2, 2 * tile_count // rows_n)
    slot_total = rows_n * capacity
    target = tile_dest[:, 0]
    matches = (target[:, None] == jnp.arange(rows_n, dtype=jnp.int32)[None, :]).astype(jnp.int32)
    order_within = jnp.sum((jnp.cumsum(matches, 0) - matches) * matches, 1)
    slot_index = target * capacity + order_within
    chosen = slot_index[:, None] == jnp.arange(slot_total, dtype=jnp.int32)[None, :]
    tiles_flat = tile_density.reshape(tile_count, tile_side * tile_side)
    outgoing = jnp.einsum(
        "ts,tc->sc", chosen.astype(jnp.bfloat16), tiles_flat, preferred_element_type=jnp.float32
    ).astype(jnp.bfloat16)
    labels = jnp.sum(jnp.where(chosen, (tile_place + 1)[:, None], 0), axis=0)
    arrived, arrived_marks = (
        lax.all_to_all(outgoing, "rows", split_axis=0, concat_axis=0, tiled=True),
        lax.all_to_all(labels, "rows", split_axis=0, concat_axis=0, tiled=True),
    )
    per_row = cols_dev // tile_side
    positions_count = rows_dev // tile_side * per_row
    placement_hot = (
        arrived_marks[:, None] - 1 == jnp.arange(positions_count, dtype=jnp.int32)[None, :]
    ).astype(jnp.bfloat16)
    cell_tiles = jnp.einsum(
        "sp,sc->pc", placement_hot, arrived, preferred_element_type=jnp.float32
    ).astype(jnp.bfloat16)
    density_grid = cell_tiles.reshape(
        rows_dev // tile_side, per_row, tile_side, tile_side
    ).transpose(0, 2, 1, 3)
    density_grid = density_grid.reshape(rows_dev, cols_dev)
    me_col = lax.axis_index("cols")
    highest = lax.Precision.HIGHEST
    slab_cols = cols_dev * cols_n
    part_cols = cols_dev // cols_n
    pieces = lax.all_to_all(density_grid[None], "cols", split_axis=2, concat_axis=0, tiled=True)
    frequency = jnp.arange(cols_n, dtype=jnp.int32)
    angles = (
        2.0
        * math.pi
        / cols_n
        * (frequency[:, None] * frequency[None, :] % cols_n).astype(jnp.float32)
    )
    values = pieces.astype(jnp.float32)
    sum_real = jnp.einsum("ejt,ek->kjt", values, jnp.cos(angles), precision=highest)
    sum_imag = -jnp.einsum("ejt,ek->kjt", values, jnp.sin(angles), precision=highest)
    columns = (me_col * part_cols + jnp.arange(part_cols, dtype=jnp.int32))[None, None, :]
    real_part, imag_part = twiddle(sum_real, sum_imag, columns, frequency[:, None, None], slab_cols)
    packed = jnp.stack([real_part, imag_part], 2).astype(jnp.bfloat16)
    returned = lax.all_to_all(packed, "cols", split_axis=0, concat_axis=3, tiled=True)
    section_one = returned.reshape(rows_dev, 2 * cols_dev)
    row_table = make_table(cols_dev, 1.0 / math.sqrt(slab_cols)).reshape(2 * cols_dev, 2 * cols_dev)
    rows_spectrum = jnp.dot(section_one, row_table, preferred_element_type=jnp.float32).astype(
        jnp.bfloat16
    )
    rows_spectrum = rows_spectrum.reshape(rows_dev, 2, cols_dev)
    me_row = lax.axis_index("rows")
    group_rows = rows_dev // rows_n
    grid_rows = rows_dev * rows_n
    col_table = make_table(rows_n, 1.0).transpose(3, 2, 1, 0)
    column_block = lax.all_to_all(rows_spectrum, "rows", split_axis=0, concat_axis=0, tiled=True)
    item_width = column_block.shape[2]
    values = column_block.reshape(rows_n, group_rows, 2, item_width)
    combined = jnp.einsum("kqap,atpc->ktqc", col_table, values, preferred_element_type=jnp.float32)
    row_index = (me_row * group_rows + jnp.arange(group_rows, dtype=jnp.int32))[None, :, None]
    row_freq = jnp.arange(rows_n, dtype=jnp.int32)[:, None, None]
    real_two, imag_two = twiddle(
        combined[:, :, 0], combined[:, :, 1], row_index, row_freq, grid_rows
    )
    section_two = lax.all_to_all(
        jnp.stack([real_two, imag_two], 2).astype(jnp.bfloat16).reshape(rows_dev, 2, item_width),
        "rows",
        split_axis=0,
        concat_axis=0,
        tiled=True,
    )
    final_table = (
        make_table(rows_dev, 1.0 / math.sqrt(grid_rows))
        .transpose(3, 2, 1, 0)
        .reshape(2 * rows_dev, 2 * rows_dev)
    )
    result_spec = jnp.dot(
        final_table, section_two.reshape(2 * rows_dev, cols_dev), preferred_element_type=jnp.float32
    )
    result_spec = result_spec.reshape(rows_dev, 2, cols_dev)
    return result_spec * psf_spectrum.astype(jnp.float32)[:, None, :]


CHUNKS = 4
TABLE_LANES = 256
MESH = pl.DeviceIdType.MESH


def fits(rows_n, cols_n, tile_count, tile_side, rows_dev, cols_dev):
    return (
        cols_n == 4
        and rows_n > 1
        and tile_side * 2 == 128
        and tile_side % (rows_n * 2 * CHUNKS) == 0
        and tile_count % 16 == 0
        and tile_count <= 128
        and cols_dev % 128 == 0
        and rows_dev % tile_side == 0
        and 2 * (tile_side // rows_n // CHUNKS) * (rows_dev // tile_side) % 16 == 0
        and 2 * tile_side // CHUNKS * (rows_dev // tile_side) <= TABLE_LANES
        and 2 * cols_dev % TABLE_LANES == 0
        and rows_n * rows_dev * cols_dev * 2 <= 1 << 22
    )


def constants(rows_n, cols_n, tile_side, rows_dev, cols_dev):
    slab_cols, grid_rows = cols_dev * cols_n, rows_dev * rows_n
    bands = rows_dev // tile_side
    band_rows = tile_side // rows_n
    step_rows = band_rows // CHUNKS

    def parts(phase, factor):
        angles = 2.0 * np.pi * phase
        return np.cos(angles) * factor, -np.sin(angles) * factor

    f = np.arange(cols_dev)
    re, im = parts((f[:, None] * f[None, :] % cols_dev) / cols_dev, 1.0 / math.sqrt(slab_cols))
    row_table = np.block([[re, im], [-im, re]])
    bf16 = jnp.bfloat16
    k = np.arange(cols_n)
    re, im = parts((f[None, :] * k[:, None] % slab_cols) / slab_cols, 1.0)
    pair = np.concatenate([re, -im], 1)
    upper = pair.astype(bf16).astype(np.float64)
    extra = np.zeros((16, 2 * cols_dev))
    extra[: 2 * cols_n] = np.stack([upper, pair - upper], 1).reshape(2 * cols_n, -1)
    row_table = np.concatenate([row_table, extra], 0)
    b = (
        tile_side * np.arange(bands)[None, None, None, :]
        + band_rows * np.arange(rows_n)[:, None, None, None]
        + step_rows * np.arange(CHUNKS)[None, :, None, None]
        + np.arange(step_rows)[None, None, :, None]
    )
    u = np.arange(rows_n)
    row = b[:, :, None, None] + rows_dev * u[None, None, None, :, None, None]
    re, im = parts((row * u[None, None, :, None, None, None] % grid_rows) / grid_rows, 1.0)
    width = step_rows * bands
    mix = np.zeros((rows_n, CHUNKS, rows_n, 2, step_rows, bands, 2, step_rows, rows_n, bands), np.float32)
    for i in range(step_rows):
        for t in range(bands):
            mix[:, :, :, 0, i, t, 0, i, :, t] = re[:, :, :, :, i, t]
            mix[:, :, :, 0, i, t, 1, i, :, t] = -im[:, :, :, :, i, t]
            mix[:, :, :, 1, i, t, 0, i, :, t] = im[:, :, :, :, i, t]
            mix[:, :, :, 1, i, t, 1, i, :, t] = re[:, :, :, :, i, t]
    mix = mix.reshape(rows_n, CHUNKS, rows_n * 2 * width, 2 * rows_n * width)
    w = np.arange(rows_dev)
    order = b.transpose(1, 0, 2, 3).reshape(CHUNKS, rows_n, 1, width)
    re, im = parts(
        (w[:, None, None, None, None] * order % rows_dev) / rows_dev, 1.0 / math.sqrt(grid_rows)
    )
    final = np.stack(
        [np.concatenate([re, -im], 3), np.concatenate([im, re], 3)], 0
    ).reshape(2 * rows_dev, 2 * rows_dev)
    lanes = TABLE_LANES
    mix = np.pad(mix.reshape(-1, mix.shape[-1]), ((0, 0), (0, lanes - mix.shape[-1])))
    blocks = [row_table[:, at : at + lanes] for at in range(0, row_table.shape[1], lanes)]
    tables = np.concatenate(blocks + [mix], 0)
    return jnp.asarray(tables.astype(bf16)), jnp.asarray(final.astype(bf16))


def exchange_kernel(
    rows_n, cols_n, tile_side, bands, per_row,
    tiles_hbm, dest_hbm, place_hbm, tables_hbm,
    out_ref,
    owned, raw, wide, banded, labels, arrived, dense, outgoing, table, mix,
    label_send, label_recv, a_send, a_recv, g_send, g_recv, e_send, e_recv, local_sem, table_sem,
):
    me_row, me_col = lax.axis_index("rows"), lax.axis_index("cols")
    tiles = tiles_hbm.shape[0]
    chunk = arrived.shape[3]
    cols_dev = per_row * tile_side
    row_peers = [lax.rem(me_row + d, rows_n) for d in range(rows_n)]
    row_sources = [lax.rem(me_row + rows_n - d, rows_n) for d in range(rows_n)]
    sibling = me_col + 1 - 2 * lax.rem(me_col, 2)
    col_blocks = [me_col, sibling, lax.rem(me_col + 2, cols_n), lax.rem(sibling + 2, cols_n)]

    barrier = pltpu.get_barrier_semaphore()
    for d in range(1, rows_n):
        pl.semaphore_signal(barrier, inc=1, device_id=(row_peers[d], me_col), device_id_type=MESH)
    for d in range(1, 3):
        pl.semaphore_signal(barrier, inc=1, device_id=(me_row, col_blocks[d]), device_id_type=MESH)

    raw_copy = pltpu.make_async_copy(tiles_hbm, raw, local_sem.at[CHUNKS + 1])
    raw_copy.start()
    owned_copies = [
        pltpu.make_async_copy(dest_hbm, owned.at[0], local_sem.at[2 * CHUNKS + 2]),
        pltpu.make_async_copy(place_hbm, owned.at[1], local_sem.at[2 * CHUNKS + 3]),
    ]
    table_rows, lanes = table.shape[0], TABLE_LANES
    table_copies = [
        pltpu.make_async_copy(
            tables_hbm.at[pl.ds(j * table_rows, table_rows), :],
            table.at[:, pl.ds(j * lanes, lanes)],
            table_sem.at[j],
        )
        for j in range(table.shape[1] // lanes)
    ]
    mix_start = table_rows * len(table_copies) + me_row * mix.shape[0]
    mix_copy = pltpu.make_async_copy(
        tables_hbm.at[pl.ds(pl.multiple_of(mix_start, 16), mix.shape[0]), pl.ds(0, mix.shape[1])],
        mix,
        local_sem.at[CHUNKS],
    )
    for copy in owned_copies + table_copies + [mix_copy]:
        copy.start()
    for copy in owned_copies:
        copy.wait()
    slab, place = owned[0], owned[1]
    code = (place % per_row) * (rows_n * bands) + slab * bands + place // per_row
    labels[0] = jnp.broadcast_to(
        jnp.concatenate([code, jnp.zeros((1, 128 - tiles), jnp.int32)], 1)
        if tiles < 128
        else code,
        labels.shape[1:],
    )
    low_lanes = lax.broadcasted_iota(jnp.int32, (max(tiles, rows_n * bands), 128), 1) < tile_side
    raw_copy.wait()
    wide[:, 0:tile_side] = raw[...].reshape(tiles * tile_side, tile_side).astype(jnp.float32)
    own_copies = [
        pltpu.make_async_copy(banded.at[h, me_row], arrived.at[h, 0], local_sem.at[h])
        for h in range(CHUNKS)
    ]

    def band_stage(h):
        for owner in range(rows_n):
            for pair in range(chunk // 128):
                row = (owner * CHUNKS + h) * (chunk // tile_side) + 2 * pair
                first = wide[pl.ds(row, tiles, stride=tile_side), :]
                second = wide[pl.ds(row + 1, tiles, stride=tile_side), :]
                both = jnp.where(low_lanes[:tiles], first, pltpu.roll(second, tile_side, 1))
                banded[h, owner, :, 128 * pair : 128 * pair + 128] = both.astype(jnp.bfloat16)
        own_copies[h].start()

    band_stage(0)
    pl.semaphore_wait(barrier, rows_n + 1)

    def band_copy(h, d):
        return pltpu.make_async_remote_copy(
            src_ref=banded.at[h, row_peers[d]],
            dst_ref=arrived.at[h, d],
            send_sem=a_send.at[h, d],
            recv_sem=a_recv.at[h, d],
            device_id=(row_peers[d], me_col),
            device_id_type=MESH,
        )

    label_copies = [
        pltpu.make_async_remote_copy(
            src_ref=labels.at[0],
            dst_ref=labels.at[d],
            send_sem=label_send.at[d],
            recv_sem=label_recv.at[d],
            device_id=(row_peers[d], me_col),
            device_id_type=MESH,
        )
        for d in range(1, rows_n)
    ]
    band_copies = [[band_copy(h, d) for d in range(1, rows_n)] for h in range(CHUNKS)]
    for copy in label_copies:
        copy.start()
    def band_start(h):
        for copy in band_copies[h]:
            copy.start()

    band_start(0)
    for h in range(1, CHUNKS):
        band_stage(h)
    band_start(1)

    for copy in label_copies:
        copy.wait_recv()
    codes = jnp.concatenate([labels[d, 0:1, 0:tiles] for d in range(rows_n)], 1)
    cells = per_row * rows_n * bands
    hot = jnp.where(
        lax.broadcasted_iota(jnp.int32, (cells, rows_n * tiles), 0) == codes, 1.0, 0.0
    ).astype(jnp.bfloat16)

    for copy in table_copies + [mix_copy]:
        copy.wait()
    terms = table[2 * cols_dev :, :].astype(jnp.float32)
    row = lax.broadcasted_iota(jnp.int32, terms.shape, 0)
    twiddle_pair = jnp.sum(jnp.where(row // 2 == me_col, terms, 0.0), axis=0, keepdims=True)
    mix_rows = mix.shape[0] // CHUNKS
    cosine, sine = twiddle_pair[:, :cols_dev], twiddle_pair[:, cols_dev:]

    gathers = []

    def block_copy(h, source, peer, slot):
        return pltpu.make_async_remote_copy(
            src_ref=dense.at[h, source],
            dst_ref=dense.at[h, slot],
            send_sem=g_send.at[h, slot],
            recv_sem=g_recv.at[h, slot],
            device_id=(me_row, col_blocks[peer]),
            device_id_type=MESH,
        )

    def density_stage(h):
        own_copies[h].wait()
        for copy in band_copies[h]:
            copy.wait_recv()
        if h + 2 < CHUNKS:
            band_start(h + 2)
        summed = jnp.dot(
            hot,
            arrived[h].reshape(rows_n * tiles, chunk),
            preferred_element_type=jnp.float32,
        )
        height = rows_n * bands
        for pair in range(chunk // 128):
            lanes = slice(128 * pair, 128 * pair + 128)
            for q in range(per_row // 2):
                left = summed[2 * q * height : (2 * q + 1) * height, lanes]
                right = summed[(2 * q + 1) * height : (2 * q + 2) * height, lanes]
                upper = jnp.where(low_lanes[:height], left, pltpu.roll(right, tile_side, 1))
                lower = jnp.where(low_lanes[:height], pltpu.roll(left, tile_side, 1), right)
                out_lanes = slice(128 * q, 128 * q + 128)
                first = 2 * pair * height
                dense[h, 0, first : first + height, out_lanes] = upper.astype(jnp.bfloat16)
                dense[h, 0, first + height : first + 2 * height, out_lanes] = lower.astype(
                    jnp.bfloat16
                )
        group = [block_copy(h, 0, 2, 2), block_copy(h, 0, 1, 1)]
        for copy in group:
            copy.start()
        gathers.append(group)

    def forward_stage(h):
        gathers[h][0].wait_recv()
        copy = block_copy(h, 2, 1, 3)
        copy.start()
        gathers[h].append(copy)

    sends = []

    def section_stage(h):
        for copy in gathers[h][1:]:
            copy.wait_recv()
        sum_real = sum_imag = None
        for d in range(cols_n):
            turn = lax.rem(col_blocks[d] * me_col, cols_n)
            cos_turn = jnp.where(turn == 0, 1.0, jnp.where(turn == 2, -1.0, 0.0))
            sin_turn = jnp.where(turn == 1, 1.0, jnp.where(turn == 3, -1.0, 0.0))
            value = dense[h, d].astype(jnp.float32)
            real, imag = value * cos_turn, value * (-sin_turn)
            sum_real = real if d == 0 else sum_real + real
            sum_imag = imag if d == 0 else sum_imag + imag
        section_one = jnp.concatenate(
            [sum_real * cosine + sum_imag * sine, sum_imag * cosine - sum_real * sine], 1
        ).astype(jnp.bfloat16)
        spectrum = jnp.dot(section_one, table[0 : 2 * cols_dev, :], preferred_element_type=jnp.float32)
        spectrum = spectrum.astype(jnp.bfloat16)
        stacked = jnp.concatenate([spectrum[:, :cols_dev], spectrum[:, cols_dev:]], 0)
        section_two = jnp.dot(
            mix[h * mix_rows : (h + 1) * mix_rows, :], stacked, preferred_element_type=jnp.float32
        )
        outgoing[h] = section_two.astype(jnp.bfloat16).reshape(outgoing.shape[1:])
        group = [
            pltpu.make_async_remote_copy(
                src_ref=outgoing.at[h, row_peers[d]],
                dst_ref=out_ref.at[h, me_row],
                send_sem=e_send.at[h, d],
                recv_sem=e_recv.at[h, d],
                device_id=(row_peers[d], me_col),
                device_id_type=MESH,
            )
            for d in range(1, rows_n)
        ]
        for copy in group:
            copy.start()
        own = pltpu.make_async_copy(
            outgoing.at[h, me_row], out_ref.at[h, me_row], local_sem.at[CHUNKS + 2 + h]
        )
        own.start()
        sends.append((group, own))

    for h in range(CHUNKS):
        density_stage(h)
        if h > 0:
            forward_stage(h - 1)
        if h > 1:
            section_stage(h - 2)
    forward_stage(CHUNKS - 1)
    for h in range(CHUNKS - 2, CHUNKS):
        section_stage(h)

    for copy in label_copies:
        copy.wait_send()
    for h in range(CHUNKS):
        for copy in band_copies[h] + gathers[h]:
            copy.wait_send()
    for h in range(CHUNKS):
        group, own = sends[h]
        own.wait()
        for d in range(1, rows_n):
            pltpu.make_async_remote_copy(
                src_ref=outgoing.at[h, row_peers[d]],
                dst_ref=out_ref.at[h, row_sources[d]],
                send_sem=e_send.at[h, d],
                recv_sem=e_recv.at[h, d],
                device_id=(row_peers[d], me_col),
                device_id_type=MESH,
            ).wait()


def final_kernel(final_ref, section_ref, psf_ref, out_ref):
    rows_dev = psf_ref.shape[0]
    result = jnp.dot(final_ref[...], section_ref[...], preferred_element_type=jnp.float32)
    psf = psf_ref[...].astype(jnp.float32)
    out_ref[:, 0, :] = result[:rows_dev] * psf
    out_ref[:, 1, :] = result[rows_dev:] * psf


def on_device_kernels(tile_density, tile_dest, tile_place, psf_spectrum):
    tile_count, tile_side, _ = tile_density.shape
    rows_dev, cols_dev = psf_spectrum.shape
    rows_n = lax.axis_size("rows")
    cols_n = lax.axis_size("cols")
    bands, per_row = rows_dev // tile_side, cols_dev // tile_side
    step_rows = tile_side // rows_n // CHUNKS
    chunk = step_rows * tile_side
    tables, final = constants(rows_n, cols_n, tile_side, rows_dev, cols_dev)
    bf16 = jnp.bfloat16
    vmem = pl.BlockSpec(memory_space=pltpu.VMEM)
    anywhere = pl.BlockSpec(memory_space=pl.ANY)
    width = 2 * step_rows * bands
    mix_side = width * rows_n
    dma = pltpu.SemaphoreType.DMA
    section = pl.pallas_call(
        functools.partial(exchange_kernel, rows_n, cols_n, tile_side, bands, per_row),
        out_shape=jax.ShapeDtypeStruct((CHUNKS, rows_n, width, cols_dev), bf16),
        in_specs=[anywhere] * 4,
        out_specs=vmem,
        scratch_shapes=[
            pltpu.VMEM((2, 1, tile_count), jnp.int32),
            pltpu.VMEM(tile_density.shape, bf16),
            pltpu.VMEM((tile_count * tile_side, 128), jnp.float32),
            pltpu.VMEM((CHUNKS, rows_n, tile_count, chunk), bf16),
            pltpu.VMEM((rows_n, 8, 128), jnp.int32),
            pltpu.VMEM((CHUNKS, rows_n, tile_count, chunk), bf16),
            pltpu.VMEM((CHUNKS, cols_n, step_rows * rows_n * bands, cols_dev), bf16),
            pltpu.VMEM((CHUNKS, rows_n, width, cols_dev), bf16),
            pltpu.VMEM((2 * cols_dev + 16, 2 * cols_dev), bf16),
            pltpu.VMEM((CHUNKS * mix_side, mix_side), bf16),
            dma((rows_n,)),
            dma((rows_n,)),
            dma((CHUNKS, rows_n)),
            dma((CHUNKS, rows_n)),
            dma((CHUNKS, cols_n)),
            dma((CHUNKS, cols_n)),
            dma((CHUNKS, rows_n)),
            dma((CHUNKS, rows_n)),
            dma((2 * CHUNKS + 4,)),
            dma((2 * cols_dev // TABLE_LANES,)),
        ],
        compiler_params=pltpu.CompilerParams(
            collective_id=0, has_side_effects=True, vmem_limit_bytes=56 << 20
        ),
    )(
        tile_density,
        tile_dest.reshape(1, tile_count),
        tile_place.reshape(1, tile_count),
        tables,
    )
    return pl.pallas_call(
        final_kernel,
        out_shape=jax.ShapeDtypeStruct((rows_dev, 2, cols_dev), jnp.float32),
        in_specs=[vmem, vmem, vmem],
        out_specs=vmem,
        compiler_params=pltpu.CompilerParams(vmem_limit_bytes=32 << 20),
    )(final, section.reshape(2 * rows_dev, cols_dev), psf_spectrum)


def solution(mesh):
    in_specs = (
        P(("rows", "cols"), None, None),
        P(("rows", "cols"), None),
        P(("rows", "cols")),
        P("rows", "cols"),
    )
    out_specs = P("rows", None, "cols")

    def local(tile_density, tile_dest, tile_place, psf_spectrum):
        fast = fits(
            lax.axis_size("rows"),
            lax.axis_size("cols"),
            *tile_density.shape[:2],
            *psf_spectrum.shape,
        )
        run = on_device_kernels if fast else on_device
        return run(tile_density, tile_dest, tile_place, psf_spectrum)

    return jax.shard_map(
        local, mesh=mesh, in_specs=in_specs, out_specs=out_specs, check_vma=False
    )
```

```python
import functools
import math

import jax
import jax.numpy as jnp
import numpy as np
from jax import lax
from jax.experimental import pallas as pl
from jax.experimental.pallas import tpu as pltpu
from jax.sharding import PartitionSpec as P


def make_table(length, factor):
    positions = jnp.arange(length, dtype=jnp.int32)
    angles = (
        2.0
        * math.pi
        / length
        * (positions[:, None] * positions[None, :] % length).astype(jnp.float32)
    )
    cosine = jnp.cos(angles) * factor
    sine_part = jnp.sin(angles) * factor
    upper_rows = jnp.stack([cosine, -sine_part], 1)
    bottom = jnp.stack([sine_part, cosine], 1)
    return jnp.stack([upper_rows, bottom], 0).astype(jnp.bfloat16)


def twiddle(real_part, imag_part, position, frequency, period):
    angles = 2.0 * math.pi / period * (position * frequency % period).astype(jnp.float32)
    cosine = jnp.cos(angles)
    sine_part = jnp.sin(angles)
    return (real_part * cosine + imag_part * sine_part, imag_part * cosine - real_part * sine_part)


def on_device(tile_density, tile_dest, tile_place, psf_spectrum):
    tile_count, tile_side, _ = tile_density.shape
    rows_dev, cols_dev = psf_spectrum.shape
    rows_n = lax.axis_size("rows")
    cols_n = lax.axis_size("cols")
    capacity = max(2, 2 * tile_count // rows_n)
    slot_total = rows_n * capacity
    target = tile_dest[:, 0]
    matches = (target[:, None] == jnp.arange(rows_n, dtype=jnp.int32)[None, :]).astype(jnp.int32)
    order_within = jnp.sum((jnp.cumsum(matches, 0) - matches) * matches, 1)
    slot_index = target * capacity + order_within
    chosen = slot_index[:, None] == jnp.arange(slot_total, dtype=jnp.int32)[None, :]
    tiles_flat = tile_density.reshape(tile_count, tile_side * tile_side)
    outgoing = jnp.einsum(
        "ts,tc->sc", chosen.astype(jnp.bfloat16), tiles_flat, preferred_element_type=jnp.float32
    ).astype(jnp.bfloat16)
    labels = jnp.sum(jnp.where(chosen, (tile_place + 1)[:, None], 0), axis=0)
    arrived, arrived_marks = (
        lax.all_to_all(outgoing, "rows", split_axis=0, concat_axis=0, tiled=True),
        lax.all_to_all(labels, "rows", split_axis=0, concat_axis=0, tiled=True),
    )
    per_row = cols_dev // tile_side
    positions_count = rows_dev // tile_side * per_row
    placement_hot = (
        arrived_marks[:, None] - 1 == jnp.arange(positions_count, dtype=jnp.int32)[None, :]
    ).astype(jnp.bfloat16)
    cell_tiles = jnp.einsum(
        "sp,sc->pc", placement_hot, arrived, preferred_element_type=jnp.float32
    ).astype(jnp.bfloat16)
    density_grid = cell_tiles.reshape(
        rows_dev // tile_side, per_row, tile_side, tile_side
    ).transpose(0, 2, 1, 3)
    density_grid = density_grid.reshape(rows_dev, cols_dev)
    me_col = lax.axis_index("cols")
    highest = lax.Precision.HIGHEST
    slab_cols = cols_dev * cols_n
    part_cols = cols_dev // cols_n
    pieces = lax.all_to_all(density_grid[None], "cols", split_axis=2, concat_axis=0, tiled=True)
    frequency = jnp.arange(cols_n, dtype=jnp.int32)
    angles = (
        2.0
        * math.pi
        / cols_n
        * (frequency[:, None] * frequency[None, :] % cols_n).astype(jnp.float32)
    )
    values = pieces.astype(jnp.float32)
    sum_real = jnp.einsum("ejt,ek->kjt", values, jnp.cos(angles), precision=highest)
    sum_imag = -jnp.einsum("ejt,ek->kjt", values, jnp.sin(angles), precision=highest)
    columns = (me_col * part_cols + jnp.arange(part_cols, dtype=jnp.int32))[None, None, :]
    real_part, imag_part = twiddle(sum_real, sum_imag, columns, frequency[:, None, None], slab_cols)
    packed = jnp.stack([real_part, imag_part], 2).astype(jnp.bfloat16)
    returned = lax.all_to_all(packed, "cols", split_axis=0, concat_axis=3, tiled=True)
    section_one = returned.reshape(rows_dev, 2 * cols_dev)
    row_table = make_table(cols_dev, 1.0 / math.sqrt(slab_cols)).reshape(2 * cols_dev, 2 * cols_dev)
    rows_spectrum = jnp.dot(section_one, row_table, preferred_element_type=jnp.float32).astype(
        jnp.bfloat16
    )
    rows_spectrum = rows_spectrum.reshape(rows_dev, 2, cols_dev)
    me_row = lax.axis_index("rows")
    group_rows = rows_dev // rows_n
    grid_rows = rows_dev * rows_n
    col_table = make_table(rows_n, 1.0).transpose(3, 2, 1, 0)
    column_block = lax.all_to_all(rows_spectrum, "rows", split_axis=0, concat_axis=0, tiled=True)
    item_width = column_block.shape[2]
    values = column_block.reshape(rows_n, group_rows, 2, item_width)
    combined = jnp.einsum("kqap,atpc->ktqc", col_table, values, preferred_element_type=jnp.float32)
    row_index = (me_row * group_rows + jnp.arange(group_rows, dtype=jnp.int32))[None, :, None]
    row_freq = jnp.arange(rows_n, dtype=jnp.int32)[:, None, None]
    real_two, imag_two = twiddle(
        combined[:, :, 0], combined[:, :, 1], row_index, row_freq, grid_rows
    )
    section_two = lax.all_to_all(
        jnp.stack([real_two, imag_two], 2).astype(jnp.bfloat16).reshape(rows_dev, 2, item_width),
        "rows",
        split_axis=0,
        concat_axis=0,
        tiled=True,
    )
    final_table = (
        make_table(rows_dev, 1.0 / math.sqrt(grid_rows))
        .transpose(3, 2, 1, 0)
        .reshape(2 * rows_dev, 2 * rows_dev)
    )
    result_spec = jnp.dot(
        final_table, section_two.reshape(2 * rows_dev, cols_dev), preferred_element_type=jnp.float32
    )
    result_spec = result_spec.reshape(rows_dev, 2, cols_dev)
    return result_spec * psf_spectrum.astype(jnp.float32)[:, None, :]


CHUNKS = 2
TABLE_LANES = 256
MESH = pl.DeviceIdType.MESH


def fits(rows_n, cols_n, tile_count, tile_side, rows_dev, cols_dev):
    return (
        cols_n == 4
        and rows_n > 1
        and tile_side * 2 == 128
        and tile_side % (rows_n * 2 * CHUNKS) == 0
        and tile_count % 16 == 0
        and tile_count <= 128
        and cols_dev % 128 == 0
        and rows_dev % tile_side == 0
        and 2 * (tile_side // rows_n // CHUNKS) * (rows_dev // tile_side) % 16 == 0
        and 2 * tile_side // CHUNKS * (rows_dev // tile_side) <= TABLE_LANES
        and 2 * cols_dev % TABLE_LANES == 0
        and rows_n * rows_dev * cols_dev * 2 <= 1 << 22
    )


def constants(rows_n, cols_n, tile_side, rows_dev, cols_dev):
    slab_cols, grid_rows = cols_dev * cols_n, rows_dev * rows_n
    bands = rows_dev // tile_side
    band_rows = tile_side // rows_n
    step_rows = band_rows // CHUNKS

    def parts(phase, factor):
        angles = 2.0 * np.pi * phase
        return np.cos(angles) * factor, -np.sin(angles) * factor

    f = np.arange(cols_dev)
    re, im = parts((f[:, None] * f[None, :] % cols_dev) / cols_dev, 1.0 / math.sqrt(slab_cols))
    row_table = np.block([[re, im], [-im, re]])
    bf16 = jnp.bfloat16
    k = np.arange(cols_n)
    re, im = parts((f[None, :] * k[:, None] % slab_cols) / slab_cols, 1.0)
    pair = np.concatenate([re, -im], 1)
    upper = pair.astype(bf16).astype(np.float64)
    extra = np.zeros((16, 2 * cols_dev))
    extra[: 2 * cols_n] = np.stack([upper, pair - upper], 1).reshape(2 * cols_n, -1)
    row_table = np.concatenate([row_table, extra], 0)
    b = (
        tile_side * np.arange(bands)[None, None, None, :]
        + band_rows * np.arange(rows_n)[:, None, None, None]
        + step_rows * np.arange(CHUNKS)[None, :, None, None]
        + np.arange(step_rows)[None, None, :, None]
    )
    u = np.arange(rows_n)
    row = b[:, :, None, None] + rows_dev * u[None, None, None, :, None, None]
    re, im = parts((row * u[None, None, :, None, None, None] % grid_rows) / grid_rows, 1.0)
    width = step_rows * bands
    mix = np.zeros((rows_n, CHUNKS, rows_n, 2, step_rows, bands, 2, step_rows, rows_n, bands), np.float32)
    for i in range(step_rows):
        for t in range(bands):
            mix[:, :, :, 0, i, t, 0, i, :, t] = re[:, :, :, :, i, t]
            mix[:, :, :, 0, i, t, 1, i, :, t] = -im[:, :, :, :, i, t]
            mix[:, :, :, 1, i, t, 0, i, :, t] = im[:, :, :, :, i, t]
            mix[:, :, :, 1, i, t, 1, i, :, t] = re[:, :, :, :, i, t]
    mix = mix.reshape(rows_n, CHUNKS, rows_n * 2 * width, 2 * rows_n * width)
    w = np.arange(rows_dev)
    order = b.transpose(1, 0, 2, 3).reshape(CHUNKS, rows_n, 1, width)
    re, im = parts(
        (w[:, None, None, None, None] * order % rows_dev) / rows_dev, 1.0 / math.sqrt(grid_rows)
    )
    final = np.stack(
        [np.concatenate([re, -im], 3), np.concatenate([im, re], 3)], 0
    ).reshape(2 * rows_dev, 2 * rows_dev)
    lanes = TABLE_LANES
    mix = np.pad(mix.reshape(-1, mix.shape[-1]), ((0, 0), (0, lanes - mix.shape[-1])))
    blocks = [row_table[:, at : at + lanes] for at in range(0, row_table.shape[1], lanes)]
    tables = np.concatenate(blocks + [mix], 0)
    return jnp.asarray(tables.astype(bf16)), jnp.asarray(final.astype(bf16))


def exchange_kernel(
    rows_n, cols_n, tile_side, bands, per_row,
    tiles_hbm, dest_hbm, place_hbm, tables_hbm,
    out_ref,
    owned, raw, wide, banded, labels, arrived, dense, outgoing, table, mix,
    label_send, label_recv, a_send, a_recv, g_send, g_recv, e_send, e_recv, local_sem, table_sem,
):
    me_row, me_col = lax.axis_index("rows"), lax.axis_index("cols")
    tiles = tiles_hbm.shape[0]
    chunk = arrived.shape[3]
    cols_dev = per_row * tile_side
    row_peers = [lax.rem(me_row + d, rows_n) for d in range(rows_n)]
    row_sources = [lax.rem(me_row + rows_n - d, rows_n) for d in range(rows_n)]
    sibling = me_col + 1 - 2 * lax.rem(me_col, 2)
    col_blocks = [me_col, sibling, lax.rem(me_col + 2, cols_n), lax.rem(sibling + 2, cols_n)]

    barrier = pltpu.get_barrier_semaphore()
    for d in range(1, rows_n):
        pl.semaphore_signal(barrier, inc=1, device_id=(row_peers[d], me_col), device_id_type=MESH)
    for d in range(1, 3):
        pl.semaphore_signal(barrier, inc=1, device_id=(me_row, col_blocks[d]), device_id_type=MESH)

    raw_copy = pltpu.make_async_copy(tiles_hbm, raw, local_sem.at[CHUNKS + 1])
    raw_copy.start()
    owned_copies = [
        pltpu.make_async_copy(dest_hbm, owned.at[0], local_sem.at[2 * CHUNKS + 2]),
        pltpu.make_async_copy(place_hbm, owned.at[1], local_sem.at[2 * CHUNKS + 3]),
    ]
    table_rows, lanes = table.shape[0], TABLE_LANES
    table_copies = [
        pltpu.make_async_copy(
            tables_hbm.at[pl.ds(j * table_rows, table_rows), :],
            table.at[:, pl.ds(j * lanes, lanes)],
            table_sem.at[j],
        )
        for j in range(table.shape[1] // lanes)
    ]
    mix_start = table_rows * len(table_copies) + me_row * mix.shape[0]
    mix_copy = pltpu.make_async_copy(
        tables_hbm.at[pl.ds(pl.multiple_of(mix_start, 16), mix.shape[0]), pl.ds(0, mix.shape[1])],
        mix,
        local_sem.at[CHUNKS],
    )
    for copy in owned_copies + table_copies + [mix_copy]:
        copy.start()
    for copy in owned_copies:
        copy.wait()
    slab, place = owned[0], owned[1]
    code = (place % per_row) * (rows_n * bands) + slab * bands + place // per_row
    labels[0] = jnp.broadcast_to(
        jnp.concatenate([code, jnp.zeros((1, 128 - tiles), jnp.int32)], 1)
        if tiles < 128
        else code,
        labels.shape[1:],
    )
    low_lanes = lax.broadcasted_iota(jnp.int32, (max(tiles, rows_n * bands), 128), 1) < tile_side
    raw_copy.wait()
    wide[:, 0:tile_side] = raw[...].reshape(tiles * tile_side, tile_side).astype(jnp.float32)
    own_copies = [
        pltpu.make_async_copy(banded.at[h, me_row], arrived.at[h, 0], local_sem.at[h])
        for h in range(CHUNKS)
    ]

    def band_stage(h):
        for owner in range(rows_n):
            for pair in range(chunk // 128):
                row = (owner * CHUNKS + h) * (chunk // tile_side) + 2 * pair
                first = wide[pl.ds(row, tiles, stride=tile_side), :]
                second = wide[pl.ds(row + 1, tiles, stride=tile_side), :]
                both = jnp.where(low_lanes[:tiles], first, pltpu.roll(second, tile_side, 1))
                banded[h, owner, :, 128 * pair : 128 * pair + 128] = both.astype(jnp.bfloat16)
        own_copies[h].start()

    band_stage(0)
    pl.semaphore_wait(barrier, rows_n + 1)

    def band_copy(h, d):
        return pltpu.make_async_remote_copy(
            src_ref=banded.at[h, row_peers[d]],
            dst_ref=arrived.at[h, d],
            send_sem=a_send.at[h, d],
            recv_sem=a_recv.at[h, d],
            device_id=(row_peers[d], me_col),
            device_id_type=MESH,
        )

    label_copies = [
        pltpu.make_async_remote_copy(
            src_ref=labels.at[0],
            dst_ref=labels.at[d],
            send_sem=label_send.at[d],
            recv_sem=label_recv.at[d],
            device_id=(row_peers[d], me_col),
            device_id_type=MESH,
        )
        for d in range(1, rows_n)
    ]
    band_copies = [[band_copy(h, d) for d in range(1, rows_n)] for h in range(CHUNKS)]
    for copy in label_copies:
        copy.start()
    def band_start(h):
        for copy in band_copies[h]:
            copy.start()

    band_start(0)
    for h in range(1, CHUNKS):
        band_stage(h)
    band_start(1)

    for copy in label_copies:
        copy.wait_recv()
    codes = jnp.concatenate([labels[d, 0:1, 0:tiles] for d in range(rows_n)], 1)
    cells = per_row * rows_n * bands
    hot = jnp.where(
        lax.broadcasted_iota(jnp.int32, (cells, rows_n * tiles), 0) == codes, 1.0, 0.0
    ).astype(jnp.bfloat16)

    for copy in table_copies + [mix_copy]:
        copy.wait()
    terms = table[2 * cols_dev :, :].astype(jnp.float32)
    row = lax.broadcasted_iota(jnp.int32, terms.shape, 0)
    twiddle_pair = jnp.sum(jnp.where(row // 2 == me_col, terms, 0.0), axis=0, keepdims=True)
    mix_rows = mix.shape[0] // CHUNKS
    cosine, sine = twiddle_pair[:, :cols_dev], twiddle_pair[:, cols_dev:]

    gathers = []

    def block_copy(h, source, peer, slot):
        return pltpu.make_async_remote_copy(
            src_ref=dense.at[h, source],
            dst_ref=dense.at[h, slot],
            send_sem=g_send.at[h, slot],
            recv_sem=g_recv.at[h, slot],
            device_id=(me_row, col_blocks[peer]),
            device_id_type=MESH,
        )

    def density_stage(h):
        own_copies[h].wait()
        for copy in band_copies[h]:
            copy.wait_recv()
        if h + 2 < CHUNKS:
            band_start(h + 2)
        summed = jnp.dot(
            hot,
            arrived[h].reshape(rows_n * tiles, chunk),
            preferred_element_type=jnp.float32,
        )
        height = rows_n * bands
        for pair in range(chunk // 128):
            lanes = slice(128 * pair, 128 * pair + 128)
            for q in range(per_row // 2):
                left = summed[2 * q * height : (2 * q + 1) * height, lanes]
                right = summed[(2 * q + 1) * height : (2 * q + 2) * height, lanes]
                upper = jnp.where(low_lanes[:height], left, pltpu.roll(right, tile_side, 1))
                lower = jnp.where(low_lanes[:height], pltpu.roll(left, tile_side, 1), right)
                out_lanes = slice(128 * q, 128 * q + 128)
                first = 2 * pair * height
                dense[h, 0, first : first + height, out_lanes] = upper.astype(jnp.bfloat16)
                dense[h, 0, first + height : first + 2 * height, out_lanes] = lower.astype(
                    jnp.bfloat16
                )
        group = [block_copy(h, 0, 2, 2), block_copy(h, 0, 1, 1)]
        for copy in group:
            copy.start()
        gathers.append(group)

    def forward_stage(h):
        gathers[h][0].wait_recv()
        copy = block_copy(h, 2, 1, 3)
        copy.start()
        gathers[h].append(copy)

    sends = []

    def section_stage(h):
        for copy in gathers[h][1:]:
            copy.wait_recv()
        sum_real = sum_imag = None
        for d in range(cols_n):
            turn = lax.rem(col_blocks[d] * me_col, cols_n)
            cos_turn = jnp.where(turn == 0, 1.0, jnp.where(turn == 2, -1.0, 0.0))
            sin_turn = jnp.where(turn == 1, 1.0, jnp.where(turn == 3, -1.0, 0.0))
            value = dense[h, d].astype(jnp.float32)
            real, imag = value * cos_turn, value * (-sin_turn)
            sum_real = real if d == 0 else sum_real + real
            sum_imag = imag if d == 0 else sum_imag + imag
        section_one = jnp.concatenate(
            [sum_real * cosine + sum_imag * sine, sum_imag * cosine - sum_real * sine], 1
        ).astype(jnp.bfloat16)
        spectrum = jnp.dot(section_one, table[0 : 2 * cols_dev, :], preferred_element_type=jnp.float32)
        spectrum = spectrum.astype(jnp.bfloat16)
        stacked = jnp.concatenate([spectrum[:, :cols_dev], spectrum[:, cols_dev:]], 0)
        section_two = jnp.dot(
            mix[h * mix_rows : (h + 1) * mix_rows, :], stacked, preferred_element_type=jnp.float32
        )
        outgoing[h] = section_two.astype(jnp.bfloat16).reshape(outgoing.shape[1:])
        group = [
            pltpu.make_async_remote_copy(
                src_ref=outgoing.at[h, row_peers[d]],
                dst_ref=out_ref.at[h, me_row],
                send_sem=e_send.at[h, d],
                recv_sem=e_recv.at[h, d],
                device_id=(row_peers[d], me_col),
                device_id_type=MESH,
            )
            for d in range(1, rows_n)
        ]
        for copy in group:
            copy.start()
        own = pltpu.make_async_copy(
            outgoing.at[h, me_row], out_ref.at[h, me_row], local_sem.at[CHUNKS + 2 + h]
        )
        own.start()
        sends.append((group, own))

    for h in range(CHUNKS):
        density_stage(h)
        if h > 0:
            forward_stage(h - 1)
        if h > 1:
            section_stage(h - 2)
    forward_stage(CHUNKS - 1)
    for h in range(CHUNKS - 2, CHUNKS):
        section_stage(h)

    for copy in label_copies:
        copy.wait_send()
    for h in range(CHUNKS):
        for copy in band_copies[h] + gathers[h]:
            copy.wait_send()
    for h in range(CHUNKS):
        group, own = sends[h]
        own.wait()
        for d in range(1, rows_n):
            pltpu.make_async_remote_copy(
                src_ref=outgoing.at[h, row_peers[d]],
                dst_ref=out_ref.at[h, row_sources[d]],
                send_sem=e_send.at[h, d],
                recv_sem=e_recv.at[h, d],
                device_id=(row_peers[d], me_col),
                device_id_type=MESH,
            ).wait()


def final_kernel(final_ref, section_hbm, psf_ref, out_ref, section, sems):
    rows_dev = psf_ref.shape[0]
    depth = section.shape[0] // CHUNKS
    copies = []
    for h in range(CHUNKS):
        rows = pl.ds(h * depth, depth)
        copies.append(
            pltpu.make_async_copy(section_hbm.at[rows, :], section.at[rows, :], sems.at[h])
        )
        copies[h].start()
    result = None
    for h in range(CHUNKS):
        copies[h].wait()
        at = slice(h * depth, h * depth + depth)
        term = jnp.dot(final_ref[:, at], section[at, :], preferred_element_type=jnp.float32)
        result = term if h == 0 else result + term
    psf = psf_ref[...].astype(jnp.float32)
    out_ref[:, 0, :] = result[:rows_dev] * psf
    out_ref[:, 1, :] = result[rows_dev:] * psf


def on_device_kernels(tile_density, tile_dest, tile_place, psf_spectrum):
    tile_count, tile_side, _ = tile_density.shape
    rows_dev, cols_dev = psf_spectrum.shape
    rows_n = lax.axis_size("rows")
    cols_n = lax.axis_size("cols")
    bands, per_row = rows_dev // tile_side, cols_dev // tile_side
    step_rows = tile_side // rows_n // CHUNKS
    chunk = step_rows * tile_side
    tables, final = constants(rows_n, cols_n, tile_side, rows_dev, cols_dev)
    bf16 = jnp.bfloat16
    vmem = pl.BlockSpec(memory_space=pltpu.VMEM)
    anywhere = pl.BlockSpec(memory_space=pl.ANY)
    width = 2 * step_rows * bands
    mix_side = width * rows_n
    dma = pltpu.SemaphoreType.DMA
    section = pl.pallas_call(
        functools.partial(exchange_kernel, rows_n, cols_n, tile_side, bands, per_row),
        out_shape=jax.ShapeDtypeStruct((CHUNKS, rows_n, width, cols_dev), bf16),
        in_specs=[anywhere] * 4,
        out_specs=vmem,
        scratch_shapes=[
            pltpu.VMEM((2, 1, tile_count), jnp.int32),
            pltpu.VMEM(tile_density.shape, bf16),
            pltpu.VMEM((tile_count * tile_side, 128), jnp.float32),
            pltpu.VMEM((CHUNKS, rows_n, tile_count, chunk), bf16),
            pltpu.VMEM((rows_n, 8, 128), jnp.int32),
            pltpu.VMEM((CHUNKS, rows_n, tile_count, chunk), bf16),
            pltpu.VMEM((CHUNKS, cols_n, step_rows * rows_n * bands, cols_dev), bf16),
            pltpu.VMEM((CHUNKS, rows_n, width, cols_dev), bf16),
            pltpu.VMEM((2 * cols_dev + 16, 2 * cols_dev), bf16),
            pltpu.VMEM((CHUNKS * mix_side, mix_side), bf16),
            dma((rows_n,)),
            dma((rows_n,)),
            dma((CHUNKS, rows_n)),
            dma((CHUNKS, rows_n)),
            dma((CHUNKS, cols_n)),
            dma((CHUNKS, cols_n)),
            dma((CHUNKS, rows_n)),
            dma((CHUNKS, rows_n)),
            dma((2 * CHUNKS + 4,)),
            dma((2 * cols_dev // TABLE_LANES,)),
        ],
        compiler_params=pltpu.CompilerParams(
            collective_id=0, has_side_effects=True, vmem_limit_bytes=56 << 20
        ),
    )(
        tile_density,
        tile_dest.reshape(1, tile_count),
        tile_place.reshape(1, tile_count),
        tables,
    )
    return pl.pallas_call(
        final_kernel,
        out_shape=jax.ShapeDtypeStruct((rows_dev, 2, cols_dev), jnp.float32),
        in_specs=[vmem, anywhere, vmem],
        out_specs=vmem,
        scratch_shapes=[pltpu.VMEM((2 * rows_dev, cols_dev), bf16), dma((CHUNKS,))],
        compiler_params=pltpu.CompilerParams(vmem_limit_bytes=56 << 20),
    )(final, section.reshape(2 * rows_dev, cols_dev), psf_spectrum)


def solution(mesh):
    in_specs = (
        P(("rows", "cols"), None, None),
        P(("rows", "cols"), None),
        P(("rows", "cols")),
        P("rows", "cols"),
    )
    out_specs = P("rows", None, "cols")

    def local(tile_density, tile_dest, tile_place, psf_spectrum):
        fast = fits(
            lax.axis_size("rows"),
            lax.axis_size("cols"),
            *tile_density.shape[:2],
            *psf_spectrum.shape,
        )
        run = on_device_kernels if fast else on_device
        return run(tile_density, tile_dest, tile_place, psf_spectrum)

    return jax.shard_map(
        local, mesh=mesh, in_specs=in_specs, out_specs=out_specs, check_vma=False
    )
```

```python
import functools
import math

import jax
import jax.numpy as jnp
import numpy as np
from jax import lax
from jax.experimental import pallas as pl
from jax.experimental.pallas import tpu as pltpu
from jax.sharding import PartitionSpec as P


def make_table(length, factor):
    positions = jnp.arange(length, dtype=jnp.int32)
    angles = (
        2.0
        * math.pi
        / length
        * (positions[:, None] * positions[None, :] % length).astype(jnp.float32)
    )
    cosine = jnp.cos(angles) * factor
    sine_part = jnp.sin(angles) * factor
    upper_rows = jnp.stack([cosine, -sine_part], 1)
    bottom = jnp.stack([sine_part, cosine], 1)
    return jnp.stack([upper_rows, bottom], 0).astype(jnp.bfloat16)


def twiddle(real_part, imag_part, position, frequency, period):
    angles = 2.0 * math.pi / period * (position * frequency % period).astype(jnp.float32)
    cosine = jnp.cos(angles)
    sine_part = jnp.sin(angles)
    return (real_part * cosine + imag_part * sine_part, imag_part * cosine - real_part * sine_part)


def on_device(tile_density, tile_dest, tile_place, psf_spectrum):
    tile_count, tile_side, _ = tile_density.shape
    rows_dev, cols_dev = psf_spectrum.shape
    rows_n = lax.axis_size("rows")
    cols_n = lax.axis_size("cols")
    capacity = max(2, 2 * tile_count // rows_n)
    slot_total = rows_n * capacity
    target = tile_dest[:, 0]
    matches = (target[:, None] == jnp.arange(rows_n, dtype=jnp.int32)[None, :]).astype(jnp.int32)
    order_within = jnp.sum((jnp.cumsum(matches, 0) - matches) * matches, 1)
    slot_index = target * capacity + order_within
    chosen = slot_index[:, None] == jnp.arange(slot_total, dtype=jnp.int32)[None, :]
    tiles_flat = tile_density.reshape(tile_count, tile_side * tile_side)
    outgoing = jnp.einsum(
        "ts,tc->sc", chosen.astype(jnp.bfloat16), tiles_flat, preferred_element_type=jnp.float32
    ).astype(jnp.bfloat16)
    labels = jnp.sum(jnp.where(chosen, (tile_place + 1)[:, None], 0), axis=0)
    arrived, arrived_marks = (
        lax.all_to_all(outgoing, "rows", split_axis=0, concat_axis=0, tiled=True),
        lax.all_to_all(labels, "rows", split_axis=0, concat_axis=0, tiled=True),
    )
    per_row = cols_dev // tile_side
    positions_count = rows_dev // tile_side * per_row
    placement_hot = (
        arrived_marks[:, None] - 1 == jnp.arange(positions_count, dtype=jnp.int32)[None, :]
    ).astype(jnp.bfloat16)
    cell_tiles = jnp.einsum(
        "sp,sc->pc", placement_hot, arrived, preferred_element_type=jnp.float32
    ).astype(jnp.bfloat16)
    density_grid = cell_tiles.reshape(
        rows_dev // tile_side, per_row, tile_side, tile_side
    ).transpose(0, 2, 1, 3)
    density_grid = density_grid.reshape(rows_dev, cols_dev)
    me_col = lax.axis_index("cols")
    highest = lax.Precision.HIGHEST
    slab_cols = cols_dev * cols_n
    part_cols = cols_dev // cols_n
    pieces = lax.all_to_all(density_grid[None], "cols", split_axis=2, concat_axis=0, tiled=True)
    frequency = jnp.arange(cols_n, dtype=jnp.int32)
    angles = (
        2.0
        * math.pi
        / cols_n
        * (frequency[:, None] * frequency[None, :] % cols_n).astype(jnp.float32)
    )
    values = pieces.astype(jnp.float32)
    sum_real = jnp.einsum("ejt,ek->kjt", values, jnp.cos(angles), precision=highest)
    sum_imag = -jnp.einsum("ejt,ek->kjt", values, jnp.sin(angles), precision=highest)
    columns = (me_col * part_cols + jnp.arange(part_cols, dtype=jnp.int32))[None, None, :]
    real_part, imag_part = twiddle(sum_real, sum_imag, columns, frequency[:, None, None], slab_cols)
    packed = jnp.stack([real_part, imag_part], 2).astype(jnp.bfloat16)
    returned = lax.all_to_all(packed, "cols", split_axis=0, concat_axis=3, tiled=True)
    section_one = returned.reshape(rows_dev, 2 * cols_dev)
    row_table = make_table(cols_dev, 1.0 / math.sqrt(slab_cols)).reshape(2 * cols_dev, 2 * cols_dev)
    rows_spectrum = jnp.dot(section_one, row_table, preferred_element_type=jnp.float32).astype(
        jnp.bfloat16
    )
    rows_spectrum = rows_spectrum.reshape(rows_dev, 2, cols_dev)
    me_row = lax.axis_index("rows")
    group_rows = rows_dev // rows_n
    grid_rows = rows_dev * rows_n
    col_table = make_table(rows_n, 1.0).transpose(3, 2, 1, 0)
    column_block = lax.all_to_all(rows_spectrum, "rows", split_axis=0, concat_axis=0, tiled=True)
    item_width = column_block.shape[2]
    values = column_block.reshape(rows_n, group_rows, 2, item_width)
    combined = jnp.einsum("kqap,atpc->ktqc", col_table, values, preferred_element_type=jnp.float32)
    row_index = (me_row * group_rows + jnp.arange(group_rows, dtype=jnp.int32))[None, :, None]
    row_freq = jnp.arange(rows_n, dtype=jnp.int32)[:, None, None]
    real_two, imag_two = twiddle(
        combined[:, :, 0], combined[:, :, 1], row_index, row_freq, grid_rows
    )
    section_two = lax.all_to_all(
        jnp.stack([real_two, imag_two], 2).astype(jnp.bfloat16).reshape(rows_dev, 2, item_width),
        "rows",
        split_axis=0,
        concat_axis=0,
        tiled=True,
    )
    final_table = (
        make_table(rows_dev, 1.0 / math.sqrt(grid_rows))
        .transpose(3, 2, 1, 0)
        .reshape(2 * rows_dev, 2 * rows_dev)
    )
    result_spec = jnp.dot(
        final_table, section_two.reshape(2 * rows_dev, cols_dev), preferred_element_type=jnp.float32
    )
    result_spec = result_spec.reshape(rows_dev, 2, cols_dev)
    return result_spec * psf_spectrum.astype(jnp.float32)[:, None, :]


CHUNKS = 4
TABLE_LANES = 256
MESH = pl.DeviceIdType.MESH


def fits(rows_n, cols_n, tile_count, tile_side, rows_dev, cols_dev):
    return (
        cols_n == 4
        and rows_n > 1
        and tile_side * 2 == 128
        and tile_side % (rows_n * 2 * CHUNKS) == 0
        and tile_count % 16 == 0
        and tile_count <= 128
        and cols_dev % 128 == 0
        and rows_dev % tile_side == 0
        and 2 * (tile_side // rows_n // CHUNKS) * (rows_dev // tile_side) % 16 == 0
        and 2 * tile_side // CHUNKS * (rows_dev // tile_side) <= TABLE_LANES
        and 2 * cols_dev % TABLE_LANES == 0
        and rows_n * rows_dev * cols_dev * 2 <= 1 << 22
    )


def constants(rows_n, cols_n, tile_side, rows_dev, cols_dev):
    slab_cols, grid_rows = cols_dev * cols_n, rows_dev * rows_n
    bands = rows_dev // tile_side
    band_rows = tile_side // rows_n
    step_rows = band_rows // CHUNKS

    def parts(phase, factor):
        angles = 2.0 * np.pi * phase
        return np.cos(angles) * factor, -np.sin(angles) * factor

    f = np.arange(cols_dev)
    re, im = parts((f[:, None] * f[None, :] % cols_dev) / cols_dev, 1.0 / math.sqrt(slab_cols))
    row_table = np.block([[re, im], [-im, re]])
    bf16 = jnp.bfloat16
    k = np.arange(cols_n)
    re, im = parts((f[None, :] * k[:, None] % slab_cols) / slab_cols, 1.0)
    pair = np.concatenate([re, -im], 1)
    upper = pair.astype(bf16).astype(np.float64)
    extra = np.zeros((16, 2 * cols_dev))
    extra[: 2 * cols_n] = np.stack([upper, pair - upper], 1).reshape(2 * cols_n, -1)
    row_table = np.concatenate([row_table, extra], 0)
    b = (
        tile_side * np.arange(bands)[None, None, None, :]
        + band_rows * np.arange(rows_n)[:, None, None, None]
        + step_rows * np.arange(CHUNKS)[None, :, None, None]
        + np.arange(step_rows)[None, None, :, None]
    )
    u = np.arange(rows_n)
    row = b[:, :, None, None] + rows_dev * u[None, None, None, :, None, None]
    re, im = parts((row * u[None, None, :, None, None, None] % grid_rows) / grid_rows, 1.0)
    width = step_rows * bands
    mix = np.zeros((rows_n, CHUNKS, rows_n, 2, step_rows, bands, 2, step_rows, rows_n, bands), np.float32)
    for i in range(step_rows):
        for t in range(bands):
            mix[:, :, :, 0, i, t, 0, i, :, t] = re[:, :, :, :, i, t]
            mix[:, :, :, 0, i, t, 1, i, :, t] = -im[:, :, :, :, i, t]
            mix[:, :, :, 1, i, t, 0, i, :, t] = im[:, :, :, :, i, t]
            mix[:, :, :, 1, i, t, 1, i, :, t] = re[:, :, :, :, i, t]
    mix = mix.reshape(rows_n, CHUNKS, rows_n * 2 * width, 2 * rows_n * width)
    w = np.arange(rows_dev)
    order = b.transpose(1, 0, 2, 3).reshape(CHUNKS, rows_n, 1, width)
    re, im = parts(
        (w[:, None, None, None, None] * order % rows_dev) / rows_dev, 1.0 / math.sqrt(grid_rows)
    )
    final = np.stack(
        [np.concatenate([re, -im], 3), np.concatenate([im, re], 3)], 0
    ).reshape(2 * rows_dev, 2 * rows_dev)
    lanes = TABLE_LANES
    mix = np.pad(mix.reshape(-1, mix.shape[-1]), ((0, 0), (0, lanes - mix.shape[-1])))
    blocks = [row_table[:, at : at + lanes] for at in range(0, row_table.shape[1], lanes)]
    tables = np.concatenate(blocks + [mix], 0)
    return jnp.asarray(tables.astype(bf16)), jnp.asarray(final.astype(bf16))


def exchange_kernel(
    rows_n, cols_n, tile_side, bands, per_row,
    tiles_hbm, dest_hbm, place_hbm, tables_hbm,
    out_ref,
    owned, raw, wide, banded, labels, arrived, dense, outgoing, table, mix,
    label_send, label_recv, a_send, a_recv, g_send, g_recv, e_send, e_recv, local_sem, table_sem,
):
    me_row, me_col = lax.axis_index("rows"), lax.axis_index("cols")
    tiles = tiles_hbm.shape[0]
    chunk = arrived.shape[3]
    cols_dev = per_row * tile_side
    row_peers = [lax.rem(me_row + d, rows_n) for d in range(rows_n)]
    row_sources = [lax.rem(me_row + rows_n - d, rows_n) for d in range(rows_n)]
    sibling = me_col + 1 - 2 * lax.rem(me_col, 2)
    col_blocks = [me_col, sibling, lax.rem(me_col + 2, cols_n), lax.rem(sibling + 2, cols_n)]

    barrier = pltpu.get_barrier_semaphore()
    for d in range(1, rows_n):
        pl.semaphore_signal(barrier, inc=1, device_id=(row_peers[d], me_col), device_id_type=MESH)
    for d in range(1, 3):
        pl.semaphore_signal(barrier, inc=1, device_id=(me_row, col_blocks[d]), device_id_type=MESH)

    raw_copy = pltpu.make_async_copy(tiles_hbm, raw, local_sem.at[CHUNKS + 1])
    raw_copy.start()
    owned_copies = [
        pltpu.make_async_copy(dest_hbm, owned.at[0], local_sem.at[2 * CHUNKS + 2]),
        pltpu.make_async_copy(place_hbm, owned.at[1], local_sem.at[2 * CHUNKS + 3]),
    ]
    table_rows, lanes = table.shape[0], TABLE_LANES
    table_copies = [
        pltpu.make_async_copy(
            tables_hbm.at[pl.ds(j * table_rows, table_rows), :],
            table.at[:, pl.ds(j * lanes, lanes)],
            table_sem.at[j],
        )
        for j in range(table.shape[1] // lanes)
    ]
    mix_start = table_rows * len(table_copies) + me_row * mix.shape[0]
    mix_copy = pltpu.make_async_copy(
        tables_hbm.at[pl.ds(pl.multiple_of(mix_start, 16), mix.shape[0]), pl.ds(0, mix.shape[1])],
        mix,
        local_sem.at[CHUNKS],
    )
    for copy in owned_copies + table_copies + [mix_copy]:
        copy.start()
    for copy in owned_copies:
        copy.wait()
    slab, place = owned[0], owned[1]
    code = (place % per_row) * (rows_n * bands) + slab * bands + place // per_row
    labels[0] = jnp.broadcast_to(
        jnp.concatenate([code, jnp.zeros((1, 128 - tiles), jnp.int32)], 1)
        if tiles < 128
        else code,
        labels.shape[1:],
    )
    low_lanes = lax.broadcasted_iota(jnp.int32, (max(tiles, rows_n * bands), 128), 1) < tile_side
    raw_copy.wait()
    wide[:, 0:tile_side] = raw[...].reshape(tiles * tile_side, tile_side).astype(jnp.float32)
    own_copies = [
        pltpu.make_async_copy(banded.at[h, me_row], arrived.at[h, 0], local_sem.at[h])
        for h in range(CHUNKS)
    ]

    def band_stage(h):
        for owner in range(rows_n):
            for pair in range(chunk // 128):
                row = (owner * CHUNKS + h) * (chunk // tile_side) + 2 * pair
                first = wide[pl.ds(row, tiles, stride=tile_side), :]
                second = wide[pl.ds(row + 1, tiles, stride=tile_side), :]
                both = jnp.where(low_lanes[:tiles], first, pltpu.roll(second, tile_side, 1))
                banded[h, owner, :, 128 * pair : 128 * pair + 128] = both.astype(jnp.bfloat16)
        own_copies[h].start()

    band_stage(0)
    pl.semaphore_wait(barrier, rows_n + 1)

    def band_copy(h, d):
        return pltpu.make_async_remote_copy(
            src_ref=banded.at[h, row_peers[d]],
            dst_ref=arrived.at[h, d],
            send_sem=a_send.at[h, d],
            recv_sem=a_recv.at[h, d],
            device_id=(row_peers[d], me_col),
            device_id_type=MESH,
        )

    label_copies = [
        pltpu.make_async_remote_copy(
            src_ref=labels.at[0],
            dst_ref=labels.at[d],
            send_sem=label_send.at[d],
            recv_sem=label_recv.at[d],
            device_id=(row_peers[d], me_col),
            device_id_type=MESH,
        )
        for d in range(1, rows_n)
    ]
    band_copies = [[band_copy(h, d) for d in range(1, rows_n)] for h in range(CHUNKS)]
    for copy in label_copies:
        copy.start()
    def band_start(h):
        for copy in band_copies[h]:
            copy.start()

    band_start(0)
    for h in range(1, CHUNKS):
        band_stage(h)
        band_start(h)

    for copy in label_copies:
        copy.wait_recv()
    codes = jnp.concatenate([labels[d, 0:1, 0:tiles] for d in range(rows_n)], 1)
    cells = per_row * rows_n * bands
    hot = jnp.where(
        lax.broadcasted_iota(jnp.int32, (cells, rows_n * tiles), 0) == codes, 1.0, 0.0
    ).astype(jnp.bfloat16)

    for copy in table_copies + [mix_copy]:
        copy.wait()
    terms = table[2 * cols_dev :, :].astype(jnp.float32)
    row = lax.broadcasted_iota(jnp.int32, terms.shape, 0)
    twiddle_pair = jnp.sum(jnp.where(row // 2 == me_col, terms, 0.0), axis=0, keepdims=True)
    mix_rows = mix.shape[0] // CHUNKS
    cosine, sine = twiddle_pair[:, :cols_dev], twiddle_pair[:, cols_dev:]

    gathers = []

    def block_copy(h, source, peer, slot):
        return pltpu.make_async_remote_copy(
            src_ref=dense.at[h, source],
            dst_ref=dense.at[h, slot],
            send_sem=g_send.at[h, slot],
            recv_sem=g_recv.at[h, slot],
            device_id=(me_row, col_blocks[peer]),
            device_id_type=MESH,
        )

    def density_stage(h):
        own_copies[h].wait()
        for copy in band_copies[h]:
            copy.wait_recv()
        summed = jnp.dot(
            hot,
            arrived[h].reshape(rows_n * tiles, chunk),
            preferred_element_type=jnp.float32,
        )
        height = rows_n * bands
        for pair in range(chunk // 128):
            lanes = slice(128 * pair, 128 * pair + 128)
            for q in range(per_row // 2):
                left = summed[2 * q * height : (2 * q + 1) * height, lanes]
                right = summed[(2 * q + 1) * height : (2 * q + 2) * height, lanes]
                upper = jnp.where(low_lanes[:height], left, pltpu.roll(right, tile_side, 1))
                lower = jnp.where(low_lanes[:height], pltpu.roll(left, tile_side, 1), right)
                out_lanes = slice(128 * q, 128 * q + 128)
                first = 2 * pair * height
                dense[h, 0, first : first + height, out_lanes] = upper.astype(jnp.bfloat16)
                dense[h, 0, first + height : first + 2 * height, out_lanes] = lower.astype(
                    jnp.bfloat16
                )
        group = [block_copy(h, 0, 2, 2), block_copy(h, 0, 1, 1)]
        for copy in group:
            copy.start()
        gathers.append(group)

    def forward_stage(h):
        gathers[h][0].wait_recv()
        copy = block_copy(h, 2, 1, 3)
        copy.start()
        gathers[h].append(copy)

    sends = []

    def section_stage(h):
        for copy in gathers[h][1:]:
            copy.wait_recv()
        sum_real = sum_imag = None
        for d in range(cols_n):
            turn = lax.rem(col_blocks[d] * me_col, cols_n)
            cos_turn = jnp.where(turn == 0, 1.0, jnp.where(turn == 2, -1.0, 0.0))
            sin_turn = jnp.where(turn == 1, 1.0, jnp.where(turn == 3, -1.0, 0.0))
            value = dense[h, d].astype(jnp.float32)
            real, imag = value * cos_turn, value * (-sin_turn)
            sum_real = real if d == 0 else sum_real + real
            sum_imag = imag if d == 0 else sum_imag + imag
        section_one = jnp.concatenate(
            [sum_real * cosine + sum_imag * sine, sum_imag * cosine - sum_real * sine], 1
        ).astype(jnp.bfloat16)
        spectrum = jnp.dot(section_one, table[0 : 2 * cols_dev, :], preferred_element_type=jnp.float32)
        spectrum = spectrum.astype(jnp.bfloat16)
        stacked = jnp.concatenate([spectrum[:, :cols_dev], spectrum[:, cols_dev:]], 0)
        section_two = jnp.dot(
            mix[h * mix_rows : (h + 1) * mix_rows, :], stacked, preferred_element_type=jnp.float32
        )
        outgoing[h] = section_two.astype(jnp.bfloat16).reshape(outgoing.shape[1:])
        group = [
            pltpu.make_async_remote_copy(
                src_ref=outgoing.at[h, row_peers[d]],
                dst_ref=out_ref.at[h, me_row],
                send_sem=e_send.at[h, d],
                recv_sem=e_recv.at[h, d],
                device_id=(row_peers[d], me_col),
                device_id_type=MESH,
            )
            for d in range(1, rows_n)
        ]
        for copy in group:
            copy.start()
        own = pltpu.make_async_copy(
            outgoing.at[h, me_row], out_ref.at[h, me_row], local_sem.at[CHUNKS + 2 + h]
        )
        own.start()
        sends.append((group, own))

    for h in range(CHUNKS):
        density_stage(h)
        if h > 0:
            forward_stage(h - 1)
        if h > 1:
            section_stage(h - 2)
    section_stage(CHUNKS - 2)
    forward_stage(CHUNKS - 1)
    section_stage(CHUNKS - 1)

    for copy in label_copies:
        copy.wait_send()
    for h in range(CHUNKS):
        for copy in band_copies[h] + gathers[h]:
            copy.wait_send()
    for h in range(CHUNKS):
        group, own = sends[h]
        own.wait()
        for d in range(1, rows_n):
            pltpu.make_async_remote_copy(
                src_ref=outgoing.at[h, row_peers[d]],
                dst_ref=out_ref.at[h, row_sources[d]],
                send_sem=e_send.at[h, d],
                recv_sem=e_recv.at[h, d],
                device_id=(row_peers[d], me_col),
                device_id_type=MESH,
            ).wait()


def final_kernel(final_ref, section_ref, psf_ref, out_ref):
    rows_dev = psf_ref.shape[0]
    result = jnp.dot(final_ref[...], section_ref[...], preferred_element_type=jnp.float32)
    psf = psf_ref[...].astype(jnp.float32)
    out_ref[:, 0, :] = result[:rows_dev] * psf
    out_ref[:, 1, :] = result[rows_dev:] * psf


def on_device_kernels(tile_density, tile_dest, tile_place, psf_spectrum):
    tile_count, tile_side, _ = tile_density.shape
    rows_dev, cols_dev = psf_spectrum.shape
    rows_n = lax.axis_size("rows")
    cols_n = lax.axis_size("cols")
    bands, per_row = rows_dev // tile_side, cols_dev // tile_side
    step_rows = tile_side // rows_n // CHUNKS
    chunk = step_rows * tile_side
    tables, final = constants(rows_n, cols_n, tile_side, rows_dev, cols_dev)
    bf16 = jnp.bfloat16
    vmem = pl.BlockSpec(memory_space=pltpu.VMEM)
    anywhere = pl.BlockSpec(memory_space=pl.ANY)
    width = 2 * step_rows * bands
    mix_side = width * rows_n
    dma = pltpu.SemaphoreType.DMA
    section = pl.pallas_call(
        functools.partial(exchange_kernel, rows_n, cols_n, tile_side, bands, per_row),
        out_shape=jax.ShapeDtypeStruct((CHUNKS, rows_n, width, cols_dev), bf16),
        in_specs=[anywhere] * 4,
        out_specs=vmem,
        scratch_shapes=[
            pltpu.VMEM((2, 1, tile_count), jnp.int32),
            pltpu.VMEM(tile_density.shape, bf16),
            pltpu.VMEM((tile_count * tile_side, 128), jnp.float32),
            pltpu.VMEM((CHUNKS, rows_n, tile_count, chunk), bf16),
            pltpu.VMEM((rows_n, 8, 128), jnp.int32),
            pltpu.VMEM((CHUNKS, rows_n, tile_count, chunk), bf16),
            pltpu.VMEM((CHUNKS, cols_n, step_rows * rows_n * bands, cols_dev), bf16),
            pltpu.VMEM((CHUNKS, rows_n, width, cols_dev), bf16),
            pltpu.VMEM((2 * cols_dev + 16, 2 * cols_dev), bf16),
            pltpu.VMEM((CHUNKS * mix_side, mix_side), bf16),
            dma((rows_n,)),
            dma((rows_n,)),
            dma((CHUNKS, rows_n)),
            dma((CHUNKS, rows_n)),
            dma((CHUNKS, cols_n)),
            dma((CHUNKS, cols_n)),
            dma((CHUNKS, rows_n)),
            dma((CHUNKS, rows_n)),
            dma((2 * CHUNKS + 4,)),
            dma((2 * cols_dev // TABLE_LANES,)),
        ],
        compiler_params=pltpu.CompilerParams(
            collective_id=0, has_side_effects=True, vmem_limit_bytes=56 << 20
        ),
    )(
        tile_density,
        tile_dest.reshape(1, tile_count),
        tile_place.reshape(1, tile_count),
        tables,
    )
    return pl.pallas_call(
        final_kernel,
        out_shape=jax.ShapeDtypeStruct((rows_dev, 2, cols_dev), jnp.float32),
        in_specs=[vmem, vmem, vmem],
        out_specs=vmem,
        compiler_params=pltpu.CompilerParams(vmem_limit_bytes=32 << 20),
    )(final, section.reshape(2 * rows_dev, cols_dev), psf_spectrum)


def solution(mesh):
    in_specs = (
        P(("rows", "cols"), None, None),
        P(("rows", "cols"), None),
        P(("rows", "cols")),
        P("rows", "cols"),
    )
    out_specs = P("rows", None, "cols")

    def local(tile_density, tile_dest, tile_place, psf_spectrum):
        fast = fits(
            lax.axis_size("rows"),
            lax.axis_size("cols"),
            *tile_density.shape[:2],
            *psf_spectrum.shape,
        )
        run = on_device_kernels if fast else on_device
        return run(tile_density, tile_dest, tile_place, psf_spectrum)

    return jax.shard_map(
        local, mesh=mesh, in_specs=in_specs, out_specs=out_specs, check_vma=False
    )
```

```python
import functools
import math

import jax
import jax.numpy as jnp
import numpy as np
from jax import lax
from jax.experimental import pallas as pl
from jax.experimental.pallas import tpu as pltpu
from jax.sharding import PartitionSpec as P


def make_table(length, factor):
    positions = jnp.arange(length, dtype=jnp.int32)
    angles = (
        2.0
        * math.pi
        / length
        * (positions[:, None] * positions[None, :] % length).astype(jnp.float32)
    )
    cosine = jnp.cos(angles) * factor
    sine_part = jnp.sin(angles) * factor
    upper_rows = jnp.stack([cosine, -sine_part], 1)
    bottom = jnp.stack([sine_part, cosine], 1)
    return jnp.stack([upper_rows, bottom], 0).astype(jnp.bfloat16)


def twiddle(real_part, imag_part, position, frequency, period):
    angles = 2.0 * math.pi / period * (position * frequency % period).astype(jnp.float32)
    cosine = jnp.cos(angles)
    sine_part = jnp.sin(angles)
    return (real_part * cosine + imag_part * sine_part, imag_part * cosine - real_part * sine_part)


def on_device(tile_density, tile_dest, tile_place, psf_spectrum):
    tile_count, tile_side, _ = tile_density.shape
    rows_dev, cols_dev = psf_spectrum.shape
    rows_n = lax.axis_size("rows")
    cols_n = lax.axis_size("cols")
    capacity = max(2, 2 * tile_count // rows_n)
    slot_total = rows_n * capacity
    target = tile_dest[:, 0]
    matches = (target[:, None] == jnp.arange(rows_n, dtype=jnp.int32)[None, :]).astype(jnp.int32)
    order_within = jnp.sum((jnp.cumsum(matches, 0) - matches) * matches, 1)
    slot_index = target * capacity + order_within
    chosen = slot_index[:, None] == jnp.arange(slot_total, dtype=jnp.int32)[None, :]
    tiles_flat = tile_density.reshape(tile_count, tile_side * tile_side)
    outgoing = jnp.einsum(
        "ts,tc->sc", chosen.astype(jnp.bfloat16), tiles_flat, preferred_element_type=jnp.float32
    ).astype(jnp.bfloat16)
    labels = jnp.sum(jnp.where(chosen, (tile_place + 1)[:, None], 0), axis=0)
    arrived, arrived_marks = (
        lax.all_to_all(outgoing, "rows", split_axis=0, concat_axis=0, tiled=True),
        lax.all_to_all(labels, "rows", split_axis=0, concat_axis=0, tiled=True),
    )
    per_row = cols_dev // tile_side
    positions_count = rows_dev // tile_side * per_row
    placement_hot = (
        arrived_marks[:, None] - 1 == jnp.arange(positions_count, dtype=jnp.int32)[None, :]
    ).astype(jnp.bfloat16)
    cell_tiles = jnp.einsum(
        "sp,sc->pc", placement_hot, arrived, preferred_element_type=jnp.float32
    ).astype(jnp.bfloat16)
    density_grid = cell_tiles.reshape(
        rows_dev // tile_side, per_row, tile_side, tile_side
    ).transpose(0, 2, 1, 3)
    density_grid = density_grid.reshape(rows_dev, cols_dev)
    me_col = lax.axis_index("cols")
    highest = lax.Precision.HIGHEST
    slab_cols = cols_dev * cols_n
    part_cols = cols_dev // cols_n
    pieces = lax.all_to_all(density_grid[None], "cols", split_axis=2, concat_axis=0, tiled=True)
    frequency = jnp.arange(cols_n, dtype=jnp.int32)
    angles = (
        2.0
        * math.pi
        / cols_n
        * (frequency[:, None] * frequency[None, :] % cols_n).astype(jnp.float32)
    )
    values = pieces.astype(jnp.float32)
    sum_real = jnp.einsum("ejt,ek->kjt", values, jnp.cos(angles), precision=highest)
    sum_imag = -jnp.einsum("ejt,ek->kjt", values, jnp.sin(angles), precision=highest)
    columns = (me_col * part_cols + jnp.arange(part_cols, dtype=jnp.int32))[None, None, :]
    real_part, imag_part = twiddle(sum_real, sum_imag, columns, frequency[:, None, None], slab_cols)
    packed = jnp.stack([real_part, imag_part], 2).astype(jnp.bfloat16)
    returned = lax.all_to_all(packed, "cols", split_axis=0, concat_axis=3, tiled=True)
    section_one = returned.reshape(rows_dev, 2 * cols_dev)
    row_table = make_table(cols_dev, 1.0 / math.sqrt(slab_cols)).reshape(2 * cols_dev, 2 * cols_dev)
    rows_spectrum = jnp.dot(section_one, row_table, preferred_element_type=jnp.float32).astype(
        jnp.bfloat16
    )
    rows_spectrum = rows_spectrum.reshape(rows_dev, 2, cols_dev)
    me_row = lax.axis_index("rows")
    group_rows = rows_dev // rows_n
    grid_rows = rows_dev * rows_n
    col_table = make_table(rows_n, 1.0).transpose(3, 2, 1, 0)
    column_block = lax.all_to_all(rows_spectrum, "rows", split_axis=0, concat_axis=0, tiled=True)
    item_width = column_block.shape[2]
    values = column_block.reshape(rows_n, group_rows, 2, item_width)
    combined = jnp.einsum("kqap,atpc->ktqc", col_table, values, preferred_element_type=jnp.float32)
    row_index = (me_row * group_rows + jnp.arange(group_rows, dtype=jnp.int32))[None, :, None]
    row_freq = jnp.arange(rows_n, dtype=jnp.int32)[:, None, None]
    real_two, imag_two = twiddle(
        combined[:, :, 0], combined[:, :, 1], row_index, row_freq, grid_rows
    )
    section_two = lax.all_to_all(
        jnp.stack([real_two, imag_two], 2).astype(jnp.bfloat16).reshape(rows_dev, 2, item_width),
        "rows",
        split_axis=0,
        concat_axis=0,
        tiled=True,
    )
    final_table = (
        make_table(rows_dev, 1.0 / math.sqrt(grid_rows))
        .transpose(3, 2, 1, 0)
        .reshape(2 * rows_dev, 2 * rows_dev)
    )
    result_spec = jnp.dot(
        final_table, section_two.reshape(2 * rows_dev, cols_dev), preferred_element_type=jnp.float32
    )
    result_spec = result_spec.reshape(rows_dev, 2, cols_dev)
    return result_spec * psf_spectrum.astype(jnp.float32)[:, None, :]


CHUNKS = 4
MESH = pl.DeviceIdType.MESH


def fits(rows_n, cols_n, tile_count, tile_side, rows_dev, cols_dev):
    return (
        cols_n == 4
        and rows_n > 1
        and tile_side * 2 == 128
        and tile_side % (rows_n * 2 * CHUNKS) == 0
        and tile_count % 16 == 0
        and tile_count <= 128
        and cols_dev % 128 == 0
        and rows_dev % tile_side == 0
        and 2 * (tile_side // rows_n // CHUNKS) * (rows_dev // tile_side) % 16 == 0
        and 2 * tile_side * (rows_dev // tile_side) <= 2 * cols_dev
        and 2 * tile_side // CHUNKS * (rows_dev // tile_side) % 128 == 0
        and cols_n * cols_dev <= 2048
        and rows_n * rows_dev * cols_dev * 2 <= 1 << 22
    )


def constants(rows_n, cols_n, tile_side, rows_dev, cols_dev):
    slab_cols, grid_rows = cols_dev * cols_n, rows_dev * rows_n
    bands = rows_dev // tile_side
    band_rows = tile_side // rows_n
    step_rows = band_rows // CHUNKS

    def parts(phase, factor):
        angles = 2.0 * np.pi * phase
        return np.cos(angles) * factor, -np.sin(angles) * factor

    bf16 = jnp.bfloat16
    k = np.arange(cols_n)
    sibling = k + 1 - 2 * (k % 2)
    held = np.stack([k, sibling, (k + 2) % cols_n, (sibling + 2) % cols_n], 1)
    column = (held[:, :, None] * cols_dev + np.arange(cols_dev)).reshape(cols_n, slab_cols, 1)
    frequency = k[:, None, None] + cols_n * np.arange(cols_dev)
    waves = np.stack(parts(np.arange(slab_cols) / slab_cols, 1.0 / math.sqrt(slab_cols)), 0)
    re, im = waves.astype(bf16)[:, column * frequency % slab_cols]
    row_tables = np.concatenate([re, im], 2)
    b = (
        tile_side * np.arange(bands)[None, None, None, :]
        + band_rows * np.arange(rows_n)[:, None, None, None]
        + step_rows * np.arange(CHUNKS)[None, :, None, None]
        + np.arange(step_rows)[None, None, :, None]
    )
    u = np.arange(rows_n)
    row = b[:, :, None, None] + rows_dev * u[None, None, None, :, None, None]
    re, im = parts((row * u[None, None, :, None, None, None] % grid_rows) / grid_rows, 1.0)
    width = step_rows * bands
    mix = np.zeros((rows_n, CHUNKS, rows_n, 2, step_rows, bands, 2, step_rows, rows_n, bands), np.float32)
    for i in range(step_rows):
        for t in range(bands):
            mix[:, :, :, 0, i, t, 0, i, :, t] = re[:, :, :, :, i, t]
            mix[:, :, :, 0, i, t, 1, i, :, t] = -im[:, :, :, :, i, t]
            mix[:, :, :, 1, i, t, 0, i, :, t] = im[:, :, :, :, i, t]
            mix[:, :, :, 1, i, t, 1, i, :, t] = re[:, :, :, :, i, t]
    mix = mix.reshape(rows_n, CHUNKS, rows_n * 2 * width, 2 * rows_n * width)
    w = np.arange(rows_dev)
    order = b.transpose(1, 0, 2, 3).reshape(CHUNKS, rows_n, 1, width)
    re, im = parts(
        (w[:, None, None, None, None] * order % rows_dev) / rows_dev, 1.0 / math.sqrt(grid_rows)
    )
    final = np.stack(
        [np.concatenate([re, -im], 3), np.concatenate([im, re], 3)], 0
    ).reshape(2 * rows_dev, 2 * rows_dev)
    side = mix.shape[-1]
    mix = mix.transpose(0, 2, 1, 3).reshape(rows_n * side, CHUNKS * side)
    mix = np.pad(mix, ((0, 0), (0, 2 * cols_dev - CHUNKS * side)))
    tables = np.concatenate([row_tables.reshape(-1, 2 * cols_dev), mix.astype(bf16)], 0)
    return jnp.asarray(tables), jnp.asarray(final.astype(bf16))


def exchange_kernel(
    rows_n, cols_n, tile_side, bands, per_row,
    tiles_hbm, dest_hbm, place_hbm, tables_hbm,
    out_ref,
    owned, raw, wide, banded, labels, arrived, dense, outgoing, table, mix,
    label_send, label_recv, a_send, a_recv, g_send, g_recv, e_send, e_recv, local_sem, table_sem,
):
    me_row, me_col = lax.axis_index("rows"), lax.axis_index("cols")
    tiles = tiles_hbm.shape[0]
    chunk = arrived.shape[3]
    cols_dev = per_row * tile_side
    row_peers = [lax.rem(me_row + d, rows_n) for d in range(rows_n)]
    row_sources = [lax.rem(me_row + rows_n - d, rows_n) for d in range(rows_n)]
    sibling = me_col + 1 - 2 * lax.rem(me_col, 2)
    col_blocks = [me_col, sibling, lax.rem(me_col + 2, cols_n), lax.rem(sibling + 2, cols_n)]

    barrier = pltpu.get_barrier_semaphore()
    for d in range(1, rows_n):
        pl.semaphore_signal(barrier, inc=1, device_id=(row_peers[d], me_col), device_id_type=MESH)
    for d in range(1, 3):
        pl.semaphore_signal(barrier, inc=1, device_id=(me_row, col_blocks[d]), device_id_type=MESH)

    raw_copy = pltpu.make_async_copy(tiles_hbm, raw, local_sem.at[CHUNKS + 1])
    raw_copy.start()
    owned_copies = [
        pltpu.make_async_copy(dest_hbm, owned.at[0], local_sem.at[2 * CHUNKS + 2]),
        pltpu.make_async_copy(place_hbm, owned.at[1], local_sem.at[2 * CHUNKS + 3]),
    ]
    table_rows = table.shape[0]
    table_start = pl.multiple_of(me_col * table_rows, 16)
    table_copies = [
        pltpu.make_async_copy(
            tables_hbm.at[pl.ds(table_start, table_rows), :], table, table_sem.at[0]
        )
    ]
    mix_start = table_rows * cols_n + me_row * mix.shape[0]
    mix_copy = pltpu.make_async_copy(
        tables_hbm.at[pl.ds(pl.multiple_of(mix_start, 16), mix.shape[0]), pl.ds(0, mix.shape[1])],
        mix,
        local_sem.at[CHUNKS],
    )
    for copy in owned_copies + table_copies + [mix_copy]:
        copy.start()
    for copy in owned_copies:
        copy.wait()
    slab, place = owned[0], owned[1]
    code = (place % per_row) * (rows_n * bands) + slab * bands + place // per_row
    labels[0] = jnp.broadcast_to(
        jnp.concatenate([code, jnp.zeros((1, 128 - tiles), jnp.int32)], 1)
        if tiles < 128
        else code,
        labels.shape[1:],
    )
    low_lanes = lax.broadcasted_iota(jnp.int32, (max(tiles, rows_n * bands), 128), 1) < tile_side
    raw_copy.wait()
    wide[:, 0:tile_side] = raw[...].reshape(tiles * tile_side, tile_side).astype(jnp.float32)
    own_copies = [
        pltpu.make_async_copy(banded.at[h, me_row], arrived.at[h, 0], local_sem.at[h])
        for h in range(CHUNKS)
    ]

    def band_stage(h):
        for owner in range(rows_n):
            for pair in range(chunk // 128):
                row = (owner * CHUNKS + h) * (chunk // tile_side) + 2 * pair
                first = wide[pl.ds(row, tiles, stride=tile_side), :]
                second = wide[pl.ds(row + 1, tiles, stride=tile_side), :]
                both = jnp.where(low_lanes[:tiles], first, pltpu.roll(second, tile_side, 1))
                banded[h, owner, :, 128 * pair : 128 * pair + 128] = both.astype(jnp.bfloat16)
        own_copies[h].start()

    band_stage(0)
    pl.semaphore_wait(barrier, rows_n + 1)

    def band_copy(h, d):
        return pltpu.make_async_remote_copy(
            src_ref=banded.at[h, row_peers[d]],
            dst_ref=arrived.at[h, d],
            send_sem=a_send.at[h, d],
            recv_sem=a_recv.at[h, d],
            device_id=(row_peers[d], me_col),
            device_id_type=MESH,
        )

    label_copies = [
        pltpu.make_async_remote_copy(
            src_ref=labels.at[0],
            dst_ref=labels.at[d],
            send_sem=label_send.at[d],
            recv_sem=label_recv.at[d],
            device_id=(row_peers[d], me_col),
            device_id_type=MESH,
        )
        for d in range(1, rows_n)
    ]
    band_copies = [[band_copy(h, d) for d in range(1, rows_n)] for h in range(CHUNKS)]
    for copy in label_copies:
        copy.start()
    def band_start(h):
        for copy in band_copies[h]:
            copy.start()

    band_start(0)
    for h in range(1, CHUNKS):
        band_stage(h)
    band_start(1)

    for copy in label_copies:
        copy.wait_recv()
    codes = jnp.concatenate([labels[d, 0:1, 0:tiles] for d in range(rows_n)], 1)
    cells = per_row * rows_n * bands
    hot = jnp.where(
        lax.broadcasted_iota(jnp.int32, (cells, rows_n * tiles), 0) == codes, 1.0, 0.0
    ).astype(jnp.bfloat16)

    for copy in table_copies + [mix_copy]:
        copy.wait()
    mix_side = mix.shape[0]

    gathers = []

    def block_copy(h, source, peer, slot):
        return pltpu.make_async_remote_copy(
            src_ref=dense.at[h, source],
            dst_ref=dense.at[h, slot],
            send_sem=g_send.at[h, slot],
            recv_sem=g_recv.at[h, slot],
            device_id=(me_row, col_blocks[peer]),
            device_id_type=MESH,
        )

    def density_stage(h):
        own_copies[h].wait()
        for copy in band_copies[h]:
            copy.wait_recv()
        if h + 2 < CHUNKS:
            band_start(h + 2)
        summed = jnp.dot(
            hot,
            arrived[h].reshape(rows_n * tiles, chunk),
            preferred_element_type=jnp.float32,
        )
        height = rows_n * bands
        for pair in range(chunk // 128):
            lanes = slice(128 * pair, 128 * pair + 128)
            for q in range(per_row // 2):
                left = summed[2 * q * height : (2 * q + 1) * height, lanes]
                right = summed[(2 * q + 1) * height : (2 * q + 2) * height, lanes]
                upper = jnp.where(low_lanes[:height], left, pltpu.roll(right, tile_side, 1))
                lower = jnp.where(low_lanes[:height], pltpu.roll(left, tile_side, 1), right)
                out_lanes = slice(128 * q, 128 * q + 128)
                first = 2 * pair * height
                dense[h, 0, first : first + height, out_lanes] = upper.astype(jnp.bfloat16)
                dense[h, 0, first + height : first + 2 * height, out_lanes] = lower.astype(
                    jnp.bfloat16
                )
        group = [block_copy(h, 0, 2, 2), block_copy(h, 0, 1, 1)]
        for copy in group:
            copy.start()
        gathers.append(group)

    def forward_stage(h):
        gathers[h][0].wait_recv()
        copy = block_copy(h, 2, 1, 3)
        copy.start()
        gathers[h].append(copy)

    sends = []

    def section_stage(h):
        spectrum = None
        for d in range(cols_n):
            if d == 1:
                gathers[h][1].wait_recv()
            if d == 3:
                gathers[h][2].wait_recv()
            term = jnp.dot(
                dense[h, d],
                table[d * cols_dev : (d + 1) * cols_dev, :],
                preferred_element_type=jnp.float32,
            )
            spectrum = term if d == 0 else spectrum + term
        spectrum = spectrum.astype(jnp.bfloat16)
        stacked = jnp.concatenate([spectrum[:, :cols_dev], spectrum[:, cols_dev:]], 0)
        section_two = jnp.dot(
            mix[:, h * mix_side : (h + 1) * mix_side], stacked, preferred_element_type=jnp.float32
        )
        outgoing[h] = section_two.astype(jnp.bfloat16).reshape(outgoing.shape[1:])
        group = [
            pltpu.make_async_remote_copy(
                src_ref=outgoing.at[h, row_peers[d]],
                dst_ref=out_ref.at[h, me_row],
                send_sem=e_send.at[h, d],
                recv_sem=e_recv.at[h, d],
                device_id=(row_peers[d], me_col),
                device_id_type=MESH,
            )
            for d in range(1, rows_n)
        ]
        for copy in group:
            copy.start()
        own = pltpu.make_async_copy(
            outgoing.at[h, me_row], out_ref.at[h, me_row], local_sem.at[CHUNKS + 2 + h]
        )
        own.start()
        sends.append((group, own))

    for h in range(CHUNKS):
        density_stage(h)
        if h > 0:
            forward_stage(h - 1)
        if h > 1:
            section_stage(h - 2)
    forward_stage(CHUNKS - 1)
    for h in range(CHUNKS - 2, CHUNKS):
        section_stage(h)

    for copy in label_copies:
        copy.wait_send()
    for h in range(CHUNKS):
        for copy in band_copies[h] + gathers[h]:
            copy.wait_send()
    for h in range(CHUNKS):
        group, own = sends[h]
        own.wait()
        for d in range(1, rows_n):
            pltpu.make_async_remote_copy(
                src_ref=outgoing.at[h, row_peers[d]],
                dst_ref=out_ref.at[h, row_sources[d]],
                send_sem=e_send.at[h, d],
                recv_sem=e_recv.at[h, d],
                device_id=(row_peers[d], me_col),
                device_id_type=MESH,
            ).wait()


def final_kernel(final_ref, section_hbm, psf_ref, out_ref, section, sems):
    rows_dev = psf_ref.shape[0]
    depth = section.shape[0] // 2
    copies = []
    for h in range(2):
        rows = pl.ds(h * depth, depth)
        copies.append(
            pltpu.make_async_copy(section_hbm.at[rows, :], section.at[rows, :], sems.at[h])
        )
        copies[h].start()
    result = None
    for h in range(2):
        copies[h].wait()
        at = slice(h * depth, h * depth + depth)
        term = jnp.dot(final_ref[:, at], section[at, :], preferred_element_type=jnp.float32)
        result = term if h == 0 else result + term
    psf = psf_ref[...].astype(jnp.float32)
    out_ref[:, 0, :] = result[:rows_dev] * psf
    out_ref[:, 1, :] = result[rows_dev:] * psf


def on_device_kernels(tile_density, tile_dest, tile_place, psf_spectrum):
    tile_count, tile_side, _ = tile_density.shape
    rows_dev, cols_dev = psf_spectrum.shape
    rows_n = lax.axis_size("rows")
    cols_n = lax.axis_size("cols")
    bands, per_row = rows_dev // tile_side, cols_dev // tile_side
    step_rows = tile_side // rows_n // CHUNKS
    chunk = step_rows * tile_side
    tables, final = constants(rows_n, cols_n, tile_side, rows_dev, cols_dev)
    bf16 = jnp.bfloat16
    vmem = pl.BlockSpec(memory_space=pltpu.VMEM)
    anywhere = pl.BlockSpec(memory_space=pl.ANY)
    width = 2 * step_rows * bands
    mix_side = width * rows_n
    dma = pltpu.SemaphoreType.DMA
    section = pl.pallas_call(
        functools.partial(exchange_kernel, rows_n, cols_n, tile_side, bands, per_row),
        out_shape=jax.ShapeDtypeStruct((CHUNKS, rows_n, width, cols_dev), bf16),
        in_specs=[anywhere] * 4,
        out_specs=anywhere,
        scratch_shapes=[
            pltpu.VMEM((2, 1, tile_count), jnp.int32),
            pltpu.VMEM(tile_density.shape, bf16),
            pltpu.VMEM((tile_count * tile_side, 128), jnp.float32),
            pltpu.VMEM((CHUNKS, rows_n, tile_count, chunk), bf16),
            pltpu.VMEM((rows_n, 8, 128), jnp.int32),
            pltpu.VMEM((CHUNKS, rows_n, tile_count, chunk), bf16),
            pltpu.VMEM((CHUNKS, cols_n, step_rows * rows_n * bands, cols_dev), bf16),
            pltpu.VMEM((CHUNKS, rows_n, width, cols_dev), bf16),
            pltpu.VMEM((cols_n * cols_dev, 2 * cols_dev), bf16),
            pltpu.VMEM((mix_side, CHUNKS * mix_side), bf16),
            dma((rows_n,)),
            dma((rows_n,)),
            dma((CHUNKS, rows_n)),
            dma((CHUNKS, rows_n)),
            dma((CHUNKS, cols_n)),
            dma((CHUNKS, cols_n)),
            dma((CHUNKS, rows_n)),
            dma((CHUNKS, rows_n)),
            dma((2 * CHUNKS + 4,)),
            dma((1,)),
        ],
        compiler_params=pltpu.CompilerParams(
            collective_id=0, has_side_effects=True, vmem_limit_bytes=56 << 20
        ),
    )(
        tile_density,
        tile_dest.reshape(1, tile_count),
        tile_place.reshape(1, tile_count),
        tables,
    )
    return pl.pallas_call(
        final_kernel,
        out_shape=jax.ShapeDtypeStruct((rows_dev, 2, cols_dev), jnp.float32),
        in_specs=[vmem, anywhere, vmem],
        out_specs=vmem,
        scratch_shapes=[pltpu.VMEM((2 * rows_dev, cols_dev), bf16), dma((2,))],
        compiler_params=pltpu.CompilerParams(vmem_limit_bytes=53 << 20),
    )(final, section.reshape(2 * rows_dev, cols_dev), psf_spectrum)


def solution(mesh):
    in_specs = (
        P(("rows", "cols"), None, None),
        P(("rows", "cols"), None),
        P(("rows", "cols")),
        P("rows", "cols"),
    )
    out_specs = P("rows", None, "cols")

    def local(tile_density, tile_dest, tile_place, psf_spectrum):
        fast = fits(
            lax.axis_size("rows"),
            lax.axis_size("cols"),
            *tile_density.shape[:2],
            *psf_spectrum.shape,
        )
        run = on_device_kernels if fast else on_device
        return run(tile_density, tile_dest, tile_place, psf_spectrum)

    return jax.shard_map(
        local, mesh=mesh, in_specs=in_specs, out_specs=out_specs, check_vma=False
    )
```

```python
import functools
import math

import jax
import jax.numpy as jnp
import numpy as np
from jax import lax
from jax.experimental import pallas as pl
from jax.experimental.pallas import tpu as pltpu
from jax.sharding import PartitionSpec as P


def make_table(length, factor):
    positions = jnp.arange(length, dtype=jnp.int32)
    angles = (
        2.0
        * math.pi
        / length
        * (positions[:, None] * positions[None, :] % length).astype(jnp.float32)
    )
    cosine = jnp.cos(angles) * factor
    sine_part = jnp.sin(angles) * factor
    upper_rows = jnp.stack([cosine, -sine_part], 1)
    bottom = jnp.stack([sine_part, cosine], 1)
    return jnp.stack([upper_rows, bottom], 0).astype(jnp.bfloat16)


def twiddle(real_part, imag_part, position, frequency, period):
    angles = 2.0 * math.pi / period * (position * frequency % period).astype(jnp.float32)
    cosine = jnp.cos(angles)
    sine_part = jnp.sin(angles)
    return (real_part * cosine + imag_part * sine_part, imag_part * cosine - real_part * sine_part)


def on_device(tile_density, tile_dest, tile_place, psf_spectrum):
    tile_count, tile_side, _ = tile_density.shape
    rows_dev, cols_dev = psf_spectrum.shape
    rows_n = lax.axis_size("rows")
    cols_n = lax.axis_size("cols")
    capacity = max(2, 2 * tile_count // rows_n)
    slot_total = rows_n * capacity
    target = tile_dest[:, 0]
    matches = (target[:, None] == jnp.arange(rows_n, dtype=jnp.int32)[None, :]).astype(jnp.int32)
    order_within = jnp.sum((jnp.cumsum(matches, 0) - matches) * matches, 1)
    slot_index = target * capacity + order_within
    chosen = slot_index[:, None] == jnp.arange(slot_total, dtype=jnp.int32)[None, :]
    tiles_flat = tile_density.reshape(tile_count, tile_side * tile_side)
    outgoing = jnp.einsum(
        "ts,tc->sc", chosen.astype(jnp.bfloat16), tiles_flat, preferred_element_type=jnp.float32
    ).astype(jnp.bfloat16)
    labels = jnp.sum(jnp.where(chosen, (tile_place + 1)[:, None], 0), axis=0)
    arrived, arrived_marks = (
        lax.all_to_all(outgoing, "rows", split_axis=0, concat_axis=0, tiled=True),
        lax.all_to_all(labels, "rows", split_axis=0, concat_axis=0, tiled=True),
    )
    per_row = cols_dev // tile_side
    positions_count = rows_dev // tile_side * per_row
    placement_hot = (
        arrived_marks[:, None] - 1 == jnp.arange(positions_count, dtype=jnp.int32)[None, :]
    ).astype(jnp.bfloat16)
    cell_tiles = jnp.einsum(
        "sp,sc->pc", placement_hot, arrived, preferred_element_type=jnp.float32
    ).astype(jnp.bfloat16)
    density_grid = cell_tiles.reshape(
        rows_dev // tile_side, per_row, tile_side, tile_side
    ).transpose(0, 2, 1, 3)
    density_grid = density_grid.reshape(rows_dev, cols_dev)
    me_col = lax.axis_index("cols")
    highest = lax.Precision.HIGHEST
    slab_cols = cols_dev * cols_n
    part_cols = cols_dev // cols_n
    pieces = lax.all_to_all(density_grid[None], "cols", split_axis=2, concat_axis=0, tiled=True)
    frequency = jnp.arange(cols_n, dtype=jnp.int32)
    angles = (
        2.0
        * math.pi
        / cols_n
        * (frequency[:, None] * frequency[None, :] % cols_n).astype(jnp.float32)
    )
    values = pieces.astype(jnp.float32)
    sum_real = jnp.einsum("ejt,ek->kjt", values, jnp.cos(angles), precision=highest)
    sum_imag = -jnp.einsum("ejt,ek->kjt", values, jnp.sin(angles), precision=highest)
    columns = (me_col * part_cols + jnp.arange(part_cols, dtype=jnp.int32))[None, None, :]
    real_part, imag_part = twiddle(sum_real, sum_imag, columns, frequency[:, None, None], slab_cols)
    packed = jnp.stack([real_part, imag_part], 2).astype(jnp.bfloat16)
    returned = lax.all_to_all(packed, "cols", split_axis=0, concat_axis=3, tiled=True)
    section_one = returned.reshape(rows_dev, 2 * cols_dev)
    row_table = make_table(cols_dev, 1.0 / math.sqrt(slab_cols)).reshape(2 * cols_dev, 2 * cols_dev)
    rows_spectrum = jnp.dot(section_one, row_table, preferred_element_type=jnp.float32).astype(
        jnp.bfloat16
    )
    rows_spectrum = rows_spectrum.reshape(rows_dev, 2, cols_dev)
    me_row = lax.axis_index("rows")
    group_rows = rows_dev // rows_n
    grid_rows = rows_dev * rows_n
    col_table = make_table(rows_n, 1.0).transpose(3, 2, 1, 0)
    column_block = lax.all_to_all(rows_spectrum, "rows", split_axis=0, concat_axis=0, tiled=True)
    item_width = column_block.shape[2]
    values = column_block.reshape(rows_n, group_rows, 2, item_width)
    combined = jnp.einsum("kqap,atpc->ktqc", col_table, values, preferred_element_type=jnp.float32)
    row_index = (me_row * group_rows + jnp.arange(group_rows, dtype=jnp.int32))[None, :, None]
    row_freq = jnp.arange(rows_n, dtype=jnp.int32)[:, None, None]
    real_two, imag_two = twiddle(
        combined[:, :, 0], combined[:, :, 1], row_index, row_freq, grid_rows
    )
    section_two = lax.all_to_all(
        jnp.stack([real_two, imag_two], 2).astype(jnp.bfloat16).reshape(rows_dev, 2, item_width),
        "rows",
        split_axis=0,
        concat_axis=0,
        tiled=True,
    )
    final_table = (
        make_table(rows_dev, 1.0 / math.sqrt(grid_rows))
        .transpose(3, 2, 1, 0)
        .reshape(2 * rows_dev, 2 * rows_dev)
    )
    result_spec = jnp.dot(
        final_table, section_two.reshape(2 * rows_dev, cols_dev), preferred_element_type=jnp.float32
    )
    result_spec = result_spec.reshape(rows_dev, 2, cols_dev)
    return result_spec * psf_spectrum.astype(jnp.float32)[:, None, :]


CHUNKS = 4
MESH = pl.DeviceIdType.MESH


def fits(rows_n, cols_n, tile_count, tile_side, rows_dev, cols_dev):
    return (
        cols_n == 4
        and rows_n > 1
        and tile_side * 2 == 128
        and tile_side % (rows_n * 2 * CHUNKS) == 0
        and tile_count % 16 == 0
        and tile_count <= 128
        and cols_dev % 128 == 0
        and rows_dev % tile_side == 0
        and 2 * (tile_side // rows_n // CHUNKS) * (rows_dev // tile_side) % 16 == 0
        and 2 * tile_side * (rows_dev // tile_side) <= 2 * cols_dev
        and 2 * tile_side // CHUNKS * (rows_dev // tile_side) % 128 == 0
        and cols_n * cols_dev <= 2048
        and tile_side % (16 * CHUNKS) == 0
        and rows_n * rows_dev * cols_dev * 2 <= 1 << 22
    )


def constants(rows_n, cols_n, tile_side, rows_dev, cols_dev):
    slab_cols, grid_rows = cols_dev * cols_n, rows_dev * rows_n
    bands = rows_dev // tile_side
    step_rows = tile_side // rows_n // CHUNKS

    def parts(phase, factor):
        angles = 2.0 * np.pi * phase
        return np.cos(angles) * factor, -np.sin(angles) * factor

    bf16 = jnp.bfloat16
    k = np.arange(cols_n)
    sibling = k + 1 - 2 * (k % 2)
    held = np.stack([k, sibling, (k + 2) % cols_n, (sibling + 2) % cols_n], 1)
    column = (held[:, :, None] * cols_dev + np.arange(cols_dev)).reshape(cols_n, slab_cols, 1)
    frequency = k[:, None, None] + cols_n * np.arange(cols_dev)
    waves = np.stack(parts(np.arange(slab_cols) / slab_cols, 1.0 / math.sqrt(slab_cols)), 0)
    re, im = waves.astype(bf16)[:, column * frequency % slab_cols]
    row_tables = np.concatenate([re, im], 2)
    b = (
        tile_side * np.arange(bands)[None, None, None, :]
        + step_rows * np.arange(rows_n)[:, None, None, None]
        + step_rows * rows_n * np.arange(CHUNKS)[None, :, None, None]
        + np.arange(step_rows)[None, None, :, None]
    )
    u = np.arange(rows_n)
    row = b[:, :, None, None] + rows_dev * u[None, None, None, :, None, None]
    re, im = parts((row * u[None, None, :, None, None, None] % grid_rows) / grid_rows, 1.0)
    width = step_rows * bands
    mix = np.zeros((rows_n, CHUNKS, rows_n, 2, step_rows, bands, 2, step_rows, rows_n, bands), np.float32)
    for i in range(step_rows):
        for t in range(bands):
            mix[:, :, :, 0, i, t, 0, i, :, t] = re[:, :, :, :, i, t]
            mix[:, :, :, 0, i, t, 1, i, :, t] = -im[:, :, :, :, i, t]
            mix[:, :, :, 1, i, t, 0, i, :, t] = im[:, :, :, :, i, t]
            mix[:, :, :, 1, i, t, 1, i, :, t] = re[:, :, :, :, i, t]
    mix = mix.reshape(rows_n, CHUNKS, rows_n * 2 * width, 2 * rows_n * width)
    w = np.arange(rows_dev)
    order = b.transpose(1, 0, 2, 3).reshape(CHUNKS, rows_n, 1, width)
    re, im = parts(
        (w[:, None, None, None, None] * order % rows_dev) / rows_dev, 1.0 / math.sqrt(grid_rows)
    )
    final = np.stack(
        [np.concatenate([re, -im], 3), np.concatenate([im, re], 3)], 0
    ).reshape(2 * rows_dev, 2 * rows_dev)
    side = mix.shape[-1]
    mix = mix.transpose(0, 2, 1, 3).reshape(rows_n * side, CHUNKS * side)
    mix = np.pad(mix, ((0, 0), (0, 2 * cols_dev - CHUNKS * side)))
    tables = np.concatenate([row_tables.reshape(-1, 2 * cols_dev), mix.astype(bf16)], 0)
    return jnp.asarray(tables), jnp.asarray(final.astype(bf16))


def exchange_kernel(
    rows_n, cols_n, tile_side, bands, per_row,
    tiles_hbm, dest_hbm, place_hbm, tables_hbm,
    out_ref,
    owned, raw, wide, banded, labels, arrived, dense, outgoing, table, mix,
    label_send, label_recv, a_send, a_recv, g_send, g_recv, e_send, e_recv, local_sem, table_sem, raw_sem,
):
    me_row, me_col = lax.axis_index("rows"), lax.axis_index("cols")
    tiles = tiles_hbm.shape[0]
    chunk = arrived.shape[3]
    cols_dev = per_row * tile_side
    row_peers = [lax.rem(me_row + d, rows_n) for d in range(rows_n)]
    row_sources = [lax.rem(me_row + rows_n - d, rows_n) for d in range(rows_n)]
    far_first = sorted(range(1, rows_n), key=lambda d: abs(2 * d - rows_n))
    sibling = me_col + 1 - 2 * lax.rem(me_col, 2)
    col_blocks = [me_col, sibling, lax.rem(me_col + 2, cols_n), lax.rem(sibling + 2, cols_n)]

    barrier = pltpu.get_barrier_semaphore()
    for d in range(1, rows_n):
        pl.semaphore_signal(barrier, inc=1, device_id=(row_peers[d], me_col), device_id_type=MESH)
    for d in range(1, 3):
        pl.semaphore_signal(barrier, inc=1, device_id=(me_row, col_blocks[d]), device_id_type=MESH)

    group_rows = tile_side // CHUNKS
    raw_copies = []
    for h in range(CHUNKS):
        rows = pl.ds(h * group_rows, group_rows)
        raw_copies.append(
            pltpu.make_async_copy(tiles_hbm.at[:, rows, :], raw.at[h], raw_sem.at[h])
        )
        raw_copies[h].start()
    owned_copies = [
        pltpu.make_async_copy(dest_hbm, owned.at[0], local_sem.at[2 * CHUNKS + 2]),
        pltpu.make_async_copy(place_hbm, owned.at[1], local_sem.at[2 * CHUNKS + 3]),
    ]
    table_rows = table.shape[0]
    table_start = pl.multiple_of(me_col * table_rows, 16)
    table_copies = [
        pltpu.make_async_copy(
            tables_hbm.at[pl.ds(table_start, table_rows), :], table, table_sem.at[0]
        )
    ]
    mix_start = table_rows * cols_n + me_row * mix.shape[0]
    mix_copy = pltpu.make_async_copy(
        tables_hbm.at[pl.ds(pl.multiple_of(mix_start, 16), mix.shape[0]), pl.ds(0, mix.shape[1])],
        mix,
        local_sem.at[CHUNKS],
    )
    for copy in owned_copies + table_copies + [mix_copy]:
        copy.start()
    for copy in owned_copies:
        copy.wait()
    slab, place = owned[0], owned[1]
    code = (place % per_row) * (rows_n * bands) + slab * bands + place // per_row
    labels[0] = jnp.broadcast_to(
        jnp.concatenate([code, jnp.zeros((1, 128 - tiles), jnp.int32)], 1)
        if tiles < 128
        else code,
        labels.shape[1:],
    )
    low_lanes = lax.broadcasted_iota(jnp.int32, (max(tiles, rows_n * bands), 128), 1) < tile_side
    own_copies = [
        pltpu.make_async_copy(banded.at[h, me_row], arrived.at[h, 0], local_sem.at[h])
        for h in range(CHUNKS)
    ]

    def band_stage(h):
        raw_copies[h].wait()
        wide[h, :, 0:tile_side] = (
            raw[h].reshape(tiles * group_rows, tile_side).astype(jnp.float32)
        )
        for owner in range(rows_n):
            for pair in range(chunk // 128):
                row = owner * (chunk // tile_side) + 2 * pair
                first = wide[h, pl.ds(row, tiles, stride=group_rows), :]
                second = wide[h, pl.ds(row + 1, tiles, stride=group_rows), :]
                both = jnp.where(low_lanes[:tiles], first, pltpu.roll(second, tile_side, 1))
                banded[h, owner, :, 128 * pair : 128 * pair + 128] = both.astype(jnp.bfloat16)
        own_copies[h].start()

    band_stage(0)
    pl.semaphore_wait(barrier, rows_n + 1)

    def band_copy(h, d):
        return pltpu.make_async_remote_copy(
            src_ref=banded.at[h, row_peers[d]],
            dst_ref=arrived.at[h, d],
            send_sem=a_send.at[h, d],
            recv_sem=a_recv.at[h, d],
            device_id=(row_peers[d], me_col),
            device_id_type=MESH,
        )

    label_copies = [
        pltpu.make_async_remote_copy(
            src_ref=labels.at[0],
            dst_ref=labels.at[d],
            send_sem=label_send.at[d],
            recv_sem=label_recv.at[d],
            device_id=(row_peers[d], me_col),
            device_id_type=MESH,
        )
        for d in range(1, rows_n)
    ]
    band_copies = [[band_copy(h, d) for d in far_first] for h in range(CHUNKS)]
    for copy in label_copies:
        copy.start()
    def band_start(h):
        for copy in band_copies[h]:
            copy.start()

    band_start(0)
    for h in range(1, CHUNKS):
        band_stage(h)
    band_start(1)

    for copy in label_copies:
        copy.wait_recv()
    codes = jnp.concatenate([labels[d, 0:1, 0:tiles] for d in range(rows_n)], 1)
    cells = per_row * rows_n * bands
    hot = jnp.where(
        lax.broadcasted_iota(jnp.int32, (cells, rows_n * tiles), 0) == codes, 1.0, 0.0
    ).astype(jnp.bfloat16)

    for copy in table_copies + [mix_copy]:
        copy.wait()
    mix_side = mix.shape[0]

    gathers = []

    def block_copy(h, source, peer, slot):
        return pltpu.make_async_remote_copy(
            src_ref=dense.at[h, source],
            dst_ref=dense.at[h, slot],
            send_sem=g_send.at[h, slot],
            recv_sem=g_recv.at[h, slot],
            device_id=(me_row, col_blocks[peer]),
            device_id_type=MESH,
        )

    def density_stage(h):
        own_copies[h].wait()
        for copy in band_copies[h]:
            copy.wait_recv()
        if h + 2 < CHUNKS:
            band_start(h + 2)
        summed = jnp.dot(
            hot,
            arrived[h].reshape(rows_n * tiles, chunk),
            preferred_element_type=jnp.float32,
        )
        height = rows_n * bands
        for pair in range(chunk // 128):
            lanes = slice(128 * pair, 128 * pair + 128)
            for q in range(per_row // 2):
                left = summed[2 * q * height : (2 * q + 1) * height, lanes]
                right = summed[(2 * q + 1) * height : (2 * q + 2) * height, lanes]
                upper = jnp.where(low_lanes[:height], left, pltpu.roll(right, tile_side, 1))
                lower = jnp.where(low_lanes[:height], pltpu.roll(left, tile_side, 1), right)
                out_lanes = slice(128 * q, 128 * q + 128)
                first = 2 * pair * height
                dense[h, 0, first : first + height, out_lanes] = upper.astype(jnp.bfloat16)
                dense[h, 0, first + height : first + 2 * height, out_lanes] = lower.astype(
                    jnp.bfloat16
                )
        group = [block_copy(h, 0, 2, 2), block_copy(h, 0, 1, 1)]
        for copy in group:
            copy.start()
        gathers.append(group)

    def forward_stage(h):
        gathers[h][0].wait_recv()
        copy = block_copy(h, 2, 1, 3)
        copy.start()
        gathers[h].append(copy)

    sends = []

    def section_stage(h):
        spectrum = None
        for d in range(cols_n):
            if d == 1:
                gathers[h][1].wait_recv()
            if d == 3:
                gathers[h][2].wait_recv()
            term = jnp.dot(
                dense[h, d],
                table[d * cols_dev : (d + 1) * cols_dev, :],
                preferred_element_type=jnp.float32,
            )
            spectrum = term if d == 0 else spectrum + term
        spectrum = spectrum.astype(jnp.bfloat16)
        stacked = jnp.concatenate([spectrum[:, :cols_dev], spectrum[:, cols_dev:]], 0)
        section_two = jnp.dot(
            mix[:, h * mix_side : (h + 1) * mix_side], stacked, preferred_element_type=jnp.float32
        )
        outgoing[h] = section_two.astype(jnp.bfloat16).reshape(outgoing.shape[1:])
        group = [
            pltpu.make_async_remote_copy(
                src_ref=outgoing.at[h, row_peers[d]],
                dst_ref=out_ref.at[h, me_row],
                send_sem=e_send.at[h, d],
                recv_sem=e_recv.at[h, d],
                device_id=(row_peers[d], me_col),
                device_id_type=MESH,
            )
            for d in far_first
        ]
        for copy in group:
            copy.start()
        own = pltpu.make_async_copy(
            outgoing.at[h, me_row], out_ref.at[h, me_row], local_sem.at[CHUNKS + 2 + h]
        )
        own.start()
        sends.append((group, own))

    for h in range(CHUNKS):
        density_stage(h)
        if h > 0:
            forward_stage(h - 1)
        if h > 1:
            section_stage(h - 2)
    forward_stage(CHUNKS - 1)
    for h in range(CHUNKS - 2, CHUNKS):
        section_stage(h)

    for copy in label_copies:
        copy.wait_send()
    for h in range(CHUNKS):
        for copy in band_copies[h] + gathers[h]:
            copy.wait_send()
    for h in range(CHUNKS):
        group, own = sends[h]
        own.wait()
        for d in range(1, rows_n):
            pltpu.make_async_remote_copy(
                src_ref=outgoing.at[h, row_peers[d]],
                dst_ref=out_ref.at[h, row_sources[d]],
                send_sem=e_send.at[h, d],
                recv_sem=e_recv.at[h, d],
                device_id=(row_peers[d], me_col),
                device_id_type=MESH,
            ).wait()


def final_kernel(final_ref, section_hbm, psf_ref, out_ref, section, sems):
    rows_dev = psf_ref.shape[0]
    depth = section.shape[0] // 2
    copies = []
    for h in range(2):
        rows = pl.ds(h * depth, depth)
        copies.append(
            pltpu.make_async_copy(section_hbm.at[rows, :], section.at[rows, :], sems.at[h])
        )
        copies[h].start()
    result = None
    for h in range(2):
        copies[h].wait()
        at = slice(h * depth, h * depth + depth)
        term = jnp.dot(final_ref[:, at], section[at, :], preferred_element_type=jnp.float32)
        result = term if h == 0 else result + term
    psf = psf_ref[...].astype(jnp.float32)
    out_ref[:, 0, :] = result[:rows_dev] * psf
    out_ref[:, 1, :] = result[rows_dev:] * psf


def on_device_kernels(tile_density, tile_dest, tile_place, psf_spectrum):
    tile_count, tile_side, _ = tile_density.shape
    rows_dev, cols_dev = psf_spectrum.shape
    rows_n = lax.axis_size("rows")
    cols_n = lax.axis_size("cols")
    bands, per_row = rows_dev // tile_side, cols_dev // tile_side
    step_rows = tile_side // rows_n // CHUNKS
    chunk = step_rows * tile_side
    tables, final = constants(rows_n, cols_n, tile_side, rows_dev, cols_dev)
    bf16 = jnp.bfloat16
    vmem = pl.BlockSpec(memory_space=pltpu.VMEM)
    anywhere = pl.BlockSpec(memory_space=pl.ANY)
    width = 2 * step_rows * bands
    mix_side = width * rows_n
    dma = pltpu.SemaphoreType.DMA
    section = pl.pallas_call(
        functools.partial(exchange_kernel, rows_n, cols_n, tile_side, bands, per_row),
        out_shape=jax.ShapeDtypeStruct((CHUNKS, rows_n, width, cols_dev), bf16),
        in_specs=[anywhere] * 4,
        out_specs=anywhere,
        scratch_shapes=[
            pltpu.VMEM((2, 1, tile_count), jnp.int32),
            pltpu.VMEM((CHUNKS, tile_count, tile_side // CHUNKS, tile_side), bf16),
            pltpu.VMEM((CHUNKS, tile_count * tile_side // CHUNKS, 128), jnp.float32),
            pltpu.VMEM((CHUNKS, rows_n, tile_count, chunk), bf16),
            pltpu.VMEM((rows_n, 8, 128), jnp.int32),
            pltpu.VMEM((CHUNKS, rows_n, tile_count, chunk), bf16),
            pltpu.VMEM((CHUNKS, cols_n, step_rows * rows_n * bands, cols_dev), bf16),
            pltpu.VMEM((CHUNKS, rows_n, width, cols_dev), bf16),
            pltpu.VMEM((cols_n * cols_dev, 2 * cols_dev), bf16),
            pltpu.VMEM((mix_side, CHUNKS * mix_side), bf16),
            dma((rows_n,)),
            dma((rows_n,)),
            dma((CHUNKS, rows_n)),
            dma((CHUNKS, rows_n)),
            dma((CHUNKS, cols_n)),
            dma((CHUNKS, cols_n)),
            dma((CHUNKS, rows_n)),
            dma((CHUNKS, rows_n)),
            dma((2 * CHUNKS + 4,)),
            dma((1,)),
            dma((CHUNKS,)),
        ],
        compiler_params=pltpu.CompilerParams(
            collective_id=0, has_side_effects=True, vmem_limit_bytes=56 << 20
        ),
    )(
        tile_density,
        tile_dest.reshape(1, tile_count),
        tile_place.reshape(1, tile_count),
        tables,
    )
    return pl.pallas_call(
        final_kernel,
        out_shape=jax.ShapeDtypeStruct((rows_dev, 2, cols_dev), jnp.float32),
        in_specs=[vmem, anywhere, vmem],
        out_specs=vmem,
        scratch_shapes=[pltpu.VMEM((2 * rows_dev, cols_dev), bf16), dma((2,))],
        compiler_params=pltpu.CompilerParams(vmem_limit_bytes=53 << 20),
    )(final, section.reshape(2 * rows_dev, cols_dev), psf_spectrum)


def solution(mesh):
    in_specs = (
        P(("rows", "cols"), None, None),
        P(("rows", "cols"), None),
        P(("rows", "cols")),
        P("rows", "cols"),
    )
    out_specs = P("rows", None, "cols")

    def local(tile_density, tile_dest, tile_place, psf_spectrum):
        fast = fits(
            lax.axis_size("rows"),
            lax.axis_size("cols"),
            *tile_density.shape[:2],
            *psf_spectrum.shape,
        )
        run = on_device_kernels if fast else on_device
        return run(tile_density, tile_dest, tile_place, psf_spectrum)

    return jax.shard_map(
        local, mesh=mesh, in_specs=in_specs, out_specs=out_specs, check_vma=False
    )
```

```python
import functools
import math

import jax
import jax.numpy as jnp
import numpy as np
from jax import lax
from jax.experimental import pallas as pl
from jax.experimental.pallas import tpu as pltpu
from jax.sharding import PartitionSpec as P


def make_table(length, factor):
    positions = jnp.arange(length, dtype=jnp.int32)
    angles = (
        2.0
        * math.pi
        / length
        * (positions[:, None] * positions[None, :] % length).astype(jnp.float32)
    )
    cosine = jnp.cos(angles) * factor
    sine_part = jnp.sin(angles) * factor
    upper_rows = jnp.stack([cosine, -sine_part], 1)
    bottom = jnp.stack([sine_part, cosine], 1)
    return jnp.stack([upper_rows, bottom], 0).astype(jnp.bfloat16)


def twiddle(real_part, imag_part, position, frequency, period):
    angles = 2.0 * math.pi / period * (position * frequency % period).astype(jnp.float32)
    cosine = jnp.cos(angles)
    sine_part = jnp.sin(angles)
    return (real_part * cosine + imag_part * sine_part, imag_part * cosine - real_part * sine_part)


def on_device(tile_density, tile_dest, tile_place, psf_spectrum):
    tile_count, tile_side, _ = tile_density.shape
    rows_dev, cols_dev = psf_spectrum.shape
    rows_n = lax.axis_size("rows")
    cols_n = lax.axis_size("cols")
    capacity = max(2, 2 * tile_count // rows_n)
    slot_total = rows_n * capacity
    target = tile_dest[:, 0]
    matches = (target[:, None] == jnp.arange(rows_n, dtype=jnp.int32)[None, :]).astype(jnp.int32)
    order_within = jnp.sum((jnp.cumsum(matches, 0) - matches) * matches, 1)
    slot_index = target * capacity + order_within
    chosen = slot_index[:, None] == jnp.arange(slot_total, dtype=jnp.int32)[None, :]
    tiles_flat = tile_density.reshape(tile_count, tile_side * tile_side)
    outgoing = jnp.einsum(
        "ts,tc->sc", chosen.astype(jnp.bfloat16), tiles_flat, preferred_element_type=jnp.float32
    ).astype(jnp.bfloat16)
    labels = jnp.sum(jnp.where(chosen, (tile_place + 1)[:, None], 0), axis=0)
    arrived, arrived_marks = (
        lax.all_to_all(outgoing, "rows", split_axis=0, concat_axis=0, tiled=True),
        lax.all_to_all(labels, "rows", split_axis=0, concat_axis=0, tiled=True),
    )
    per_row = cols_dev // tile_side
    positions_count = rows_dev // tile_side * per_row
    placement_hot = (
        arrived_marks[:, None] - 1 == jnp.arange(positions_count, dtype=jnp.int32)[None, :]
    ).astype(jnp.bfloat16)
    cell_tiles = jnp.einsum(
        "sp,sc->pc", placement_hot, arrived, preferred_element_type=jnp.float32
    ).astype(jnp.bfloat16)
    density_grid = cell_tiles.reshape(
        rows_dev // tile_side, per_row, tile_side, tile_side
    ).transpose(0, 2, 1, 3)
    density_grid = density_grid.reshape(rows_dev, cols_dev)
    me_col = lax.axis_index("cols")
    highest = lax.Precision.HIGHEST
    slab_cols = cols_dev * cols_n
    part_cols = cols_dev // cols_n
    pieces = lax.all_to_all(density_grid[None], "cols", split_axis=2, concat_axis=0, tiled=True)
    frequency = jnp.arange(cols_n, dtype=jnp.int32)
    angles = (
        2.0
        * math.pi
        / cols_n
        * (frequency[:, None] * frequency[None, :] % cols_n).astype(jnp.float32)
    )
    values = pieces.astype(jnp.float32)
    sum_real = jnp.einsum("ejt,ek->kjt", values, jnp.cos(angles), precision=highest)
    sum_imag = -jnp.einsum("ejt,ek->kjt", values, jnp.sin(angles), precision=highest)
    columns = (me_col * part_cols + jnp.arange(part_cols, dtype=jnp.int32))[None, None, :]
    real_part, imag_part = twiddle(sum_real, sum_imag, columns, frequency[:, None, None], slab_cols)
    packed = jnp.stack([real_part, imag_part], 2).astype(jnp.bfloat16)
    returned = lax.all_to_all(packed, "cols", split_axis=0, concat_axis=3, tiled=True)
    section_one = returned.reshape(rows_dev, 2 * cols_dev)
    row_table = make_table(cols_dev, 1.0 / math.sqrt(slab_cols)).reshape(2 * cols_dev, 2 * cols_dev)
    rows_spectrum = jnp.dot(section_one, row_table, preferred_element_type=jnp.float32).astype(
        jnp.bfloat16
    )
    rows_spectrum = rows_spectrum.reshape(rows_dev, 2, cols_dev)
    me_row = lax.axis_index("rows")
    group_rows = rows_dev // rows_n
    grid_rows = rows_dev * rows_n
    col_table = make_table(rows_n, 1.0).transpose(3, 2, 1, 0)
    column_block = lax.all_to_all(rows_spectrum, "rows", split_axis=0, concat_axis=0, tiled=True)
    item_width = column_block.shape[2]
    values = column_block.reshape(rows_n, group_rows, 2, item_width)
    combined = jnp.einsum("kqap,atpc->ktqc", col_table, values, preferred_element_type=jnp.float32)
    row_index = (me_row * group_rows + jnp.arange(group_rows, dtype=jnp.int32))[None, :, None]
    row_freq = jnp.arange(rows_n, dtype=jnp.int32)[:, None, None]
    real_two, imag_two = twiddle(
        combined[:, :, 0], combined[:, :, 1], row_index, row_freq, grid_rows
    )
    section_two = lax.all_to_all(
        jnp.stack([real_two, imag_two], 2).astype(jnp.bfloat16).reshape(rows_dev, 2, item_width),
        "rows",
        split_axis=0,
        concat_axis=0,
        tiled=True,
    )
    final_table = (
        make_table(rows_dev, 1.0 / math.sqrt(grid_rows))
        .transpose(3, 2, 1, 0)
        .reshape(2 * rows_dev, 2 * rows_dev)
    )
    result_spec = jnp.dot(
        final_table, section_two.reshape(2 * rows_dev, cols_dev), preferred_element_type=jnp.float32
    )
    result_spec = result_spec.reshape(rows_dev, 2, cols_dev)
    return result_spec * psf_spectrum.astype(jnp.float32)[:, None, :]


CHUNKS = 4
MESH = pl.DeviceIdType.MESH


def fits(rows_n, cols_n, tile_count, tile_side, rows_dev, cols_dev):
    return (
        cols_n == 4
        and rows_n > 1
        and tile_side * 2 == 128
        and tile_side % (rows_n * 2 * CHUNKS) == 0
        and tile_count % 16 == 0
        and tile_count <= 128
        and cols_dev % 128 == 0
        and rows_dev % tile_side == 0
        and 2 * (tile_side // rows_n // CHUNKS) * (rows_dev // tile_side) % 16 == 0
        and 2 * tile_side * (rows_dev // tile_side) <= 2 * cols_dev
        and 2 * tile_side // CHUNKS * (rows_dev // tile_side) % 128 == 0
        and cols_n * cols_dev <= 2048
        and tile_side % (16 * CHUNKS) == 0
        and rows_n * rows_dev * cols_dev * 2 <= 1 << 22
    )


def constants(rows_n, cols_n, tile_side, rows_dev, cols_dev):
    slab_cols, grid_rows = cols_dev * cols_n, rows_dev * rows_n
    bands = rows_dev // tile_side
    step_rows = tile_side // rows_n // CHUNKS

    def parts(phase, factor):
        angles = 2.0 * np.pi * phase
        return np.cos(angles) * factor, -np.sin(angles) * factor

    bf16 = jnp.bfloat16
    k = np.arange(cols_n)
    sibling = k + 1 - 2 * (k % 2)
    held = np.stack([k, sibling, (k + 2) % cols_n, (sibling + 2) % cols_n], 1)
    column = (held[:, :, None] * cols_dev + np.arange(cols_dev)).reshape(cols_n, slab_cols, 1)
    frequency = k[:, None, None] + cols_n * np.arange(cols_dev)
    waves = np.stack(parts(np.arange(slab_cols) / slab_cols, 1.0 / math.sqrt(slab_cols)), 0)
    re, im = waves.astype(bf16)[:, column * frequency % slab_cols]
    row_tables = np.concatenate([re, im], 2)
    b = (
        tile_side * np.arange(bands)[None, None, None, :]
        + step_rows * np.arange(rows_n)[:, None, None, None]
        + step_rows * rows_n * np.arange(CHUNKS)[None, :, None, None]
        + np.arange(step_rows)[None, None, :, None]
    )
    u = np.arange(rows_n)
    row = b[:, :, None, None] + rows_dev * u[None, None, None, :, None, None]
    re, im = parts((row * u[None, None, :, None, None, None] % grid_rows) / grid_rows, 1.0)
    width = step_rows * bands
    mix = np.zeros((rows_n, CHUNKS, rows_n, 2, step_rows, bands, 2, step_rows, rows_n, bands), np.float32)
    for i in range(step_rows):
        for t in range(bands):
            mix[:, :, :, 0, i, t, 0, i, :, t] = re[:, :, :, :, i, t]
            mix[:, :, :, 0, i, t, 1, i, :, t] = -im[:, :, :, :, i, t]
            mix[:, :, :, 1, i, t, 0, i, :, t] = im[:, :, :, :, i, t]
            mix[:, :, :, 1, i, t, 1, i, :, t] = re[:, :, :, :, i, t]
    mix = mix.reshape(rows_n, CHUNKS, rows_n * 2 * width, 2 * rows_n * width)
    w = np.arange(rows_dev)
    order = b.transpose(1, 0, 2, 3).reshape(CHUNKS, rows_n, 1, width)
    re, im = parts(
        (w[:, None, None, None, None] * order % rows_dev) / rows_dev, 1.0 / math.sqrt(grid_rows)
    )
    final = np.stack(
        [np.concatenate([re, -im], 3), np.concatenate([im, re], 3)], 0
    ).reshape(2 * rows_dev, 2 * rows_dev)
    side = mix.shape[-1]
    mix = mix.transpose(0, 2, 1, 3).reshape(rows_n * side, CHUNKS * side)
    mix = np.pad(mix, ((0, 0), (0, 2 * cols_dev - CHUNKS * side)))
    tables = np.concatenate([row_tables.reshape(-1, 2 * cols_dev), mix.astype(bf16)], 0)
    return jnp.asarray(tables), jnp.asarray(final.astype(bf16))


def exchange_kernel(
    rows_n, cols_n, tile_side, bands, per_row,
    tiles_hbm, dest_hbm, place_hbm, tables_hbm,
    out_ref,
    owned, raw, wide, banded, labels, arrived, dense, outgoing, table, mix,
    label_send, label_recv, a_send, a_recv, g_send, g_recv, e_send, e_recv, local_sem, table_sem, raw_sem,
):
    me_row, me_col = lax.axis_index("rows"), lax.axis_index("cols")
    tiles = tiles_hbm.shape[0]
    chunk = arrived.shape[3]
    cols_dev = per_row * tile_side
    row_peers = [lax.rem(me_row + d, rows_n) for d in range(rows_n)]
    row_sources = [lax.rem(me_row + rows_n - d, rows_n) for d in range(rows_n)]
    far_first = sorted(range(1, rows_n), key=lambda d: abs(2 * d - rows_n))
    sibling = me_col + 1 - 2 * lax.rem(me_col, 2)
    col_blocks = [me_col, sibling, lax.rem(me_col + 2, cols_n), lax.rem(sibling + 2, cols_n)]

    barrier = pltpu.get_barrier_semaphore()
    for d in range(1, rows_n):
        pl.semaphore_signal(barrier, inc=1, device_id=(row_peers[d], me_col), device_id_type=MESH)
    for d in range(1, 3):
        pl.semaphore_signal(barrier, inc=1, device_id=(me_row, col_blocks[d]), device_id_type=MESH)

    group_rows = tile_side // CHUNKS
    raw_copies = []
    for h in range(CHUNKS):
        rows = pl.ds(h * group_rows, group_rows)
        raw_copies.append(
            pltpu.make_async_copy(tiles_hbm.at[:, rows, :], raw.at[h], raw_sem.at[h])
        )
        raw_copies[h].start()
    owned_copies = [
        pltpu.make_async_copy(dest_hbm, owned.at[0], local_sem.at[2 * CHUNKS + 2]),
        pltpu.make_async_copy(place_hbm, owned.at[1], local_sem.at[2 * CHUNKS + 3]),
    ]
    table_rows = table.shape[0]
    table_start = pl.multiple_of(me_col * table_rows, 16)
    table_copies = [
        pltpu.make_async_copy(
            tables_hbm.at[pl.ds(table_start, table_rows), :], table, table_sem.at[0]
        )
    ]
    mix_start = table_rows * cols_n + me_row * mix.shape[0]
    mix_copy = pltpu.make_async_copy(
        tables_hbm.at[pl.ds(pl.multiple_of(mix_start, 16), mix.shape[0]), pl.ds(0, mix.shape[1])],
        mix,
        local_sem.at[CHUNKS],
    )
    for copy in owned_copies + table_copies + [mix_copy]:
        copy.start()
    for copy in owned_copies:
        copy.wait()
    slab, place = owned[0], owned[1]
    code = (place % per_row) * (rows_n * bands) + slab * bands + place // per_row
    labels[0] = jnp.broadcast_to(
        jnp.concatenate([code, jnp.zeros((1, 128 - tiles), jnp.int32)], 1)
        if tiles < 128
        else code,
        labels.shape[1:],
    )
    low_lanes = lax.broadcasted_iota(jnp.int32, (max(tiles, rows_n * bands), 128), 1) < tile_side
    own_copies = [
        pltpu.make_async_copy(banded.at[h, me_row], arrived.at[h, 0], local_sem.at[h])
        for h in range(CHUNKS)
    ]

    def band_stage(h):
        raw_copies[h].wait()
        wide[h, :, 0:tile_side] = (
            raw[h].reshape(tiles * group_rows, tile_side).astype(jnp.float32)
        )
        for owner in range(rows_n):
            for pair in range(chunk // 128):
                row = owner * (chunk // tile_side) + 2 * pair
                first = wide[h, pl.ds(row, tiles, stride=group_rows), :]
                second = wide[h, pl.ds(row + 1, tiles, stride=group_rows), :]
                both = jnp.where(low_lanes[:tiles], first, pltpu.roll(second, tile_side, 1))
                banded[h, owner, :, 128 * pair : 128 * pair + 128] = both.astype(jnp.bfloat16)
        own_copies[h].start()

    band_stage(0)
    pl.semaphore_wait(barrier, rows_n + 1)

    def band_copy(h, d):
        return pltpu.make_async_remote_copy(
            src_ref=banded.at[h, row_peers[d]],
            dst_ref=arrived.at[h, d],
            send_sem=a_send.at[h, d],
            recv_sem=a_recv.at[h, d],
            device_id=(row_peers[d], me_col),
            device_id_type=MESH,
        )

    label_copies = [
        pltpu.make_async_remote_copy(
            src_ref=labels.at[0],
            dst_ref=labels.at[d],
            send_sem=label_send.at[d],
            recv_sem=label_recv.at[d],
            device_id=(row_peers[d], me_col),
            device_id_type=MESH,
        )
        for d in range(1, rows_n)
    ]
    band_copies = [[band_copy(h, d) for d in far_first] for h in range(CHUNKS)]
    for copy in label_copies:
        copy.start()
    def band_start(h):
        for copy in band_copies[h]:
            copy.start()

    band_start(0)
    for h in range(1, CHUNKS):
        band_stage(h)
    band_start(1)

    for copy in label_copies:
        copy.wait_recv()
    codes = jnp.concatenate([labels[d, 0:1, 0:tiles] for d in range(rows_n)], 1)
    cells = per_row * rows_n * bands
    hot = jnp.where(
        lax.broadcasted_iota(jnp.int32, (cells, rows_n * tiles), 0) == codes, 1.0, 0.0
    ).astype(jnp.bfloat16)

    for copy in table_copies + [mix_copy]:
        copy.wait()
    mix_side = mix.shape[0]

    gathers = []

    def block_copy(h, source, peer, slot):
        return pltpu.make_async_remote_copy(
            src_ref=dense.at[h, source],
            dst_ref=dense.at[h, slot],
            send_sem=g_send.at[h, slot],
            recv_sem=g_recv.at[h, slot],
            device_id=(me_row, col_blocks[peer]),
            device_id_type=MESH,
        )

    def density_stage(h):
        own_copies[h].wait()
        for copy in band_copies[h]:
            copy.wait_recv()
        if h + 2 < CHUNKS:
            band_start(h + 2)
        summed = jnp.dot(
            hot,
            arrived[h].reshape(rows_n * tiles, chunk),
            preferred_element_type=jnp.float32,
        )
        height = rows_n * bands
        for pair in range(chunk // 128):
            lanes = slice(128 * pair, 128 * pair + 128)
            for q in range(per_row // 2):
                left = summed[2 * q * height : (2 * q + 1) * height, lanes]
                right = summed[(2 * q + 1) * height : (2 * q + 2) * height, lanes]
                upper = jnp.where(low_lanes[:height], left, pltpu.roll(right, tile_side, 1))
                lower = jnp.where(low_lanes[:height], pltpu.roll(left, tile_side, 1), right)
                out_lanes = slice(128 * q, 128 * q + 128)
                first = 2 * pair * height
                dense[h, 0, first : first + height, out_lanes] = upper.astype(jnp.bfloat16)
                dense[h, 0, first + height : first + 2 * height, out_lanes] = lower.astype(
                    jnp.bfloat16
                )
        group = [block_copy(h, 0, 2, 2), block_copy(h, 0, 1, 1)]
        for copy in group:
            copy.start()
        gathers.append(group)

    def forward_stage(h):
        gathers[h][0].wait_recv()
        copy = block_copy(h, 2, 1, 3)
        copy.start()
        gathers[h].append(copy)

    sends = []

    def section_stage(h):
        spectrum = None
        for d in range(cols_n):
            if d == 1:
                gathers[h][1].wait_recv()
            if d == 3:
                gathers[h][2].wait_recv()
            term = jnp.dot(
                dense[h, d],
                table[d * cols_dev : (d + 1) * cols_dev, :],
                preferred_element_type=jnp.float32,
            )
            spectrum = term if d == 0 else spectrum + term
        spectrum = spectrum.astype(jnp.bfloat16)
        stacked = jnp.concatenate([spectrum[:, :cols_dev], spectrum[:, cols_dev:]], 0)
        section_two = jnp.dot(
            mix[:, h * mix_side : (h + 1) * mix_side], stacked, preferred_element_type=jnp.float32
        )
        outgoing[h] = section_two.astype(jnp.bfloat16).reshape(outgoing.shape[1:])
        group = [
            pltpu.make_async_remote_copy(
                src_ref=outgoing.at[h, row_peers[d]],
                dst_ref=out_ref.at[h, me_row],
                send_sem=e_send.at[h, d],
                recv_sem=e_recv.at[h, d],
                device_id=(row_peers[d], me_col),
                device_id_type=MESH,
            )
            for d in far_first
        ]
        for copy in group:
            copy.start()
        own = pltpu.make_async_copy(
            outgoing.at[h, me_row], out_ref.at[h, me_row], local_sem.at[CHUNKS + 2 + h]
        )
        own.start()
        sends.append((group, own))

    for h in range(CHUNKS):
        if h > 0:
            forward_stage(h - 1)
        density_stage(h)
        if h > 0:
            section_stage(h - 1)
    forward_stage(CHUNKS - 1)
    section_stage(CHUNKS - 1)

    for copy in label_copies:
        copy.wait_send()
    for h in range(CHUNKS):
        for copy in band_copies[h] + gathers[h]:
            copy.wait_send()
    for h in range(CHUNKS):
        group, own = sends[h]
        own.wait()
        for d in range(1, rows_n):
            pltpu.make_async_remote_copy(
                src_ref=outgoing.at[h, row_peers[d]],
                dst_ref=out_ref.at[h, row_sources[d]],
                send_sem=e_send.at[h, d],
                recv_sem=e_recv.at[h, d],
                device_id=(row_peers[d], me_col),
                device_id_type=MESH,
            ).wait()


def final_kernel(final_ref, section_hbm, psf_ref, out_ref, section, sems):
    rows_dev = psf_ref.shape[0]
    depth = section.shape[0] // 2
    copies = []
    for h in range(2):
        rows = pl.ds(h * depth, depth)
        copies.append(
            pltpu.make_async_copy(section_hbm.at[rows, :], section.at[rows, :], sems.at[h])
        )
        copies[h].start()
    result = None
    for h in range(2):
        copies[h].wait()
        at = slice(h * depth, h * depth + depth)
        term = jnp.dot(final_ref[:, at], section[at, :], preferred_element_type=jnp.float32)
        result = term if h == 0 else result + term
    psf = psf_ref[...].astype(jnp.float32)
    out_ref[:, 0, :] = result[:rows_dev] * psf
    out_ref[:, 1, :] = result[rows_dev:] * psf


def on_device_kernels(tile_density, tile_dest, tile_place, psf_spectrum):
    tile_count, tile_side, _ = tile_density.shape
    rows_dev, cols_dev = psf_spectrum.shape
    rows_n = lax.axis_size("rows")
    cols_n = lax.axis_size("cols")
    bands, per_row = rows_dev // tile_side, cols_dev // tile_side
    step_rows = tile_side // rows_n // CHUNKS
    chunk = step_rows * tile_side
    tables, final = constants(rows_n, cols_n, tile_side, rows_dev, cols_dev)
    bf16 = jnp.bfloat16
    vmem = pl.BlockSpec(memory_space=pltpu.VMEM)
    anywhere = pl.BlockSpec(memory_space=pl.ANY)
    width = 2 * step_rows * bands
    mix_side = width * rows_n
    dma = pltpu.SemaphoreType.DMA
    section = pl.pallas_call(
        functools.partial(exchange_kernel, rows_n, cols_n, tile_side, bands, per_row),
        out_shape=jax.ShapeDtypeStruct((CHUNKS, rows_n, width, cols_dev), bf16),
        in_specs=[anywhere] * 4,
        out_specs=anywhere,
        scratch_shapes=[
            pltpu.VMEM((2, 1, tile_count), jnp.int32),
            pltpu.VMEM((CHUNKS, tile_count, tile_side // CHUNKS, tile_side), bf16),
            pltpu.VMEM((CHUNKS, tile_count * tile_side // CHUNKS, 128), jnp.float32),
            pltpu.VMEM((CHUNKS, rows_n, tile_count, chunk), bf16),
            pltpu.VMEM((rows_n, 8, 128), jnp.int32),
            pltpu.VMEM((CHUNKS, rows_n, tile_count, chunk), bf16),
            pltpu.VMEM((CHUNKS, cols_n, step_rows * rows_n * bands, cols_dev), bf16),
            pltpu.VMEM((CHUNKS, rows_n, width, cols_dev), bf16),
            pltpu.VMEM((cols_n * cols_dev, 2 * cols_dev), bf16),
            pltpu.VMEM((mix_side, CHUNKS * mix_side), bf16),
            dma((rows_n,)),
            dma((rows_n,)),
            dma((CHUNKS, rows_n)),
            dma((CHUNKS, rows_n)),
            dma((CHUNKS, cols_n)),
            dma((CHUNKS, cols_n)),
            dma((CHUNKS, rows_n)),
            dma((CHUNKS, rows_n)),
            dma((2 * CHUNKS + 4,)),
            dma((1,)),
            dma((CHUNKS,)),
        ],
        compiler_params=pltpu.CompilerParams(
            collective_id=0, has_side_effects=True, vmem_limit_bytes=56 << 20
        ),
    )(
        tile_density,
        tile_dest.reshape(1, tile_count),
        tile_place.reshape(1, tile_count),
        tables,
    )
    return pl.pallas_call(
        final_kernel,
        out_shape=jax.ShapeDtypeStruct((rows_dev, 2, cols_dev), jnp.float32),
        in_specs=[vmem, anywhere, vmem],
        out_specs=vmem,
        scratch_shapes=[pltpu.VMEM((2 * rows_dev, cols_dev), bf16), dma((2,))],
        compiler_params=pltpu.CompilerParams(vmem_limit_bytes=53 << 20),
    )(final, section.reshape(2 * rows_dev, cols_dev), psf_spectrum)


def solution(mesh):
    in_specs = (
        P(("rows", "cols"), None, None),
        P(("rows", "cols"), None),
        P(("rows", "cols")),
        P("rows", "cols"),
    )
    out_specs = P("rows", None, "cols")

    def local(tile_density, tile_dest, tile_place, psf_spectrum):
        fast = fits(
            lax.axis_size("rows"),
            lax.axis_size("cols"),
            *tile_density.shape[:2],
            *psf_spectrum.shape,
        )
        run = on_device_kernels if fast else on_device
        return run(tile_density, tile_dest, tile_place, psf_spectrum)

    return jax.shard_map(
        local, mesh=mesh, in_specs=in_specs, out_specs=out_specs, check_vma=False
    )
```
